128 devices in a mesh: tm: 32 (over x, y, core), rows: 4 (over z).
Axes of the slice: x: 4, y: 4, z: 4, core: 2. Of those that a mesh axis runs over, the one named last changes fastest.
Arguments:
- latents: bfloat16 [32, 64, 128, 512], P('tm', 'rows'), may hold values from -36 to 36
- conv_weight: bfloat16 [3, 3, 3, 512, 512], replicated, may hold values from -0.0546875 to 0.0546875
- w_query: bfloat16 [512, 512], replicated, may hold values from -4 to 4
- w_key: bfloat16 [512, 512], replicated, may hold values from -4 to 4
- w_value: bfloat16 [512, 512], replicated, may hold values from -0.25 to 0.25
- w_out: bfloat16 [512, 512], replicated, may hold values from -0.25 to 0.25
Outputs:
- block_out: bfloat16 [32, 64, 128, 512], P('tm', 'rows')
The draws below stay inside these ranges and needn't reach their ends.
All inputs are finite; a program needn't handle non-finite values.
Results may differ from the reference program's by a relative error of at most 0.0055.
Values may be sent and summed in bfloat16 or wider, within the bound.
No kernel may reach another device: no remote copies, remote signals or barrier semaphores. Data moves between devices by JAX's collectives and lax.ppermute only.
A program may use at most 192 MiB of HBM per device.

```python
import math
import jax
import jax.numpy as jnp
from jax import lax

C = 512
GROUPS = 32
COLS = 128
FRAMES = 32
H = 64


def shared_matrix(key):
    return jnp.clip(jax.random.normal(key, (C, C), jnp.float32), -6.0, 6.0) / math.sqrt(C)


def draw_latents(key, part):
    key = jax.random.fold_in(key, 11)
    key_base = jax.random.fold_in(key, 0)
    key_chan = jax.random.fold_in(key, 1)
    key_group = jax.random.fold_in(key, 3)
    base = jax.random.normal(key_base, (FRAMES, H, COLS, C), jnp.float32)
    base = jnp.clip(base, -5.0, 5.0)
    position = jnp.arange(H, dtype=jnp.float32) / max(H - 1, 1)
    row_scale = 1.0 + 2.0 * position
    chan_scale = jnp.exp(jax.random.uniform(key_chan, (C,), jnp.float32, math.log(0.5), math.log(2.0)))
    group_level = jnp.clip(jax.random.normal(key_group, (GROUPS,), jnp.float32), -2.0, 2.0)
    group_level = jnp.repeat(group_level, C // GROUPS)
    offset = (0.5 + 2.0 * position)[:, None, None] * group_level
    return (base * row_scale[None, :, None, None] * chan_scale + offset[None]).astype(jnp.bfloat16)


def draw_w_query(key, part):
    key = jax.random.fold_in(key, 21)
    return shared_matrix(key).astype(jnp.bfloat16)


def draw_w_key(key, part):
    key = jax.random.fold_in(key, 37)
    return shared_matrix(key).astype(jnp.bfloat16)


def centred(own_key, shape, scale, reach, kind=jnp.bfloat16):
    drawn = scale * jax.random.normal(own_key, shape, jnp.float32)
    return jnp.clip(drawn, min=-reach, max=reach).astype(kind)


def setup_inputs(seed: int = 0) -> dict:
    arg_keys = jax.random.split(jax.random.key(seed), 7)
    latents = draw_latents(jax.random.fold_in(arg_keys[6], 71), 0)
    conv_weight = centred(arg_keys[1], (3, 3, 3, C, C), (27 * C) ** -0.5, 0.0546875)
    w_query = draw_w_query(jax.random.fold_in(arg_keys[6], 71), 0)
    w_key = draw_w_key(jax.random.fold_in(arg_keys[6], 71), 0)
    w_value = centred(arg_keys[4], (C, C), C ** -0.5, 0.25)
    w_out = centred(arg_keys[5], (C, C), C ** -0.5, 0.25)
    return {"latents": latents, "conv_weight": conv_weight, "w_query": w_query, "w_key": w_key, "w_value": w_value, "w_out": w_out}


def group_norm(values):
    frames, height, width, chans = values.shape
    grouped = values.reshape(frames, height, width, GROUPS, chans // GROUPS)
    center = lax.optimization_barrier(jnp.mean(grouped, axis=(1, 2, 4), keepdims=True))
    shifted = grouped - center
    spread = lax.optimization_barrier(jnp.mean(shifted * shifted, axis=(1, 2, 4), keepdims=True))
    return (shifted * lax.rsqrt(spread + 1e-06)).reshape(values.shape)

def causal_conv(acted, conv_weight):
    frames, height, width, chans = acted.shape
    padded = jnp.pad(acted, ((2, 0), (1, 1), (1, 1), (0, 0)))
    folded = conv_weight.reshape(3, 3, 3 * chans, chans)

    def one_frame(index):
        slab = lax.dynamic_slice_in_dim(padded, index.astype(jnp.int32), 3, 0)
        total = jnp.zeros((height * width, chans), jnp.float32)
        for time_tap in range(3):
            for row_tap in range(3):
                window = jnp.concatenate([slab[time_tap, row_tap:row_tap + height, col_tap:col_tap + width] for col_tap in range(3)], axis=-1)
                total = total + jnp.dot(window.reshape(height * width, 3 * chans), folded[time_tap, row_tap], preferred_element_type=jnp.float32)
        return total.reshape(height, width, chans)
    return lax.map(one_frame, jnp.arange(frames, dtype=jnp.int32))

def reference(latents, conv_weight, w_query, w_key, w_value, w_out):
    frames, height, width, chans = latents.shape
    acted = jax.nn.silu(group_norm(latents.astype(jnp.float32))).astype(jnp.bfloat16)
    conv = causal_conv(acted, conv_weight)
    mid = (latents.astype(jnp.float32) + conv).astype(jnp.bfloat16)
    normed = group_norm(mid.astype(jnp.float32)).astype(jnp.bfloat16)
    flat = normed.reshape(frames * height * width, chans)
    query = jnp.dot(flat, w_query, preferred_element_type=jnp.float32).astype(jnp.bfloat16).reshape(frames, height * width, chans)
    keys = jnp.dot(flat, w_key, preferred_element_type=jnp.float32).astype(jnp.bfloat16).reshape(frames, height * width, chans)
    values = jnp.dot(flat, w_value, preferred_element_type=jnp.float32).astype(jnp.bfloat16).reshape(frames, height * width, chans)
    scores = jnp.einsum('tpc,spc->pts', query.astype(jnp.float32), keys.astype(jnp.float32)) / jnp.sqrt(jnp.float32(chans))
    causal = jnp.arange(frames)[:, None] >= jnp.arange(frames)[None, :]
    scores = jnp.where(causal[None], scores, jnp.float32(-1e+30))
    weights = jax.nn.softmax(scores, axis=-1).astype(jnp.bfloat16)
    attended = jnp.einsum('pts,spc->tpc', weights.astype(jnp.float32), values.astype(jnp.float32)).astype(jnp.bfloat16)
    update = jnp.dot(attended.reshape(-1, chans), w_out, preferred_element_type=jnp.float32)
    return (mid.astype(jnp.float32) + update.reshape(frames, height, width, chans)).astype(jnp.bfloat16)
```

```python
import functools

import jax
import jax.numpy as jnp
from jax import lax
from jax.experimental import pallas as pl
from jax.experimental.pallas import tpu as pltpu
from jax.sharding import PartitionSpec as P

GROUPS = 32
T = 32
C = 512
S = 8
W = S + 2
MSG = 104
EPS = 1e-6
BF, F32 = jnp.bfloat16, jnp.float32
HI = lax.Precision.HIGHEST


def iota(shape, dim):
    return lax.broadcasted_iota(jnp.int32, shape, dim)


def dot(a, b, precision=None):
    return jnp.dot(a, b, preferred_element_type=F32, precision=precision)


def params():
    return pltpu.CompilerParams(vmem_limit_bytes=56 * 2**20)


def cost(flops, nbytes):
    return pl.CostEstimate(flops=flops, bytes_accessed=nbytes, transcendentals=0)


def to_groups(lane):
    return (iota((C, 128), 0) // 16 + lane == iota((C, 128), 1)).astype(F32)


def from_groups(lane, dtype=F32):
    return (iota((128, C), 1) // 16 + lane == iota((128, C), 0)).astype(dtype)


def group_stats(mean, m2, count, lane):
    group_mean = dot(mean, to_groups(lane), HI) * (1.0 / 16.0)
    off = mean - dot(group_mean, from_groups(lane), HI)
    return group_mean + dot(m2 + count * (off * off), to_groups(lane + 32), HI)


def merge(parts, count):
    n = parts.shape[0]
    total = jnp.sum(parts, axis=0)
    mean = total * (1.0 / n)
    off = parts - mean[None]
    between = pltpu.roll(jnp.sum(off * off, axis=0), 32, 1)
    is_mean = (iota(total.shape, 1) // 32) % 2 == 0
    return jnp.where(is_mean, mean, total + count * between)


def latent_stats_kernel(x_ref, out_ref):
    n = x_ref.shape[0]
    step = 256

    def add(i, total):
        rows = x_ref[pl.ds(pl.multiple_of(i * step, step), step), :].astype(F32)
        return total + jnp.sum(rows.reshape(step // 8, 8, C), axis=0)

    total = lax.fori_loop(0, n // step, add, jnp.zeros((8, C), F32))
    mean = jnp.sum(total, axis=0, keepdims=True) * (1.0 / n)

    def add_square(i, total):
        rows = x_ref[pl.ds(pl.multiple_of(i * step, step), step), :].astype(F32) - mean
        return total + jnp.sum((rows * rows).reshape(step // 8, 8, C), axis=0)

    total = lax.fori_loop(0, n // step, add_square, jnp.zeros((8, C), F32))
    m2 = jnp.sum(total, axis=0, keepdims=True)
    wide = lambda v: jnp.broadcast_to(v, (8, C))
    out_ref[...] = group_stats(wide(mean), wide(m2), float(n), 0)


def message_kernel(top_ref, x_ref, bottom_ref, s0, s1, s2, s3, out_ref):
    pair = pl.program_id(0)
    parts = jnp.stack([s0[...], s1[...], s2[...], s3[...]])
    n = 2048.0 * 16.0
    whole = merge(parts, n)
    is_mean = iota(whole.shape, 1) < 32
    stats = jnp.where(is_mean, whole, lax.rsqrt(whole * (1.0 / (4.0 * n)) + EPS))
    stats = jnp.where(iota(whole.shape, 1) < 64, stats, 0.0)
    high = stats.astype(BF).astype(F32)
    middle = (stats - high).astype(BF).astype(F32)
    low = stats - high - middle
    row = jnp.concatenate([high, middle, low, jnp.zeros_like(low)], axis=1)[:1]
    for odd in range(2):
        start = 16 * pair if odd else 16 * pair - 16
        start = jnp.clip(start, 0, 96)
        first = 16 * pair + 8 * odd - 1 - start
        start = pl.multiple_of(start, 16)
        out_row, source = iota((MSG, W * 32), 0), iota((MSG, W * 32), 1)
        column = first + out_row % W
        pick = (source == (out_row // W) * 32 + column) & (column >= 0) & (column < 32)
        pick = (pick & (out_row < W * W)).astype(BF)
        for half in range(2):
            cols = pl.ds(start, 32)
            if half == 0:
                block = jnp.concatenate([top_ref[:, cols, :], x_ref[0:9, cols, :]], axis=0)
            else:
                block = jnp.concatenate([x_ref[7:16, cols, :], bottom_ref[:, cols, :]], axis=0)
            message = dot(pick, block.reshape(W * 32, C))
            message = jnp.where(iota((MSG, C), 0) == W * W, row, message)
            out_ref[2 * odd + half] = message.astype(BF)


def conv_kernel(place_ref, in_ref, w_ref, mid_ref, stats_ref, acted, latent, acc):
    step = pl.program_id(0)
    b, e = step // 3, step % 3

    @pl.when(step == 0)
    def _():
        block, z = place_ref[0], place_ref[1]
        half, column = block % 2, block // 2
        tail = in_ref[:, 96:MSG, :].reshape(T * 8, C)
        pick = (iota((T, T * 8), 1) == iota((T, T * 8), 0) * 8 + 4).astype(BF)
        pieces = dot(pick, tail).astype(BF)
        mean, scale = (
            sum(dot(pieces[:, 128 * i : 128 * i + 128], from_groups(lane, BF)) for i in range(3))
            for lane in (0, 32)
        )

        def activate(first, pixels):
            rows = pixels * T
            values = in_ref[:, first : first + pixels, :].reshape(rows, C)
            turn = iota((rows, rows), 0)
            turn = (iota((rows, rows), 1) == (turn % T) * pixels + turn // T).astype(BF)
            turned = dot(turn, values).reshape(pixels, T, C)
            u = (turned - mean[None]) * scale[None]
            act = u / (1.0 + jnp.exp(-u))
            p = iota((pixels, T, C), 0) + first
            r, c = p // W, p % W
            out = (c == 0) & (column == 0) | (c == W - 1) & (column == 15)
            out = out | (r == 0) & (half == 0) & (z == 0) | (r == W - 1) & (half == 1) & (z == 3)
            act = jnp.where(out, 0.0, act)
            flat = act.reshape(rows, C)
            frame = iota((rows, C), 0) % T
            for i in range(pixels):
                where = first + i
                if where >= W * W:
                    break
                r, c = where // W, where % W
                if 1 <= r <= S and 1 <= c <= S:
                    latent[(r - 1) * S + c - 1] = turned[i].astype(BF)
            count = min(pixels, W * W - first)
            for tap in range(3):
                by = 2 - tap
                moved = flat if by == 0 else jnp.where(frame < by, 0.0, pltpu.roll(flat, by, 0))
                moved = moved.astype(BF).reshape(pixels, T, C)
                for i in range(count):
                    acted[(first + i) // W, (first + i) % W, :, C * tap : C * tap + C] = moved[i]

        for k in range(6):
            activate(16 * k, 16)
        activate(96, 8)
        acc[...] = jnp.zeros_like(acc)

    weight = w_ref[...].reshape(3 * C, C)

    def row(r, _):
        left = acted[pl.ds(2 * r + b, 2), pl.ds(e, S)].reshape(2 * S * T, 3 * C)
        at = pl.ds(pl.multiple_of(r * 2 * S * T, 2 * S * T), 2 * S * T)
        acc[at, :] += dot(left, weight)
        return 0

    lax.fori_loop(0, S // 2, row, 0)

    @pl.when(step == 8)
    def _():
        mid = (latent[...].astype(F32) + acc[...].reshape(S * S, T, C)).astype(BF)
        mid_ref[...] = mid
        values = mid_ref[...].astype(F32)
        mean = jnp.sum(values, axis=0) * (1.0 / (S * S))
        off = mid_ref[...].astype(F32) - mean[None]
        m2 = jnp.sum(off * off, axis=0)
        half = T // 2
        stats_ref[...] = group_stats(mean[:half], m2[:half], float(S * S), 0) + group_stats(
            mean[half:], m2[half:], float(S * S), 64
        )


def merge_kernel(s0, s1, s2, s3, out_ref):
    parts = jnp.stack([s0[...], s1[...], s2[...], s3[...]])
    whole = merge(parts, float(S * S * 16))
    out_ref[...] = jnp.broadcast_to(whole[None], out_ref.shape)


def attend_kernel(mid_ref, parts_ref, wq_ref, wk_ref, wv_ref, wo_ref, out_ref, norm):
    @pl.when(pl.program_id(0) == 0)
    def _():
        count = float(S * S * 16 * 4)
        whole = merge(parts_ref[...], count)
        is_mean = (iota(whole.shape, 1) // 32) % 2 == 0
        whole = jnp.where(is_mean, whole, lax.rsqrt(whole * (1.0 / (32.0 * count)) + EPS))
        for i in range(2):
            for j in range(2):
                norm[i, 16 * j : 16 * j + 16] = dot(whole, from_groups(64 * j + 32 * i), HI)

    pixels = mid_ref.shape[0]
    rows = pixels * T
    mid = mid_ref[...].astype(F32)
    flat = ((mid - norm[0][None]) * norm[1][None]).astype(BF).reshape(rows, C)
    query = dot(flat, wq_ref[...]).astype(BF)
    keys = dot(flat, wk_ref[...]).astype(BF)
    values = dot(flat, wv_ref[...]).astype(BF)
    n = 256
    t, s = iota((n, n), 0), iota((n, n), 1)
    seen = (t // T == s // T) & (t >= s)
    parts = []
    for i in range(rows // n):
        at = slice(i * n, i * n + n)
        scores = lax.dot_general(
            query[at], keys[at], (((1,), (1,)), ((), ())), preferred_element_type=F32
        ) * (1.0 / (C**0.5))
        scores = jnp.where(seen, scores, -1e30)
        weights = jnp.exp(scores - jnp.max(scores, axis=1, keepdims=True))
        weights = (weights / jnp.sum(weights, axis=1, keepdims=True)).astype(BF)
        parts.append(dot(weights, values[at]).astype(BF))
    update = dot(jnp.concatenate(parts, axis=0), wo_ref[...])
    out = (mid.reshape(rows, C) + update).astype(BF)
    turn = iota((rows, rows), 0)
    turn = (iota((rows, rows), 1) == (turn % pixels) * T + turn // pixels).astype(BF)
    out_ref[...] = dot(turn, out).astype(BF).reshape(T, pixels, C)


def neighbours(array, axis):
    n = lax.axis_size(axis)
    return [array] + [lax.ppermute(array, axis, [(i, (i + by) % n) for i in range(n)]) for by in range(1, n)]


def local(latents, conv_weight, w_query, w_key, w_value, w_out):
    bands = lax.axis_size("rows")
    x = latents.reshape(16, 128, C)
    down = [(i, i + 1) for i in range(bands - 1)]
    top = lax.ppermute(x[15:16], "rows", down)
    bottom = lax.ppermute(x[0:1], "rows", [(j, i) for i, j in down])
    vmem = pl.BlockSpec(memory_space=pltpu.VMEM)
    stats = pl.pallas_call(
        latent_stats_kernel,
        out_shape=jax.ShapeDtypeStruct((8, 128), F32),
        in_specs=[vmem],
        out_specs=vmem,
        compiler_params=params(),
        cost_estimate=cost(2048 * C * 4, 2048 * C * 2),
        name="latent_stats",
    )(x.reshape(2048, C))
    whole = lambda *shape: pl.BlockSpec(shape, lambda i: (0,) * len(shape))
    messages = pl.pallas_call(
        message_kernel,
        grid=(8,),
        out_shape=jax.ShapeDtypeStruct((32, MSG, C), BF),
        in_specs=[whole(1, 128, C), whole(16, 128, C), whole(1, 128, C)] + [whole(8, 128)] * 4,
        out_specs=pl.BlockSpec((4, MSG, C), lambda i: (i, 0, 0)),
        compiler_params=params(),
        cost_estimate=cost(32 * MSG * 320 * C * 2, 6 * 2**20),
        name="messages",
    )(top, x, bottom, *neighbours(stats, "rows"))
    patch = lax.all_to_all(messages.reshape(1, 32, MSG, C), "tm", split_axis=1, concat_axis=0, tiled=True)
    place = jnp.stack([lax.axis_index("tm"), lax.axis_index("rows")]).astype(jnp.int32)
    mid, stats = pl.pallas_call(
        conv_kernel,
        grid=(9,),
        out_shape=(jax.ShapeDtypeStruct((S * S, T, C), BF), jax.ShapeDtypeStruct((T // 2, 128), F32)),
        in_specs=[
            pl.BlockSpec(memory_space=pltpu.SMEM),
            whole(T, MSG, C),
            pl.BlockSpec((3, 1, 1, C, C), lambda i: (0, i // 3, i % 3, 0, 0)),
        ],
        out_specs=(whole(S * S, T, C), whole(T // 2, 128)),
        scratch_shapes=[
            pltpu.VMEM((W, W, T, 3 * C), BF),
            pltpu.VMEM((S * S, T, C), BF),
            pltpu.VMEM((S * S * T, C), F32),
        ],
        compiler_params=params(),
        cost_estimate=cost(2048 * 27 * C * C * 2, 20 * 2**20),
        name="conv",
    )(place, patch.reshape(T, MSG, C), conv_weight)
    parts = pl.pallas_call(
        merge_kernel,
        out_shape=jax.ShapeDtypeStruct((32, T // 2, 128), F32),
        in_specs=[vmem] * 4,
        out_specs=vmem,
        compiler_params=params(),
        name="merge",
    )(*neighbours(stats, "rows"))
    parts = lax.all_to_all(parts[None], "tm", split_axis=1, concat_axis=0, tiled=True)
    pixels = 16
    out = pl.pallas_call(
        attend_kernel,
        grid=(S * S // pixels,),
        out_shape=jax.ShapeDtypeStruct((T, S * S, C), BF),
        in_specs=[pl.BlockSpec((pixels, T, C), lambda i: (i, 0, 0)), whole(32, T // 2, 128)] + [whole(C, C)] * 4,
        out_specs=pl.BlockSpec((T, pixels, C), lambda i: (0, i, 0)),
        scratch_shapes=[pltpu.VMEM((2, T, C), F32)],
        compiler_params=params(),
        cost_estimate=cost(2048 * C * C * 2 * 6, 8 * 2**20),
        name="attend",
    )(mid, parts.reshape(32, T // 2, 128), w_query, w_key, w_value, w_out)
    back = lax.all_to_all(out[:, None], "tm", split_axis=0, concat_axis=1, tiled=True)
    back = back.reshape(16, 2, S, S, C).transpose(1, 2, 0, 3, 4)
    return back.reshape(1, 16, 128, C)


def solution(mesh):
    in_specs = (P("tm", "rows", None, None), P(), P(), P(), P(), P())
    out_specs = P("tm", "rows", None, None)
    return jax.shard_map(local, mesh=mesh, in_specs=in_specs, out_specs=out_specs, check_vma=False)
```

```python
import functools

import jax
import jax.numpy as jnp
from jax import lax
from jax.experimental import pallas as pl
from jax.experimental.pallas import tpu as pltpu
from jax.sharding import PartitionSpec as P

GROUPS = 32
T = 32
C = 512
S = 8
W = S + 2
P2 = T // 2
RIM = 40
EPS = 1e-6
BF, F32 = jnp.bfloat16, jnp.float32
HI = lax.Precision.HIGHEST


def iota(shape, dim):
    return lax.broadcasted_iota(jnp.int32, shape, dim)


def dot(a, b, precision=None):
    return jnp.dot(a, b, preferred_element_type=F32, precision=precision)


def params():
    return pltpu.CompilerParams(vmem_limit_bytes=56 * 2**20)


def cost(flops, nbytes):
    return pl.CostEstimate(flops=flops, bytes_accessed=nbytes, transcendentals=0)


def to_groups(lane):
    return (iota((C, 128), 0) // 16 + lane == iota((C, 128), 1)).astype(F32)


def from_groups(lane, dtype=F32):
    return (iota((128, C), 1) // 16 + lane == iota((128, C), 0)).astype(dtype)


def group_stats(mean, m2, count, lane):
    group_mean = dot(mean, to_groups(lane), HI) * (1.0 / 16.0)
    off = mean - dot(group_mean, from_groups(lane), HI)
    return group_mean + dot(m2 + count * (off * off), to_groups(lane + 32), HI)


def merge(parts, count):
    n = parts.shape[0]
    total = jnp.sum(parts, axis=0)
    mean = total * (1.0 / n)
    off = parts - mean[None]
    between = pltpu.roll(jnp.sum(off * off, axis=0), 32, 1)
    is_mean = (iota(total.shape, 1) // 32) % 2 == 0
    return jnp.where(is_mean, mean, total + count * between)


def latent_stats_kernel(x_ref, out_ref):
    n = x_ref.shape[0]
    step = 256

    def add(i, total):
        rows = x_ref[pl.ds(pl.multiple_of(i * step, step), step), :].astype(F32)
        return total + jnp.sum(rows.reshape(step // 8, 8, C), axis=0)

    total = lax.fori_loop(0, n // step, add, jnp.zeros((8, C), F32))
    mean = jnp.sum(total, axis=0, keepdims=True) * (1.0 / n)

    def add_square(i, total):
        rows = x_ref[pl.ds(pl.multiple_of(i * step, step), step), :].astype(F32) - mean
        return total + jnp.sum((rows * rows).reshape(step // 8, 8, C), axis=0)

    total = lax.fori_loop(0, n // step, add_square, jnp.zeros((8, C), F32))
    m2 = jnp.sum(total, axis=0, keepdims=True)
    wide = lambda v: jnp.broadcast_to(v, (8, C))
    out_ref[...] = group_stats(wide(mean), wide(m2), float(n), 0)


def finish(whole, count):
    is_mean = (iota(whole.shape, 1) // 32) % 2 == 0
    return jnp.where(is_mean, whole, lax.rsqrt(whole * (1.0 / count) + EPS))


def place_kernel(place_ref, s0, s1, s2, s3, out_ref):
    n = 2048.0 * 16.0
    whole = finish(merge(jnp.stack([s0[...], s1[...], s2[...], s3[...]]), n), 4.0 * n)[:1]
    frame = place_ref[0]
    row = (frame % 2) * P2 + frame // 2
    here = (iota((T, 128), 0) == row) & (iota((T, 128), 1) < 64)
    out_ref[...] = jnp.where(here, whole, 0.0)


def rim_kernel(top_ref, x_ref, bottom_ref, out_ref):
    pair = pl.program_id(0)
    for odd in range(2):
        start = 16 * pair if odd else 16 * pair - 16
        start = jnp.clip(start, 0, 96)
        first = 16 * pair + 8 * odd - 1 - start
        start = pl.multiple_of(start, 16)
        p, source = iota((RIM, W * 32), 0), iota((RIM, W * 32), 1)
        r = jnp.where(p < 10, 0, jnp.where(p < 20, 9, jnp.where(p < 28, p - 19, p - 27)))
        c = jnp.where(p < 10, p, jnp.where(p < 20, p - 10, jnp.where(p < 28, 0, 9)))
        column = first + c
        pick = (source == r * 32 + column) & (column >= 0) & (column < 32) & (p < 36)
        pick = pick.astype(BF)
        for half in range(2):
            cols = pl.ds(start, 32)
            if half == 0:
                block = jnp.concatenate([top_ref[:, cols, :], x_ref[0:9, cols, :]], axis=0)
            else:
                block = jnp.concatenate([x_ref[7:16, cols, :], bottom_ref[:, cols, :]], axis=0)
            out_ref[2 * odd + half] = dot(pick, block.reshape(W * 32, C)).astype(BF)


def weights_kernel(w_ref, out_ref):
    g = [w_ref[i, 0, 0].astype(F32) for i in range(3)]
    ends = (g[0] + g[2]) * 0.5
    out_ref[0, 0, 0] = w_ref[0, 0, 0]
    out_ref[1, 0, 0] = (ends + g[1] * 0.5).astype(BF)
    out_ref[2, 0, 0] = (ends - g[1] * 0.5).astype(BF)
    out_ref[3, 0, 0] = w_ref[2, 0, 0]


def expand(stats_ref, norm):
    for i in range(2):
        norm[i] = dot(stats_ref[...], from_groups(32 * i), HI).reshape(2, P2, C)


def turned(in_ref, first, pixels):
    rows = pixels * T
    to, at = iota((rows, rows), 0), iota((rows, rows), 1)
    frame = 2 * (to % P2) + (to // P2) % 2
    turn = (at == frame * pixels + to // T).astype(BF)
    values = in_ref[:, first : first + pixels, :].reshape(rows, C)
    return dot(turn, values).reshape(pixels, 2, P2, C)


def activate(values, norm):
    u = (values - norm[0][None]) * norm[1][None]
    return (u / (1.0 + jnp.exp(-u))).astype(BF).astype(F32)


def time_terms(act):
    pixels = act.shape[0]
    even, odd = act[:, 0], act[:, 1]
    start = iota((pixels * P2, C), 0) % P2 == 0

    def before(v):
        v = pltpu.roll(v.reshape(pixels * P2, C), 1, 0)
        return jnp.where(start, 0.0, v).reshape(pixels, P2, C)

    even1, odd1 = before(even), before(odd)
    return [v.astype(BF) for v in (even1 - even, odd1 + even, even - odd1, odd1 - odd)]


def signs(j):
    return jnp.where(j == 3, 0.0, 1.0), jnp.where(j == 0, 0.0, jnp.where(j == 1, 1.0, -1.0))


def conv_kernel(in_ref, stats_ref, w_ref, y_ref, latent_ref, terms, norm):
    j = pl.program_id(0)

    @pl.when(j == 0)
    def _():
        expand(stats_ref, norm)
        for i in range(4):
            terms[i, 0] = jnp.zeros((S, P2, 3 * C), BF)
            terms[i, W - 1] = jnp.zeros((S, P2, 3 * C), BF)
            terms[i, 1 : S + 1, 0, :, 0:C] = jnp.zeros((S, P2, C), BF)
            terms[i, 1 : S + 1, S - 1, :, 2 * C :] = jnp.zeros((S, P2, C), BF)
        for k in range(S // 2):
            values = turned(in_ref, 16 * k, 16)
            latent_ref[16 * k : 16 * k + 16] = values.astype(BF)
            at = slice(2 * k + 1, 2 * k + 3)
            for i, v in enumerate(time_terms(activate(values, norm))):
                v = v.reshape(2, S, P2, C)
                terms[i, at, 1:S, :, 0:C] = v[:, : S - 1]
                terms[i, at, :, :, C : 2 * C] = v
                terms[i, at, 0 : S - 1, :, 2 * C :] = v[:, 1:]
        y_ref[...] = jnp.zeros_like(y_ref)

    even, odd = signs(j)
    for q in range(S // 2):
        m = sum(
            dot(terms[j, 2 * q + b : 2 * q + b + 2].reshape(2 * S * P2, 3 * C), w_ref[0, b].reshape(3 * C, C))
            for b in range(3)
        ).reshape(2 * S, P2, C)
        at = slice(16 * q, 16 * q + 16)
        y_ref[at, 0] += even * m
        y_ref[at, 1] += odd * m


def border_kernel(place_ref, in_ref, stats_ref, y_ref, latent_ref, w_ref, mid_ref, out_ref, terms, side, norm):
    j = pl.program_id(0)

    @pl.when(j == 0)
    def _():
        expand(stats_ref, norm)
        block, z = place_ref[0], place_ref[1]
        half, column = block % 2, block // 2
        above = (half == 0) & (z == 0)
        below = (half == 1) & (z == 3)
        left, right = column == 0, column == 15
        for first, pixels in ((0, 16), (16, 16), (32, 8)):
            act = activate(turned(in_ref, first, pixels), norm)
            p = iota((pixels, 2, P2, C), 0) + first
            out = above & (p < 10) | below & (p >= 10) & (p < 20)
            out = out | left & ((p == 0) | (p == 10) | (p >= 20) & (p < 28))
            out = out | right & ((p == 9) | (p == 19) | (p >= 28))
            for i, v in enumerate(time_terms(jnp.where(out, 0.0, act))):
                terms[i, first : first + pixels] = v
        side[...] = jnp.zeros_like(side)

    even, odd = signs(j)
    zero = jnp.zeros((1, P2, C), BF)

    def add(k, parts, weight):
        m = dot(jnp.concatenate(parts, axis=2).reshape(S * P2, 3 * C), weight.reshape(3 * C, C))
        m = m.reshape(S, P2, C)
        side[k, 0] += even * m
        side[k, 1] += odd * m

    for k, b in ((0, 0), (1, 2)):
        add(k, [terms[j, 10 * k + e : 10 * k + e + S] for e in range(3)], w_ref[0, b])
    for k, e in ((2, 0), (3, 2)):
        line = terms[j, 20 + 8 * (k - 2) : 28 + 8 * (k - 2)]
        parts = [jnp.concatenate([zero, line[:-1]], axis=0), line, jnp.concatenate([line[1:], zero], axis=0)]
        add(k, parts, w_ref[0, :, e])

    @pl.when(j == 3)
    def _():
        total = jnp.zeros((2, P2, C), F32)
        for p in range(S * S):
            r, c = p // S, p % S
            v = y_ref[p]
            for k, is_side, at in ((0, r == 0, c), (1, r == S - 1, c), (2, c == 0, r), (3, c == S - 1, r)):
                if is_side:
                    v = v + side[k, :, at]
            v = (latent_ref[p].astype(F32) + v).astype(BF)
            mid_ref[p] = v
            total = total + v.astype(F32)
        mean = total * (1.0 / (S * S))
        total = jnp.zeros((2, P2, C), F32)
        for p in range(S * S):
            off = mid_ref[p].astype(F32) - mean
            total = total + off * off
        out_ref[...] = sum(group_stats(mean[i], total[i], float(S * S), 64 * i) for i in range(2))


def merge_kernel(s0, s1, s2, s3, out_ref):
    parts = jnp.stack([s0[...], s1[...], s2[...], s3[...]])
    whole = merge(parts, float(S * S * 16))
    out_ref[...] = jnp.broadcast_to(whole[None], out_ref.shape)


def attend_kernel(mid_ref, parts_ref, wq_ref, wk_ref, wv_ref, wo_ref, out_ref, norm):
    @pl.when(pl.program_id(0) == 0)
    def _():
        count = float(S * S * 16 * 4)
        whole = finish(merge(parts_ref[...], count), 32.0 * count)
        for i in range(2):
            for j in range(2):
                norm[i, j] = dot(whole, from_groups(64 * j + 32 * i), HI)

    pixels = mid_ref.shape[0]
    rows = pixels * T
    mid = mid_ref[...].astype(F32)
    flat = ((mid - norm[0][None]) * norm[1][None]).astype(BF).reshape(rows, C)
    query = dot(flat, wq_ref[...]).astype(BF)
    keys = dot(flat, wk_ref[...]).astype(BF)
    values = dot(flat, wv_ref[...]).astype(BF)
    n = 256
    row, column = iota((n, n), 0), iota((n, n), 1)
    frame = lambda v: 2 * (v % P2) + (v // P2) % 2
    seen = (row // T == column // T) & (frame(row) >= frame(column))
    parts = []
    for i in range(rows // n):
        at = slice(i * n, i * n + n)
        scores = lax.dot_general(
            query[at], keys[at], (((1,), (1,)), ((), ())), preferred_element_type=F32
        ) * (1.0 / (C**0.5))
        scores = jnp.where(seen, scores, -1e30)
        weights = jnp.exp(scores - jnp.max(scores, axis=1, keepdims=True))
        weights = (weights / jnp.sum(weights, axis=1, keepdims=True)).astype(BF)
        parts.append(dot(weights, values[at]).astype(BF))
    update = dot(jnp.concatenate(parts, axis=0), wo_ref[...])
    out = (mid.reshape(rows, C) + update).astype(BF)
    to = iota((rows, rows), 0)
    frame = to // pixels
    turn = (iota((rows, rows), 1) == (to % pixels) * T + (frame % 2) * P2 + frame // 2).astype(BF)
    out_ref[...] = dot(turn, out).astype(BF).reshape(T, pixels, C)


def neighbours(array, axis):
    n = lax.axis_size(axis)
    return [array] + [lax.ppermute(array, axis, [(i, (i + by) % n) for i in range(n)]) for by in range(1, n)]


def sum_over(array, size, stride):
    span = size * stride
    total = array
    for by in range(1, size):
        pairs = [(i, i - i % span + (i + by * stride) % span) for i in range(32)]
        total = total + lax.ppermute(array, "tm", pairs)
    return total


def local(latents, conv_weight, w_query, w_key, w_value, w_out):
    bands = lax.axis_size("rows")
    x = latents.reshape(16, 128, C)
    vmem = pl.BlockSpec(memory_space=pltpu.VMEM)
    smem = pl.BlockSpec(memory_space=pltpu.SMEM)
    whole = lambda *shape: pl.BlockSpec(shape, lambda i: (0,) * len(shape))
    exchange = functools.partial(lax.all_to_all, axis_name="tm", split_axis=1, concat_axis=0, tiled=True)
    place = jnp.stack([lax.axis_index("tm"), lax.axis_index("rows")]).astype(jnp.int32)

    messages = x.reshape(2, S, 16, S, C).transpose(2, 0, 1, 3, 4)
    patch = exchange(messages.reshape(1, 32, S * S, C)).reshape(T, S * S, C)

    stats = pl.pallas_call(
        latent_stats_kernel,
        out_shape=jax.ShapeDtypeStruct((8, 128), F32),
        in_specs=[vmem],
        out_specs=vmem,
        compiler_params=params(),
        cost_estimate=cost(2048 * C * 4, 2048 * C * 2),
        name="latent_stats",
    )(x.reshape(2048, C))
    stats = pl.pallas_call(
        place_kernel,
        out_shape=jax.ShapeDtypeStruct((T, 128), F32),
        in_specs=[smem] + [vmem] * 4,
        out_specs=vmem,
        compiler_params=params(),
        cost_estimate=cost(2**20, 2**16),
        name="place_stats",
    )(place, *neighbours(stats, "rows"))
    for size, stride in ((4, 2), (4, 8), (2, 1)):
        stats = sum_over(stats, size, stride)

    weights = pl.pallas_call(
        weights_kernel,
        grid=(3, 3),
        out_shape=jax.ShapeDtypeStruct((4, 3, 3, C, C), BF),
        in_specs=[pl.BlockSpec((3, 1, 1, C, C), lambda b, e: (0, b, e, 0, 0))],
        out_specs=pl.BlockSpec((4, 1, 1, C, C), lambda b, e: (0, b, e, 0, 0)),
        compiler_params=params(),
        cost_estimate=cost(9 * 4 * C * C, 9 * 7 * C * C * 2),
        name="weights",
    )(conv_weight)

    down = [(i, i + 1) for i in range(bands - 1)]
    top = lax.ppermute(x[15:16], "rows", down)
    bottom = lax.ppermute(x[0:1], "rows", [(j, i) for i, j in down])
    rim = pl.pallas_call(
        rim_kernel,
        grid=(8,),
        out_shape=jax.ShapeDtypeStruct((32, RIM, C), BF),
        in_specs=[whole(1, 128, C), whole(16, 128, C), whole(1, 128, C)],
        out_specs=pl.BlockSpec((4, RIM, C), lambda i: (i, 0, 0)),
        compiler_params=params(),
        cost_estimate=cost(32 * RIM * 320 * C * 2, 4 * 2**20),
        name="rim",
    )(top, x, bottom)
    rim, patch = lax.optimization_barrier((rim, patch))
    rim = exchange(rim[None]).reshape(T, RIM, C)

    frames = jax.ShapeDtypeStruct((S * S, 2, P2, C), BF)
    y, turned_latents = pl.pallas_call(
        conv_kernel,
        grid=(4,),
        out_shape=(jax.ShapeDtypeStruct((S * S, 2, P2, C), F32), frames),
        in_specs=[
            whole(T, S * S, C),
            whole(T, 128),
            pl.BlockSpec((1, 3, 3, C, C), lambda i: (i, 0, 0, 0, 0)),
        ],
        out_specs=(whole(S * S, 2, P2, C), whole(S * S, 2, P2, C)),
        scratch_shapes=[pltpu.VMEM((4, W, S, P2, 3 * C), BF), pltpu.VMEM((2, 2, P2, C), F32)],
        compiler_params=params(),
        cost_estimate=cost(1024 * 36 * C * C * 2, 28 * 2**20),
        name="conv",
    )(patch, stats, weights)
    mid, stats = pl.pallas_call(
        border_kernel,
        grid=(4,),
        out_shape=(frames, jax.ShapeDtypeStruct((P2, 128), F32)),
        in_specs=[
            smem,
            whole(T, RIM, C),
            whole(T, 128),
            whole(S * S, 2, P2, C),
            whole(S * S, 2, P2, C),
            pl.BlockSpec((1, 3, 3, C, C), lambda i: (i, 0, 0, 0, 0)),
        ],
        out_specs=(whole(S * S, 2, P2, C), whole(P2, 128)),
        scratch_shapes=[
            pltpu.VMEM((4, RIM, P2, C), BF),
            pltpu.VMEM((4, 2, S, P2, C), F32),
            pltpu.VMEM((2, 2, P2, C), F32),
        ],
        compiler_params=params(),
        cost_estimate=cost(16 * 128 * 3 * C * C * 2, 28 * 2**20),
        name="border",
    )(place, rim, stats, y, turned_latents, weights)
    parts = pl.pallas_call(
        merge_kernel,
        out_shape=jax.ShapeDtypeStruct((32, P2, 128), F32),
        in_specs=[vmem] * 4,
        out_specs=vmem,
        compiler_params=params(),
        name="merge",
    )(*neighbours(stats, "rows"))
    parts = exchange(parts[None]).reshape(32, P2, 128)
    pixels = 16
    out = pl.pallas_call(
        attend_kernel,
        grid=(S * S // pixels,),
        out_shape=jax.ShapeDtypeStruct((T, S * S, C), BF),
        in_specs=[pl.BlockSpec((pixels, 2, P2, C), lambda i: (i, 0, 0, 0)), whole(32, P2, 128)] + [whole(C, C)] * 4,
        out_specs=pl.BlockSpec((T, pixels, C), lambda i: (0, i, 0)),
        scratch_shapes=[pltpu.VMEM((2, 2, P2, C), F32)],
        compiler_params=params(),
        cost_estimate=cost(2048 * C * C * 2 * 6, 8 * 2**20),
        name="attend",
    )(mid, parts, w_query, w_key, w_value, w_out)
    back = lax.all_to_all(out[:, None], "tm", split_axis=0, concat_axis=1, tiled=True)
    back = back.reshape(16, 2, S, S, C).transpose(1, 2, 0, 3, 4)
    return back.reshape(1, 16, 128, C)


def solution(mesh):
    in_specs = (P("tm", "rows", None, None), P(), P(), P(), P(), P())
    out_specs = P("tm", "rows", None, None)
    return jax.shard_map(local, mesh=mesh, in_specs=in_specs, out_specs=out_specs, check_vma=False)
```

```python
import jax
import jax.numpy as jnp
from jax import lax
from jax.experimental import pallas as pl
from jax.experimental.pallas import tpu as pltpu
from jax.sharding import Mesh
from jax.sharding import PartitionSpec as P

GROUPS = 32
T = 32
C = 512
S = 8
W = S + 2
P2 = T // 2
MSG = 104
TM = ("x", "y", "core")
EPS = 1e-6
BF, F32 = jnp.bfloat16, jnp.float32
HI = lax.Precision.HIGHEST


def iota(shape, dim):
    return lax.broadcasted_iota(jnp.int32, shape, dim)


def dot(a, b, precision=None):
    return jnp.dot(a, b, preferred_element_type=F32, precision=precision)


def params():
    return pltpu.CompilerParams(vmem_limit_bytes=56 * 2**20)


def cost(flops, nbytes):
    return pl.CostEstimate(flops=flops, bytes_accessed=nbytes, transcendentals=0)


def to_groups(lane):
    return (iota((C, 128), 0) // 16 + lane == iota((C, 128), 1)).astype(F32)


def from_groups(lane, dtype=F32):
    return (iota((128, C), 1) // 16 + lane == iota((128, C), 0)).astype(dtype)


def group_stats(mean, m2, count, lane):
    group_mean = dot(mean, to_groups(lane), HI) * (1.0 / 16.0)
    off = mean - dot(group_mean, from_groups(lane), HI)
    return group_mean + dot(m2 + count * (off * off), to_groups(lane + 32), HI)


def merge(parts, count):
    n = parts.shape[0]
    total = jnp.sum(parts, axis=0)
    mean = total * (1.0 / n)
    off = parts - mean[None]
    between = pltpu.roll(jnp.sum(off * off, axis=0), 32, 1)
    is_mean = (iota(total.shape, 1) // 32) % 2 == 0
    return jnp.where(is_mean, mean, total + count * between)


def split_terms(v):
    high = v.astype(BF).astype(F32)
    middle = (v - high).astype(BF).astype(F32)
    return jnp.concatenate([high, middle, v - high - middle, jnp.zeros_like(v)], axis=1)


def join_terms(v):
    return sum(v[:, 128 * i : 128 * i + 128].astype(F32) for i in range(3))


def latent_stats_kernel(x_ref, up_ref, down_ref, out_ref):
    n = x_ref.shape[0]
    step = 256

    def add(i, total):
        rows = x_ref[pl.ds(pl.multiple_of(i * step, step), step), :].astype(F32)
        return total + jnp.sum(rows.reshape(step // 8, 8, C), axis=0)

    total = lax.fori_loop(0, n // step, add, jnp.zeros((8, C), F32))
    mean = jnp.sum(total, axis=0, keepdims=True) * (1.0 / n)

    def add_square(i, total):
        rows = x_ref[pl.ds(pl.multiple_of(i * step, step), step), :].astype(F32) - mean
        return total + jnp.sum((rows * rows).reshape(step // 8, 8, C), axis=0)

    total = lax.fori_loop(0, n // step, add_square, jnp.zeros((8, C), F32))
    m2 = jnp.sum(total, axis=0, keepdims=True)
    wide = lambda v: jnp.broadcast_to(v, (8, C))
    row = split_terms(group_stats(wide(mean), wide(m2), float(n), 0))
    row = jnp.concatenate([row, jnp.zeros_like(row)], axis=0).astype(BF)
    out_ref[...] = row
    up_ref[:128, :] = x_ref[n - 128 :, :]
    down_ref[:128, :] = x_ref[:128, :]
    up_ref[128:, :] = row
    down_ref[128:, :] = row


def finish(whole, count):
    is_mean = (iota(whole.shape, 1) // 32) % 2 == 0
    return jnp.where(is_mean, whole, lax.rsqrt(whole * (1.0 / count) + EPS))


def message_kernel(x_ref, up_ref, down_ref, own_ref, far_ref, out_ref, wide, sides):
    step = pl.program_id(0)

    @pl.when(step == 0)
    def _():
        n = 2048.0 * 16.0
        parts = [own_ref[...], far_ref[...], up_ref[128:, :], down_ref[128:, :]]
        whole = merge(jnp.stack([join_terms(v)[:8] for v in parts]), n)
        row = split_terms(jnp.where(iota(whole.shape, 1) < 64, finish(whole, 4.0 * n), 0.0))
        for q in range(4):
            lanes = slice(128 * q, 128 * q + 128)
            wide[q, 0] = up_ref[:128, lanes].astype(F32)
            wide[q, 17] = down_ref[:128, lanes].astype(F32)
            wide[q, 1:17] = x_ref[:, :, lanes].astype(F32)
            for half in range(2):
                sides[q, half] = jnp.zeros((16 * 24, 128), F32)
                sides[q, half, pl.ds(20, 16, stride=24), :] = jnp.broadcast_to(row[:1, lanes], (16, 128))
                for r in range(W):
                    left = wide[q, S * half + r, pl.ds(7, 15, stride=8), :]
                    right = wide[q, S * half + r, pl.ds(8, 15, stride=8), :]
                    sides[q, half, pl.ds(24 + r, 15, stride=24), :] = left
                    sides[q, half, pl.ds(W + r, 15, stride=24), :] = right

    for k in range(4):
        for half in range(2):
            cb = 4 * step + k
            cols = pl.ds(pl.multiple_of(8 * cb, 8), 8)
            rows = pl.ds(pl.multiple_of(24 * cb, 8), 24)
            for q in range(4):
                main = wide[q, S * half : S * half + W, cols, :].reshape(W * S, 128)
                side = sides[q, half, rows, :]
                message = jnp.concatenate([main, side], axis=0).astype(BF)
                out_ref[2 * k + half, :, 128 * q : 128 * q + 128] = message


def weights_kernel(w_ref, out_ref):
    g = [w_ref[i, 0, 0].astype(F32) for i in range(3)]
    ends = (g[0] + g[2]) * 0.5
    out_ref[0, 0, 0] = w_ref[0, 0, 0]
    out_ref[1, 0, 0] = (ends + g[1] * 0.5).astype(BF)
    out_ref[2, 0, 0] = (ends - g[1] * 0.5).astype(BF)
    out_ref[3, 0, 0] = w_ref[2, 0, 0]


def turned(in_ref, first, pixels):
    rows = pixels * T
    to, at = iota((rows, rows), 0), iota((rows, rows), 1)
    frame = 2 * (to % P2) + (to // P2) % 2
    turn = (at == frame * pixels + to // T).astype(BF)
    values = in_ref[:, first : first + pixels, :].reshape(rows, C)
    return dot(turn, values).reshape(pixels, 2, P2, C)


def activate(values, norm):
    u = (values - norm[0][None]) * norm[1][None]
    return (u / (1.0 + jnp.exp(-u))).astype(BF).astype(F32)


def time_terms(act):
    pixels = act.shape[0]
    even, odd = act[:, 0], act[:, 1]
    start = iota((pixels * P2, C), 0) % P2 == 0

    def before(v):
        v = pltpu.roll(v.reshape(pixels * P2, C), 1, 0)
        return jnp.where(start, 0.0, v).reshape(pixels, P2, C)

    even1, odd1 = before(even), before(odd)
    return [v.astype(BF) for v in (even1 - even, odd1 + even, even - odd1, odd1 - odd)]


def signs(j):
    return jnp.where(j == 3, 0.0, 1.0), jnp.where(j == 0, 0.0, jnp.where(j == 1, 1.0, -1.0))


def conv_kernel(place_ref, in_ref, w_ref, mid_ref, stats_ref, terms, latent, y_ref, norm):
    j = pl.program_id(0)

    @pl.when(j == 0)
    def _():
        block, z = place_ref[0], place_ref[1]
        half, column = block % 2, block // 2
        above = (half == 0) & (z == 0)
        below = (half == 1) & (z == 3)
        tail = in_ref[:, 96:MSG, :].reshape(T * 8, C)
        row = iota((T, T * 8), 0)
        row = 2 * (row % P2) + row // P2
        pieces = dot((iota((T, T * 8), 1) == row * 8 + 4).astype(BF), tail).astype(BF)
        for i in range(2):
            norm[i] = sum(
                dot(pieces[:, 128 * k : 128 * k + 128], from_groups(32 * i, BF)) for k in range(3)
            ).reshape(2, P2, C)

        for k in range(W // 2):
            values = turned(in_ref, 16 * k, 16)
            act = activate(values, norm)
            if k == 0:
                act = jnp.where(above & (iota(act.shape, 0) < S), 0.0, act)
            if k == W // 2 - 1:
                act = jnp.where(below & (iota(act.shape, 0) >= S), 0.0, act)
            for i in range(2):
                r = 2 * k + i - 1
                if 0 <= r < S:
                    latent[S * r : S * r + S] = values[S * i : S * i + S].astype(BF)
            at = slice(2 * k, 2 * k + 2)
            for i, v in enumerate(time_terms(act)):
                v = v.reshape(2, S, P2, C)
                terms[i, at, 1:S, :, 0:C] = v[:, : S - 1]
                terms[i, at, :, :, C : 2 * C] = v
                terms[i, at, 0 : S - 1, :, 2 * C :] = v[:, 1:]
        for first, pixels in ((80, 16), (96, 8)):
            act = activate(turned(in_ref, first, pixels), norm)
            p = iota(act.shape, 0) + first
            out = (column == 0) & (p < 90) | (column == 15) & (p >= 90)
            out = out | above & ((p == 80) | (p == 90)) | below & ((p == 89) | (p == 99))
            for i, v in enumerate(time_terms(jnp.where(out, 0.0, act))):
                for q in range(pixels):
                    if first + q < 90:
                        terms[i, first + q - 80, 0, :, 0:C] = v[q]
                    elif first + q < 100:
                        terms[i, first + q - 90, S - 1, :, 2 * C :] = v[q]
        y_ref[...] = jnp.zeros_like(y_ref)

    even, odd = signs(j)
    for q in range(S // 2):
        m = sum(
            dot(terms[j, 2 * q + b : 2 * q + b + 2].reshape(2 * S * P2, 3 * C), w_ref[0, b].reshape(3 * C, C))
            for b in range(3)
        ).reshape(2 * S, P2, C)
        at = slice(16 * q, 16 * q + 16)
        y_ref[at, 0] += even * m
        y_ref[at, 1] += odd * m

    @pl.when(j == 3)
    def _():
        total = jnp.zeros((2, P2, C), F32)
        for p in range(S * S):
            v = (latent[p].astype(F32) + y_ref[p]).astype(BF)
            mid_ref[p] = v
            total = total + v.astype(F32)
        mean = total * (1.0 / (S * S))
        total = jnp.zeros((2, P2, C), F32)
        for p in range(S * S):
            off = mid_ref[p].astype(F32) - mean
            total = total + off * off
        stats = sum(group_stats(mean[i], total[i], float(S * S), 64 * i) for i in range(2))
        stats_ref[...] = jnp.broadcast_to(stats[None], stats_ref.shape)


def merge_kernel(parts_ref, out_ref):
    whole = merge(parts_ref[...], float(S * S * 16))
    out_ref[...] = jnp.broadcast_to(whole[None], out_ref.shape)


def attend_kernel(mid_ref, parts_ref, wq_ref, wk_ref, wv_ref, wo_ref, out_ref, norm):
    @pl.when(pl.program_id(0) == 0)
    def _():
        count = float(S * S * 16 * 8)
        whole = finish(merge(parts_ref[...], count), 16.0 * count)
        for i in range(2):
            for j in range(2):
                norm[i, j] = dot(whole, from_groups(64 * j + 32 * i), HI)

    pixels = mid_ref.shape[0]
    rows = pixels * T
    mid = mid_ref[...].astype(F32)
    flat = ((mid - norm[0][None]) * norm[1][None]).astype(BF).reshape(rows, C)
    query = dot(flat, wq_ref[...]).astype(BF)
    keys = dot(flat, wk_ref[...]).astype(BF)
    values = dot(flat, wv_ref[...]).astype(BF)
    n = 256
    row, column = iota((n, n), 0), iota((n, n), 1)
    frame = lambda v: 2 * (v % P2) + (v // P2) % 2
    seen = (row // T == column // T) & (frame(row) >= frame(column))
    parts = []
    for i in range(rows // n):
        at = slice(i * n, i * n + n)
        scores = lax.dot_general(
            query[at], keys[at], (((1,), (1,)), ((), ())), preferred_element_type=F32
        ) * (1.0 / (C**0.5))
        scores = jnp.where(seen, scores, -1e30)
        weights = jnp.exp(scores - jnp.max(scores, axis=1, keepdims=True))
        weights = (weights / jnp.sum(weights, axis=1, keepdims=True)).astype(BF)
        parts.append(dot(weights, values[at]).astype(BF))
    update = dot(jnp.concatenate(parts, axis=0), wo_ref[...])
    out = (mid.reshape(rows, C) + update).astype(BF)
    to = iota((rows, rows), 0)
    frame = to // pixels
    turn = (iota((rows, rows), 1) == (to % pixels) * T + (frame % 2) * P2 + frame // 2).astype(BF)
    out_ref[...] = dot(turn, out).astype(BF).reshape(T, pixels, C)


def local(latents, conv_weight, w_query, w_key, w_value, w_out):
    x = latents.reshape(16, 128, C)
    vmem = pl.BlockSpec(memory_space=pltpu.VMEM)
    smem = pl.BlockSpec(memory_space=pltpu.SMEM)
    whole = lambda *shape: pl.BlockSpec(shape, lambda i: (0,) * len(shape))
    exchange = lambda v, axes: lax.all_to_all(v[None], axes, split_axis=1, concat_axis=0, tiled=True)[:, 0]
    place = jnp.stack([lax.axis_index(TM), lax.axis_index("rows")]).astype(jnp.int32)

    row = jax.ShapeDtypeStruct((144, C), BF)
    up, down, own = pl.pallas_call(
        latent_stats_kernel,
        out_shape=(row, row, jax.ShapeDtypeStruct((16, C), BF)),
        in_specs=[vmem],
        out_specs=(vmem,) * 3,
        compiler_params=params(),
        cost_estimate=cost(2048 * C * 4, 2048 * C * 2),
        name="latent_stats",
    )(x.reshape(2048, C))
    around = lambda v, by: lax.ppermute(v, "rows", [(i, (i + by) % 4) for i in range(4)])
    up, down, far = around(up, 1), around(down, 3), around(own, 2)
    messages = pl.pallas_call(
        message_kernel,
        grid=(4,),
        out_shape=jax.ShapeDtypeStruct((32, MSG, C), BF),
        in_specs=[whole(16, 128, C), whole(144, C), whole(144, C), whole(16, C), whole(16, C)],
        out_specs=pl.BlockSpec((8, MSG, C), lambda i: (i, 0, 0)),
        scratch_shapes=[pltpu.VMEM((4, 18, 128, 128), F32), pltpu.VMEM((4, 2, 16 * 24, 128), F32)],
        compiler_params=params(),
        cost_estimate=cost(2**22, 6 * 2**20),
        name="messages",
    )(x, up, down, own, far)
    patch = exchange(messages, TM)
    weights = pl.pallas_call(
        weights_kernel,
        grid=(3, 3),
        out_shape=jax.ShapeDtypeStruct((4, 3, 3, C, C), BF),
        in_specs=[pl.BlockSpec((3, 1, 1, C, C), lambda b, e: (0, b, e, 0, 0))],
        out_specs=pl.BlockSpec((4, 1, 1, C, C), lambda b, e: (0, b, e, 0, 0)),
        compiler_params=params(),
        cost_estimate=cost(9 * 4 * C * C, 9 * 7 * C * C * 2),
        name="weights",
    )(conv_weight)

    mid, stats = pl.pallas_call(
        conv_kernel,
        grid=(4,),
        out_shape=(jax.ShapeDtypeStruct((S * S, 2, P2, C), BF), jax.ShapeDtypeStruct((8, P2, 128), F32)),
        in_specs=[smem, whole(T, MSG, C), pl.BlockSpec((1, 3, 3, C, C), lambda i: (i, 0, 0, 0, 0))],
        out_specs=(whole(S * S, 2, P2, C), whole(8, P2, 128)),
        scratch_shapes=[
            pltpu.VMEM((4, W, S, P2, 3 * C), BF),
            pltpu.VMEM((S * S, 2, P2, C), BF),
            pltpu.VMEM((S * S, 2, P2, C), F32),
            pltpu.VMEM((2, 2, P2, C), F32),
        ],
        compiler_params=params(),
        cost_estimate=cost(1024 * 36 * C * C * 2, 28 * 2**20),
        name="conv",
    )(place, patch, weights)
    parts = pl.pallas_call(
        merge_kernel,
        out_shape=jax.ShapeDtypeStruct((16, P2, 128), F32),
        in_specs=[vmem],
        out_specs=vmem,
        compiler_params=params(),
        name="merge",
    )(exchange(stats, ("core", "rows")))
    parts = exchange(parts, ("x", "y"))
    pixels = 16
    out = pl.pallas_call(
        attend_kernel,
        grid=(S * S // pixels,),
        out_shape=jax.ShapeDtypeStruct((T, S * S, C), BF),
        in_specs=[pl.BlockSpec((pixels, 2, P2, C), lambda i: (i, 0, 0, 0)), whole(16, P2, 128)] + [whole(C, C)] * 4,
        out_specs=pl.BlockSpec((T, pixels, C), lambda i: (0, i, 0)),
        scratch_shapes=[pltpu.VMEM((2, 2, P2, C), F32)],
        compiler_params=params(),
        cost_estimate=cost(2048 * C * C * 2 * 6, 8 * 2**20),
        name="attend",
    )(mid, parts, w_query, w_key, w_value, w_out)
    back = exchange(out, TM)
    back = back.reshape(16, 2, S, S, C).transpose(1, 2, 0, 3, 4)
    return back.reshape(1, 16, 128, C)


def solution(mesh):
    mesh = Mesh(mesh.devices.reshape(4, 4, 2, 4), TM + ("rows",))
    in_specs = (P(TM, "rows", None, None), P(), P(), P(), P(), P())
    out_specs = P(TM, "rows", None, None)
    return jax.shard_map(local, mesh=mesh, in_specs=in_specs, out_specs=out_specs, check_vma=False)
```

```python
import jax
import jax.numpy as jnp
from jax import lax
from jax.experimental import pallas as pl
from jax.experimental.pallas import tpu as pltpu
from jax.sharding import Mesh
from jax.sharding import PartitionSpec as P

GROUPS = 32
T = 32
C = 512
S = 8
W = S + 2
P2 = T // 2
MSG = 104
TM = ("x", "y", "core")
EPS = 1e-6
BF, F32 = jnp.bfloat16, jnp.float32
HI = lax.Precision.HIGHEST


def iota(shape, dim):
    return lax.broadcasted_iota(jnp.int32, shape, dim)


def dot(a, b, precision=None):
    return jnp.dot(a, b, preferred_element_type=F32, precision=precision)


def params():
    return pltpu.CompilerParams(vmem_limit_bytes=56 * 2**20)


def cost(flops, nbytes):
    return pl.CostEstimate(flops=flops, bytes_accessed=nbytes, transcendentals=0)


def to_groups(lane):
    return (iota((C, 128), 0) // 16 + lane == iota((C, 128), 1)).astype(F32)


def from_groups(lane, dtype=F32):
    return (iota((128, C), 1) // 16 + lane == iota((128, C), 0)).astype(dtype)


def group_stats(mean, m2, count, lane):
    group_mean = dot(mean, to_groups(lane), HI) * (1.0 / 16.0)
    off = mean - dot(group_mean, from_groups(lane), HI)
    return group_mean + dot(m2 + count * (off * off), to_groups(lane + 32), HI)


def merge(parts, count):
    n = parts.shape[0]
    total = jnp.sum(parts, axis=0)
    mean = total * (1.0 / n)
    off = parts - mean[None]
    between = pltpu.roll(jnp.sum(off * off, axis=0), 32, 1)
    is_mean = (iota(total.shape, 1) // 32) % 2 == 0
    return jnp.where(is_mean, mean, total + count * between)


def split_terms(v):
    high = v.astype(BF).astype(F32)
    middle = (v - high).astype(BF).astype(F32)
    return jnp.concatenate([high, middle, v - high - middle, jnp.zeros_like(v)], axis=1)


def join_terms(v):
    return sum(v[:, 128 * i : 128 * i + 128].astype(F32) for i in range(3))


def latent_stats_kernel(x_ref, up_ref, down_ref, out_ref):
    n = x_ref.shape[0]
    step = 256

    def add(i, total):
        rows = x_ref[pl.ds(pl.multiple_of(i * step, step), step), :].astype(F32)
        return total + jnp.sum(rows.reshape(step // 8, 8, C), axis=0)

    total = lax.fori_loop(0, n // step, add, jnp.zeros((8, C), F32))
    mean = jnp.sum(total, axis=0, keepdims=True) * (1.0 / n)

    def add_square(i, total):
        rows = x_ref[pl.ds(pl.multiple_of(i * step, step), step), :].astype(F32) - mean
        return total + jnp.sum((rows * rows).reshape(step // 8, 8, C), axis=0)

    total = lax.fori_loop(0, n // step, add_square, jnp.zeros((8, C), F32))
    m2 = jnp.sum(total, axis=0, keepdims=True)
    wide = lambda v: jnp.broadcast_to(v, (8, C))
    row = split_terms(group_stats(wide(mean), wide(m2), float(n), 0))
    row = jnp.concatenate([row, jnp.zeros_like(row)], axis=0).astype(BF)
    out_ref[...] = row
    up_ref[:128, :] = x_ref[n - 128 :, :]
    down_ref[:128, :] = x_ref[:128, :]
    up_ref[128:, :] = row
    down_ref[128:, :] = row


def finish(whole, count):
    is_mean = (iota(whole.shape, 1) // 32) % 2 == 0
    return jnp.where(is_mean, whole, lax.rsqrt(whole * (1.0 / count) + EPS))


def message_kernel(x_ref, up_ref, down_ref, own_ref, far_ref, out_ref, wide, sides):
    step = pl.program_id(0)

    @pl.when(step == 0)
    def _():
        n = 2048.0 * 16.0
        parts = [own_ref[...], far_ref[...], up_ref[128:, :], down_ref[128:, :]]
        whole = merge(jnp.stack([join_terms(v)[:8] for v in parts]), n)
        row = split_terms(jnp.where(iota(whole.shape, 1) < 64, finish(whole, 4.0 * n), 0.0))
        for q in range(4):
            lanes = slice(128 * q, 128 * q + 128)
            wide[q, 0] = up_ref[:128, lanes].astype(F32)
            wide[q, 17] = down_ref[:128, lanes].astype(F32)
            wide[q, 1:17] = x_ref[:, :, lanes].astype(F32)
            for half in range(2):
                sides[q, half] = jnp.zeros((16 * 24, 128), F32)
                sides[q, half, pl.ds(20, 16, stride=24), :] = jnp.broadcast_to(row[:1, lanes], (16, 128))
                for r in range(W):
                    left = wide[q, S * half + r, pl.ds(7, 15, stride=8), :]
                    right = wide[q, S * half + r, pl.ds(8, 15, stride=8), :]
                    sides[q, half, pl.ds(24 + r, 15, stride=24), :] = left
                    sides[q, half, pl.ds(W + r, 15, stride=24), :] = right

    for k in range(4):
        for half in range(2):
            cb = 4 * step + k
            cols = pl.ds(pl.multiple_of(8 * cb, 8), 8)
            rows = pl.ds(pl.multiple_of(24 * cb, 8), 24)
            for q in range(4):
                main = wide[q, S * half : S * half + W, cols, :].reshape(W * S, 128)
                side = sides[q, half, rows, :]
                message = jnp.concatenate([main, side], axis=0).astype(BF)
                out_ref[2 * k + half, :, 128 * q : 128 * q + 128] = message


def weights_kernel(w_ref, out_ref):
    def products(g):
        ends = (g[0] + g[2]) * 0.5
        middle = g[1] * 0.5
        return g[0], ends + middle, ends - middle, g[2]

    w = [[w_ref[a, 0, e].astype(F32) for e in range(3)] for a in range(3)]
    columns = [products(w[a]) for a in range(3)]
    for l in range(4):
        for j, v in enumerate(products([columns[a][l] for a in range(3)])):
            out_ref[4 * j + l, 0] = v.astype(BF)


def turned(in_ref, first, pixels):
    rows = pixels * T
    to, at = iota((rows, rows), 0), iota((rows, rows), 1)
    frame = 2 * (to % P2) + (to // P2) % 2
    turn = (at == frame * pixels + to // T).astype(BF)
    values = in_ref[:, first : first + pixels, :].reshape(rows, C)
    return dot(turn, values).reshape(pixels, 2, P2, C)


def activate(values, norm):
    u = (values - norm[0][None]) * norm[1][None]
    return (u / (1.0 + jnp.exp(-u))).astype(BF).astype(F32)


def time_terms(act):
    pixels = act.shape[0]
    even, odd = act[:, 0], act[:, 1]
    start = iota((pixels * P2, C), 0) % P2 == 0

    def before(v):
        v = pltpu.roll(v.reshape(pixels * P2, C), 1, 0)
        return jnp.where(start, 0.0, v).reshape(pixels, P2, C)

    even1, odd1 = before(even), before(odd)
    return even1 - even, odd1 + even, even - odd1, odd1 - odd


def signs(j):
    return jnp.where(j == 3, 0.0, 1.0), jnp.where(j == 0, 0.0, jnp.where(j == 1, 1.0, -1.0))


def conv_kernel(place_ref, in_ref, w_ref, mid_ref, stats_ref, terms, sides, latent, y_ref, norm, held, sems):
    def fetch(j, l):
        slot = 4 * (j % 2) + l
        return pltpu.make_async_copy(w_ref.at[4 * j + l], held.at[slot], sems.at[slot])

    for j in range(2):
        for l in range(4):
            fetch(j, l).start()

    block, z = place_ref[0], place_ref[1]
    half, column = block % 2, block // 2
    above = (half == 0) & (z == 0)
    below = (half == 1) & (z == 3)
    tail = in_ref[:, 96:MSG, :].reshape(T * 8, C)
    row = iota((T, T * 8), 0)
    row = 2 * (row % P2) + row // P2
    pieces = dot((iota((T, T * 8), 1) == row * 8 + 4).astype(BF), tail).astype(BF)
    for i in range(2):
        norm[i] = sum(
            dot(pieces[:, 128 * k : 128 * k + 128], from_groups(32 * i, BF)) for k in range(3)
        ).reshape(2, P2, C)

    for first, pixels in ((80, 16), (96, 8)):
        act = activate(turned(in_ref, first, pixels), norm)
        p = iota(act.shape, 0) + first
        out = (column == 0) & (p < 90) | (column == 15) & (p >= 90)
        out = out | above & ((p == 80) | (p == 90)) | below & ((p == 89) | (p == 99))
        for j, v in enumerate(time_terms(jnp.where(out, 0.0, act))):
            for q in range(pixels):
                if first + q < 100:
                    sides[j, (first + q - 80) // W, (first + q) % W] = v[q]
    for k in range(W // 2):
        values = turned(in_ref, 16 * k, 16)
        act = activate(values, norm)
        if k == 0:
            act = jnp.where(above & (iota(act.shape, 0) < S), 0.0, act)
        if k == W // 2 - 1:
            act = jnp.where(below & (iota(act.shape, 0) >= S), 0.0, act)
        for i in range(2):
            r = 2 * k + i - 1
            if 0 <= r < S:
                latent[S * r : S * r + S] = values[S * i : S * i + S].astype(BF)
        at = slice(2 * k, 2 * k + 2)
        for j, v in enumerate(time_terms(act)):
            left, right = sides[j, 0, at][:, None], sides[j, 1, at][:, None]
            v = jnp.concatenate([left, v.reshape(2, S, P2, C), right], axis=1).reshape(2, W // 2, 2, P2, C)
            even, odd = v[:, :, 0], v[:, :, 1]
            before, after, odd_before = even[:, :-1], even[:, 1:], odd[:, :-1]
            for l, u in enumerate((before - after, odd_before + after, after - odd_before, odd_before - odd[:, 1:])):
                terms[j, l, at] = u.astype(BF)
    y_ref[...] = jnp.zeros_like(y_ref)

    def term(j, _):
        @pl.when((j == 1) | (j == 2))
        def _():
            for l in range(4):
                fetch(j + 1, l).start()

        even, odd = signs(j)
        for q in range(2):
            m = []
            for l in range(4):
                if q == 0:
                    fetch(j, l).wait()
                m.append(
                    sum(
                        dot(terms[j, l, 4 * q + b : 4 * q + b + 4].reshape(16 * P2, C), held[4 * (j % 2) + l, b])
                        for b in range(3)
                    ).reshape(4, 4, P2, C)
                )
            at = slice(4 * q, 4 * q + 4)
            for c, v in enumerate((m[0] + m[1] + m[2], m[1] - m[2] - m[3])):
                y_ref[at, :, c, 0] += even * v
                y_ref[at, :, c, 1] += odd * v
        return 0

    lax.fori_loop(0, 4, term, 0)

    total = jnp.zeros((2, P2, C), F32)
    for p in range(S * S):
        v = (latent[p].astype(F32) + y_ref[p // S, p % S // 2, p % 2]).astype(BF)
        mid_ref[p] = v
        total = total + v.astype(F32)
    mean = total * (1.0 / (S * S))
    total = jnp.zeros((2, P2, C), F32)
    for p in range(S * S):
        off = mid_ref[p].astype(F32) - mean
        total = total + off * off
    stats = sum(group_stats(mean[i], total[i], float(S * S), 64 * i) for i in range(2))
    stats_ref[...] = jnp.broadcast_to(stats[None], stats_ref.shape)


def merge_kernel(parts_ref, out_ref):
    whole = merge(parts_ref[...], float(S * S * 16))
    out_ref[...] = jnp.broadcast_to(whole[None], out_ref.shape)


def attend_kernel(mid_ref, parts_ref, score_ref, update_ref, out_ref, norm):
    @pl.when(pl.program_id(0) == 0)
    def _():
        count = float(S * S * 16 * 8)
        whole = finish(merge(parts_ref[...], count), 16.0 * count)
        for i in range(2):
            for j in range(2):
                norm[i, j] = dot(whole, from_groups(64 * j + 32 * i), HI)

    pixels = mid_ref.shape[0]
    rows = pixels * T
    mid = mid_ref[...].astype(F32)
    flat = ((mid - norm[0][None]) * norm[1][None]).astype(BF).reshape(rows, C)
    query = dot(flat, score_ref[...]).astype(BF)
    n = 256
    row, column = iota((n, n), 0), iota((n, n), 1)
    frame = lambda v: 2 * (v % P2) + (v // P2) % 2
    seen = (row // T == column // T) & (frame(row) >= frame(column))
    parts = []
    for i in range(rows // n):
        at = slice(i * n, i * n + n)
        scores = lax.dot_general(query[at], flat[at], (((1,), (1,)), ((), ())), preferred_element_type=F32)
        scores = jnp.where(seen, scores, -1e30)
        weights = jnp.exp(scores - jnp.max(scores, axis=1, keepdims=True))
        weights = (weights / jnp.sum(weights, axis=1, keepdims=True)).astype(BF)
        parts.append(dot(weights, flat[at]).astype(BF))
    update = dot(jnp.concatenate(parts, axis=0), update_ref[...])
    out = (mid.reshape(rows, C) + update).astype(BF)
    to = iota((n, n), 0)
    frame = to // S
    turn = (iota((n, n), 1) == (to % S) * T + (frame % 2) * P2 + frame // 2).astype(BF)
    for i in range(rows // (2 * n)):
        pair = [dot(turn, out[(2 * i + k) * n : (2 * i + k + 1) * n]).reshape(T, S, C) for k in range(2)]
        out_ref[:, 16 * i : 16 * i + 16, :] = jnp.concatenate(pair, axis=1).astype(BF)


def local(latents, conv_weight, w_query, w_key, w_value, w_out):
    x = latents.reshape(16, 128, C)
    vmem = pl.BlockSpec(memory_space=pltpu.VMEM)
    smem = pl.BlockSpec(memory_space=pltpu.SMEM)
    whole = lambda *shape: pl.BlockSpec(shape, lambda i: (0,) * len(shape))
    exchange = lambda v, axes: lax.all_to_all(v[None], axes, split_axis=1, concat_axis=0, tiled=True)[:, 0]
    place = jnp.stack([lax.axis_index(TM), lax.axis_index("rows")]).astype(jnp.int32)

    row = jax.ShapeDtypeStruct((144, C), BF)
    up, down, own = pl.pallas_call(
        latent_stats_kernel,
        out_shape=(row, row, jax.ShapeDtypeStruct((16, C), BF)),
        in_specs=[vmem],
        out_specs=(vmem,) * 3,
        compiler_params=params(),
        cost_estimate=cost(2048 * C * 4, 2048 * C * 2),
        name="latent_stats",
    )(x.reshape(2048, C))
    around = lambda v, by: lax.ppermute(v, "rows", [(i, (i + by) % 4) for i in range(4)])
    up, down, far = around(up, 1), around(down, 3), around(own, 2)
    messages = pl.pallas_call(
        message_kernel,
        grid=(4,),
        out_shape=jax.ShapeDtypeStruct((32, MSG, C), BF),
        in_specs=[whole(16, 128, C), whole(144, C), whole(144, C), whole(16, C), whole(16, C)],
        out_specs=pl.BlockSpec((8, MSG, C), lambda i: (i, 0, 0)),
        scratch_shapes=[pltpu.VMEM((4, 18, 128, 128), F32), pltpu.VMEM((4, 2, 16 * 24, 128), F32)],
        compiler_params=params(),
        cost_estimate=cost(2**22, 6 * 2**20),
        name="messages",
    )(x, up, down, own, far)
    patch = exchange(messages, TM)
    weights = pl.pallas_call(
        weights_kernel,
        grid=(3, 4),
        out_shape=jax.ShapeDtypeStruct((16, 3, C, C), BF),
        in_specs=[pl.BlockSpec((3, 1, 3, 128, C), lambda b, i: (0, b, 0, i, 0))],
        out_specs=pl.BlockSpec((16, 1, 128, C), lambda b, i: (0, b, i, 0)),
        compiler_params=params(),
        cost_estimate=cost(9 * 8 * C * C, 75 * C * C * 2),
        name="weights",
    )(conv_weight)
    score = dot(w_query, w_key.T) * (1.0 / C**0.5)
    score, update = score.astype(BF), dot(w_value, w_out).astype(BF)

    mid, stats = pl.pallas_call(
        conv_kernel,
        out_shape=(jax.ShapeDtypeStruct((S * S, 2, P2, C), BF), jax.ShapeDtypeStruct((8, P2, 128), F32)),
        in_specs=[smem, vmem, pl.BlockSpec(memory_space=pl.ANY)],
        out_specs=(vmem, vmem),
        scratch_shapes=[
            pltpu.VMEM((4, 4, W, S // 2, P2, C), BF),
            pltpu.VMEM((4, 2, W, P2, C), F32),
            pltpu.VMEM((S * S, 2, P2, C), BF),
            pltpu.VMEM((S, S // 2, 2, 2, P2, C), F32),
            pltpu.VMEM((2, 2, P2, C), F32),
            pltpu.VMEM((8, 3, C, C), BF),
            pltpu.SemaphoreType.DMA((8,)),
        ],
        compiler_params=params(),
        cost_estimate=cost(512 * 48 * C * C * 2, 28 * 2**20),
        name="conv",
    )(place, patch, weights)
    parts = pl.pallas_call(
        merge_kernel,
        out_shape=jax.ShapeDtypeStruct((16, P2, 128), F32),
        in_specs=[vmem],
        out_specs=vmem,
        compiler_params=params(),
        name="merge",
    )(exchange(stats, ("core", "rows")))
    parts = exchange(parts, ("x", "y"))
    pixels = 32
    out = pl.pallas_call(
        attend_kernel,
        grid=(S * S // pixels,),
        out_shape=jax.ShapeDtypeStruct((T, S * S, C), BF),
        in_specs=[pl.BlockSpec((pixels, 2, P2, C), lambda i: (i, 0, 0, 0)), whole(16, P2, 128)] + [whole(C, C)] * 2,
        out_specs=pl.BlockSpec((T, pixels, C), lambda i: (0, i, 0)),
        scratch_shapes=[pltpu.VMEM((2, 2, P2, C), F32)],
        compiler_params=params(),
        cost_estimate=cost(2048 * C * C * 2 * 4, 8 * 2**20),
        name="attend",
    )(mid, parts, score, update)
    back = exchange(out, TM)
    back = back.reshape(16, 2, S, S, C).transpose(1, 2, 0, 3, 4)
    return back.reshape(1, 16, 128, C)


def solution(mesh):
    mesh = Mesh(mesh.devices.reshape(4, 4, 2, 4), TM + ("rows",))
    in_specs = (P(TM, "rows", None, None), P(), P(), P(), P(), P())
    out_specs = P(TM, "rows", None, None)
    return jax.shard_map(local, mesh=mesh, in_specs=in_specs, out_specs=out_specs, check_vma=False)
```

```python
import jax
import jax.numpy as jnp
from jax import lax
from jax.experimental import pallas as pl
from jax.experimental.pallas import tpu as pltpu
from jax.sharding import Mesh
from jax.sharding import PartitionSpec as P

GROUPS = 32
T = 32
C = 512
S = 8
W = S + 2
P2 = T // 2
MSG = 104
TM = ("x", "y", "core")
EPS = 1e-6
BF, F32 = jnp.bfloat16, jnp.float32
HI = lax.Precision.HIGHEST


def iota(shape, dim):
    return lax.broadcasted_iota(jnp.int32, shape, dim)


def dot(a, b, precision=None):
    return jnp.dot(a, b, preferred_element_type=F32, precision=precision)


def params():
    return pltpu.CompilerParams(vmem_limit_bytes=56 * 2**20)


def cost(flops, nbytes):
    return pl.CostEstimate(flops=flops, bytes_accessed=nbytes, transcendentals=0)


def to_groups(lane):
    return (iota((C, 128), 0) // 16 + lane == iota((C, 128), 1)).astype(F32)


def from_groups(lane, dtype=F32):
    return (iota((128, C), 1) // 16 + lane == iota((128, C), 0)).astype(dtype)


def group_stats(mean, m2, count, lane):
    group_mean = dot(mean, to_groups(lane), HI) * (1.0 / 16.0)
    off = mean - dot(group_mean, from_groups(lane), HI)
    return group_mean + dot(m2 + count * (off * off), to_groups(lane + 32), HI)


def merge(parts, count):
    n = parts.shape[0]
    total = jnp.sum(parts, axis=0)
    mean = total * (1.0 / n)
    off = parts - mean[None]
    between = pltpu.roll(jnp.sum(off * off, axis=0), 32, 1)
    is_mean = (iota(total.shape, 1) // 32) % 2 == 0
    return jnp.where(is_mean, mean, total + count * between)


def split_terms(v):
    high = v.astype(BF).astype(F32)
    middle = (v - high).astype(BF).astype(F32)
    return jnp.concatenate([high, middle, v - high - middle, jnp.zeros_like(v)], axis=1)


def join_terms(v):
    return sum(v[:, 128 * i : 128 * i + 128].astype(F32) for i in range(3))


def latent_stats_kernel(x_ref, up_ref, down_ref, out_ref):
    n = x_ref.shape[0]
    step = 256

    def add(i, total):
        rows = x_ref[pl.ds(pl.multiple_of(i * step, step), step), :].astype(F32)
        return total + jnp.sum(rows.reshape(step // 8, 8, C), axis=0)

    total = lax.fori_loop(0, n // step, add, jnp.zeros((8, C), F32))
    mean = jnp.sum(total, axis=0, keepdims=True) * (1.0 / n)

    def add_square(i, total):
        rows = x_ref[pl.ds(pl.multiple_of(i * step, step), step), :].astype(F32) - mean
        return total + jnp.sum((rows * rows).reshape(step // 8, 8, C), axis=0)

    total = lax.fori_loop(0, n // step, add_square, jnp.zeros((8, C), F32))
    m2 = jnp.sum(total, axis=0, keepdims=True)
    wide = lambda v: jnp.broadcast_to(v, (8, C))
    row = split_terms(group_stats(wide(mean), wide(m2), float(n), 0))
    row = jnp.concatenate([row, jnp.zeros_like(row)], axis=0).astype(BF)
    out_ref[...] = row
    up_ref[:128, :] = x_ref[n - 128 :, :]
    down_ref[:128, :] = x_ref[:128, :]
    up_ref[128:, :] = row
    down_ref[128:, :] = row


def finish(whole, count):
    is_mean = (iota(whole.shape, 1) // 32) % 2 == 0
    return jnp.where(is_mean, whole, lax.rsqrt(whole * (1.0 / count) + EPS))


def message_kernel(x_ref, up_ref, down_ref, own_ref, far_ref, out_ref, wide, sides):
    step = pl.program_id(0)

    @pl.when(step == 0)
    def _():
        n = 2048.0 * 16.0
        parts = [own_ref[...], far_ref[...], up_ref[128:, :], down_ref[128:, :]]
        whole = merge(jnp.stack([join_terms(v)[:8] for v in parts]), n)
        row = split_terms(jnp.where(iota(whole.shape, 1) < 64, finish(whole, 4.0 * n), 0.0))
        for q in range(4):
            lanes = slice(128 * q, 128 * q + 128)
            wide[q, 0] = up_ref[:128, lanes].astype(F32)
            wide[q, 17] = down_ref[:128, lanes].astype(F32)
            wide[q, 1:17] = x_ref[:, :, lanes].astype(F32)
            for half in range(2):
                sides[q, half] = jnp.zeros((16 * 24, 128), F32)
                sides[q, half, pl.ds(20, 16, stride=24), :] = jnp.broadcast_to(row[:1, lanes], (16, 128))
                for r in range(W):
                    left = wide[q, S * half + r, pl.ds(7, 15, stride=8), :]
                    right = wide[q, S * half + r, pl.ds(8, 15, stride=8), :]
                    sides[q, half, pl.ds(24 + r, 15, stride=24), :] = left
                    sides[q, half, pl.ds(W + r, 15, stride=24), :] = right

    for k in range(4):
        for half in range(2):
            cb = 4 * step + k
            cols = pl.ds(pl.multiple_of(8 * cb, 8), 8)
            rows = pl.ds(pl.multiple_of(24 * cb, 8), 24)
            for q in range(4):
                main = wide[q, S * half : S * half + W, cols, :].reshape(W * S, 128)
                side = sides[q, half, rows, :]
                message = jnp.concatenate([main, side], axis=0).astype(BF)
                out_ref[2 * k + half, :, 128 * q : 128 * q + 128] = message


def weights_kernel(w_ref, out_ref):
    def products(g):
        ends = (g[0] + g[2]) * 0.5
        middle = g[1] * 0.5
        return g[0], ends + middle, ends - middle, g[2]

    w = [[w_ref[a, 0, e].astype(F32) for e in range(3)] for a in range(3)]
    columns = [products(w[a]) for a in range(3)]
    for l in range(4):
        for j, v in enumerate(products([columns[a][l] for a in range(3)])):
            out_ref[4 * j + l, 0] = v.astype(BF)


def turned(in_ref, first, pixels):
    rows = pixels * T
    to, at = iota((rows, rows), 0), iota((rows, rows), 1)
    frame = 2 * (to % P2) + (to // P2) % 2
    turn = (at == frame * pixels + to // T).astype(BF)
    values = in_ref[:, pl.ds(first, pixels), :].reshape(rows, C)
    return dot(turn, values).reshape(pixels, 2, P2, C)


def activate(values, norm):
    u = (values - norm[0][None]) * norm[1][None]
    return (u / (1.0 + jnp.exp(-u))).astype(BF).astype(F32)


def time_terms(act):
    pixels = act.shape[0]
    even, odd = act[:, 0], act[:, 1]
    start = iota((pixels * P2, C), 0) % P2 == 0

    def before(v):
        v = pltpu.roll(v.reshape(pixels * P2, C), 1, 0)
        return jnp.where(start, 0.0, v).reshape(pixels, P2, C)

    even1, odd1 = before(even), before(odd)
    return even1 - even, odd1 + even, even - odd1, odd1 - odd


def conv_kernel(place_ref, in_ref, w_ref, mid_ref, stats_ref, terms, sides, latent, sums, norm, held, sems):
    def fetch(j, l):
        slot = 4 * (j % 3) + l
        return pltpu.make_async_copy(w_ref.at[4 * j + l], held.at[slot], sems.at[slot])

    for j in range(3):
        for l in range(4):
            fetch(j, l).start()

    block, z = place_ref[0], place_ref[1]
    half, column = block % 2, block // 2
    above = (half == 0) & (z == 0)
    below = (half == 1) & (z == 3)
    tail = in_ref[:, 96:MSG, :].reshape(T * 8, C)
    row = iota((T, T * 8), 0)
    row = 2 * (row % P2) + row // P2
    pieces = dot((iota((T, T * 8), 1) == row * 8 + 4).astype(BF), tail).astype(BF)
    for i in range(2):
        norm[i] = sum(
            dot(pieces[:, 128 * k : 128 * k + 128], from_groups(32 * i, BF)) for k in range(3)
        ).reshape(2, P2, C)

    for first, pixels in ((80, 16), (96, 8)):
        act = activate(turned(in_ref, first, pixels), norm)
        p = iota(act.shape, 0) + first
        out = (column == 0) & (p < 90) | (column == 15) & (p >= 90)
        out = out | above & ((p == 80) | (p == 90)) | below & ((p == 89) | (p == 99))
        for j, v in enumerate(time_terms(jnp.where(out, 0.0, act))):
            for q in range(pixels):
                if first + q < 100:
                    sides[j, (first + q - 80) // W, (first + q) % W] = v[q]

    def two_rows(k, _):
        first = pl.multiple_of(16 * k, 16)
        values = turned(in_ref, first, 16)
        latent[pl.ds(first, 16)] = values.astype(BF)
        act = activate(values, norm)
        r = iota(act.shape, 0) // S + 2 * k
        act = jnp.where(above & (r == 0) | below & (r == W - 1), 0.0, act)
        at = pl.ds(2 * k, 2)
        for j, v in enumerate(time_terms(act)):
            left, right = sides[j, 0, at][:, None], sides[j, 1, at][:, None]
            v = jnp.concatenate([left, v.reshape(2, S, P2, C), right], axis=1).reshape(2, W // 2, 2, P2, C)
            even, odd = v[:, :, 0], v[:, :, 1]
            before, after, odd_before = even[:, :-1], even[:, 1:], odd[:, :-1]
            for l, u in enumerate((before - after, odd_before + after, after - odd_before, odd_before - odd[:, 1:])):
                terms[j, l, at] = u.astype(BF)
        return 0

    lax.fori_loop(0, W // 2, two_rows, 0)

    def term(j, _):
        @pl.when(j == 1)
        def _():
            for l in range(4):
                fetch(j + 2, l).start()

        for l in range(4):
            fetch(j, l).wait()
        for q in range(2):
            m = []
            for l in range(4):
                rows = [terms[j, l, 4 * q + b : 4 * q + b + 4].reshape(16 * P2, C) for b in range(3)]
                weight = held[4 * (j % 3) + l].reshape(3 * C, C)
                m.append(dot(jnp.concatenate(rows, axis=1), weight).reshape(4, 4, P2, C))
            sums[j, 0, 4 * q : 4 * q + 4] = m[0] + m[1] + m[2]
            sums[j, 1, 4 * q : 4 * q + 4] = m[1] - m[2] - m[3]
        return 0

    lax.fori_loop(0, 4, term, 0)

    def finish_row(r, total):
        for c in range(S):
            m = [sums[j, c % 2, r, c // 2] for j in range(4)]
            for i, v in enumerate((m[0] + m[1] + m[2], m[1] - m[2] - m[3])):
                v = (latent[S * r + S + c, i].astype(F32) + v).astype(BF)
                mid_ref[S * r + c, i] = v
                total[i] = total[i] + v.astype(F32)
        return total

    zero = jnp.zeros((P2, C), F32)
    total = lax.fori_loop(0, S, finish_row, [zero, zero])
    mean = [v * (1.0 / (S * S)) for v in total]

    def squares(r, total):
        for c in range(S):
            for i in range(2):
                off = mid_ref[S * r + c, i].astype(F32) - mean[i]
                total[i] = total[i] + off * off
        return total

    total = lax.fori_loop(0, S, squares, [zero, zero])
    stats = sum(group_stats(mean[i], total[i], float(S * S), 64 * i) for i in range(2))
    stats_ref[...] = jnp.broadcast_to(stats[None], stats_ref.shape)


def merge_kernel(parts_ref, out_ref):
    whole = merge(parts_ref[...], float(S * S * 16))
    out_ref[...] = jnp.broadcast_to(whole[None], out_ref.shape)


def attend_kernel(mid_ref, parts_ref, score_ref, update_ref, out_ref, norm):
    @pl.when(pl.program_id(0) == 0)
    def _():
        count = float(S * S * 16 * 8)
        whole = finish(merge(parts_ref[...], count), 16.0 * count)
        for i in range(2):
            for j in range(2):
                norm[i, j] = dot(whole, from_groups(64 * j + 32 * i), HI)

    pixels = mid_ref.shape[0]
    rows = pixels * T
    mid = mid_ref[...].astype(F32)
    flat = ((mid - norm[0][None]) * norm[1][None]).astype(BF).reshape(rows, C)
    query = dot(flat, score_ref[...]).astype(BF)
    n = 256
    row, column = iota((n, n), 0), iota((n, n), 1)
    frame = lambda v: 2 * (v % P2) + (v // P2) % 2
    seen = (row // T == column // T) & (frame(row) >= frame(column))
    parts = []
    for i in range(rows // n):
        at = slice(i * n, i * n + n)
        scores = lax.dot_general(query[at], flat[at], (((1,), (1,)), ((), ())), preferred_element_type=F32)
        scores = jnp.where(seen, scores, -1e30)
        weights = jnp.exp(scores - jnp.max(scores, axis=1, keepdims=True))
        weights = (weights / jnp.sum(weights, axis=1, keepdims=True)).astype(BF)
        parts.append(dot(weights, flat[at]).astype(BF))
    update = dot(jnp.concatenate(parts, axis=0), update_ref[...])
    out = (mid.reshape(rows, C) + update).astype(BF)
    to = iota((n, n), 0)
    frame = to // S
    turn = (iota((n, n), 1) == (to % S) * T + (frame % 2) * P2 + frame // 2).astype(BF)
    for i in range(rows // (2 * n)):
        pair = [dot(turn, out[(2 * i + k) * n : (2 * i + k + 1) * n]).reshape(T, S, C) for k in range(2)]
        out_ref[:, 16 * i : 16 * i + 16, :] = jnp.concatenate(pair, axis=1).astype(BF)


def local(latents, conv_weight, w_query, w_key, w_value, w_out):
    x = latents.reshape(16, 128, C)
    vmem = pl.BlockSpec(memory_space=pltpu.VMEM)
    smem = pl.BlockSpec(memory_space=pltpu.SMEM)
    whole = lambda *shape: pl.BlockSpec(shape, lambda i: (0,) * len(shape))
    exchange = lambda v, axes: lax.all_to_all(v[None], axes, split_axis=1, concat_axis=0, tiled=True)[:, 0]
    place = jnp.stack([lax.axis_index(TM), lax.axis_index("rows")]).astype(jnp.int32)

    row = jax.ShapeDtypeStruct((144, C), BF)
    up, down, own = pl.pallas_call(
        latent_stats_kernel,
        out_shape=(row, row, jax.ShapeDtypeStruct((16, C), BF)),
        in_specs=[vmem],
        out_specs=(vmem,) * 3,
        compiler_params=params(),
        cost_estimate=cost(2048 * C * 4, 2048 * C * 2),
        name="latent_stats",
    )(x.reshape(2048, C))
    around = lambda v, by: lax.ppermute(v, "rows", [(i, (i + by) % 4) for i in range(4)])
    up, down, far = around(up, 1), around(down, 3), around(own, 2)
    messages = pl.pallas_call(
        message_kernel,
        grid=(4,),
        out_shape=jax.ShapeDtypeStruct((32, MSG, C), BF),
        in_specs=[whole(16, 128, C), whole(144, C), whole(144, C), whole(16, C), whole(16, C)],
        out_specs=pl.BlockSpec((8, MSG, C), lambda i: (i, 0, 0)),
        scratch_shapes=[pltpu.VMEM((4, 18, 128, 128), F32), pltpu.VMEM((4, 2, 16 * 24, 128), F32)],
        compiler_params=params(),
        cost_estimate=cost(2**22, 6 * 2**20),
        name="messages",
    )(x, up, down, own, far)
    patch = exchange(messages, TM)
    weights = pl.pallas_call(
        weights_kernel,
        grid=(3, 4),
        out_shape=jax.ShapeDtypeStruct((16, 3, C, C), BF),
        in_specs=[pl.BlockSpec((3, 1, 3, 128, C), lambda b, i: (0, b, 0, i, 0))],
        out_specs=pl.BlockSpec((16, 1, 128, C), lambda b, i: (0, b, i, 0)),
        compiler_params=params(),
        cost_estimate=cost(9 * 8 * C * C, 75 * C * C * 2),
        name="weights",
    )(conv_weight)
    score = dot(w_query, w_key.T) * (1.0 / C**0.5)
    score, update = score.astype(BF), dot(w_value, w_out).astype(BF)

    mid, stats = pl.pallas_call(
        conv_kernel,
        out_shape=(jax.ShapeDtypeStruct((S * S, 2, P2, C), BF), jax.ShapeDtypeStruct((8, P2, 128), F32)),
        in_specs=[smem, vmem, pl.BlockSpec(memory_space=pl.ANY)],
        out_specs=(vmem, vmem),
        scratch_shapes=[
            pltpu.VMEM((4, 4, W, S // 2, P2, C), BF),
            pltpu.VMEM((4, 2, W, P2, C), F32),
            pltpu.VMEM((W * S, 2, P2, C), BF),
            pltpu.VMEM((4, 2, S, S // 2, P2, C), F32),
            pltpu.VMEM((2, 2, P2, C), F32),
            pltpu.VMEM((12, 3, C, C), BF),
            pltpu.SemaphoreType.DMA((12,)),
        ],
        compiler_params=params(),
        cost_estimate=cost(512 * 48 * C * C * 2, 28 * 2**20),
        name="conv",
    )(place, patch, weights)
    parts = pl.pallas_call(
        merge_kernel,
        out_shape=jax.ShapeDtypeStruct((16, P2, 128), F32),
        in_specs=[vmem],
        out_specs=vmem,
        compiler_params=params(),
        name="merge",
    )(exchange(stats, ("core", "rows")))
    parts = exchange(parts, ("x", "y"))
    pixels = 32
    out = pl.pallas_call(
        attend_kernel,
        grid=(S * S // pixels,),
        out_shape=jax.ShapeDtypeStruct((T, S * S, C), BF),
        in_specs=[pl.BlockSpec((pixels, 2, P2, C), lambda i: (i, 0, 0, 0)), whole(16, P2, 128)] + [whole(C, C)] * 2,
        out_specs=pl.BlockSpec((T, pixels, C), lambda i: (0, i, 0)),
        scratch_shapes=[pltpu.VMEM((2, 2, P2, C), F32)],
        compiler_params=params(),
        cost_estimate=cost(2048 * C * C * 2 * 4, 8 * 2**20),
        name="attend",
    )(mid, parts, score, update)
    back = exchange(out, TM)
    back = back.reshape(16, 2, S, S, C).transpose(1, 2, 0, 3, 4)
    return back.reshape(1, 16, 128, C)


def solution(mesh):
    mesh = Mesh(mesh.devices.reshape(4, 4, 2, 4), TM + ("rows",))
    in_specs = (P(TM, "rows", None, None), P(), P(), P(), P(), P())
    out_specs = P(TM, "rows", None, None)
    return jax.shard_map(local, mesh=mesh, in_specs=in_specs, out_specs=out_specs, check_vma=False)
```

```python
import jax
import jax.numpy as jnp
from jax import lax
from jax.experimental import pallas as pl
from jax.experimental.pallas import tpu as pltpu
from jax.sharding import Mesh
from jax.sharding import PartitionSpec as P

GROUPS = 32
T = 32
C = 512
S = 8
W = S + 2
P2 = T // 2
RIM = 40
TM = ("x", "y", "core")
EPS = 1e-6
BF, F32 = jnp.bfloat16, jnp.float32
HI = lax.Precision.HIGHEST


def iota(shape, dim):
    return lax.broadcasted_iota(jnp.int32, shape, dim)


def dot(a, b, precision=None):
    return jnp.dot(a, b, preferred_element_type=F32, precision=precision)


def params():
    return pltpu.CompilerParams(vmem_limit_bytes=56 * 2**20)


def cost(flops, nbytes):
    return pl.CostEstimate(flops=flops, bytes_accessed=nbytes, transcendentals=0)


def to_groups(lane):
    return (iota((C, 128), 0) // 16 + lane == iota((C, 128), 1)).astype(F32)


def from_groups(lane, dtype=F32):
    return (iota((128, C), 1) // 16 + lane == iota((128, C), 0)).astype(dtype)


def group_stats(mean, m2, count, lane):
    group_mean = dot(mean, to_groups(lane), HI) * (1.0 / 16.0)
    off = mean - dot(group_mean, from_groups(lane), HI)
    return group_mean + dot(m2 + count * (off * off), to_groups(lane + 32), HI)


def merge(parts, count):
    n = parts.shape[0]
    total = jnp.sum(parts, axis=0)
    mean = total * (1.0 / n)
    off = parts - mean[None]
    between = pltpu.roll(jnp.sum(off * off, axis=0), 32, 1)
    is_mean = (iota(total.shape, 1) // 32) % 2 == 0
    return jnp.where(is_mean, mean, total + count * between)


def split_terms(v):
    high = v.astype(BF).astype(F32)
    middle = (v - high).astype(BF).astype(F32)
    return jnp.concatenate([high, middle, v - high - middle, jnp.zeros_like(v)], axis=1)


def join_terms(v):
    return sum(v[:, 128 * i : 128 * i + 128].astype(F32) for i in range(3))


def latent_stats_kernel(x_ref, up_ref, down_ref, out_ref):
    n = x_ref.shape[0]
    step = 256

    def add(i, total):
        rows = x_ref[pl.ds(pl.multiple_of(i * step, step), step), :].astype(F32)
        return total + jnp.sum(rows.reshape(step // 8, 8, C), axis=0)

    total = lax.fori_loop(0, n // step, add, jnp.zeros((8, C), F32))
    mean = jnp.sum(total, axis=0, keepdims=True) * (1.0 / n)

    def add_square(i, total):
        rows = x_ref[pl.ds(pl.multiple_of(i * step, step), step), :].astype(F32) - mean
        return total + jnp.sum((rows * rows).reshape(step // 8, 8, C), axis=0)

    total = lax.fori_loop(0, n // step, add_square, jnp.zeros((8, C), F32))
    m2 = jnp.sum(total, axis=0, keepdims=True)
    wide = lambda v: jnp.broadcast_to(v, (8, C))
    row = split_terms(group_stats(wide(mean), wide(m2), float(n), 0))
    row = jnp.concatenate([row, jnp.zeros_like(row)], axis=0).astype(BF)
    out_ref[...] = row
    up_ref[:128, :] = x_ref[n - 128 :, :]
    down_ref[:128, :] = x_ref[:128, :]
    up_ref[128:, :] = row
    down_ref[128:, :] = row


def finish(whole, count):
    is_mean = (iota(whole.shape, 1) // 32) % 2 == 0
    return jnp.where(is_mean, whole, lax.rsqrt(whole * (1.0 / count) + EPS))


def inner_kernel(x_ref, out_ref):
    x = x_ref[...].astype(F32).reshape(2, S, 4, S, C)
    for k in range(4):
        for half in range(2):
            out_ref[2 * k + half] = x[half, :, k].reshape(S * S, C).astype(BF)


def rim_kernel(x_ref, up_ref, down_ref, own_ref, far_ref, out_ref):
    pair = pl.program_id(0)
    n = 2048.0 * 16.0
    parts = [own_ref[...], far_ref[...], up_ref[128:, :], down_ref[128:, :]]
    whole = merge(jnp.stack([join_terms(v)[:8] for v in parts]), n)
    stats = split_terms(jnp.where(iota(whole.shape, 1) < 64, finish(whole, 4.0 * n), 0.0))[:1]
    for odd in range(2):
        start = 16 * pair if odd else 16 * pair - 16
        start = jnp.clip(start, 0, 96)
        first = 16 * pair + 8 * odd - 1 - start
        start = pl.multiple_of(start, 16)
        p, source = iota((RIM, W * 32), 0), iota((RIM, W * 32), 1)
        r = jnp.where(p < 10, 0, jnp.where(p < 20, 9, jnp.where(p < 28, p - 19, p - 27)))
        c = jnp.where(p < 10, p, jnp.where(p < 20, p - 10, jnp.where(p < 28, 0, 9)))
        column = first + c
        pick = (source == r * 32 + column) & (column >= 0) & (column < 32) & (p < 36)
        pick = pick.astype(BF)
        for half in range(2):
            cols = pl.ds(start, 32)
            if half == 0:
                block = jnp.concatenate([up_ref[cols, :][None], x_ref[0:9, cols, :]], axis=0)
            else:
                block = jnp.concatenate([x_ref[7:16, cols, :], down_ref[cols, :][None]], axis=0)
            message = dot(pick, block.reshape(W * 32, C))
            out_ref[2 * odd + half] = jnp.where(iota((RIM, C), 0) == 36, stats, message).astype(BF)


def weights_kernel(w_ref, out_ref):
    def products(g):
        ends = (g[0] + g[2]) * 0.5
        middle = g[1] * 0.5
        return g[0], ends + middle, ends - middle, g[2]

    w = [[w_ref[a, 0, e].astype(F32) for e in range(3)] for a in range(3)]
    columns = [products(w[a]) for a in range(3)]
    for l in range(4):
        for j, v in enumerate(products([columns[a][l] for a in range(3)])):
            out_ref[4 * j + l, 0] = v.astype(BF)


def turned(in_ref, first, pixels):
    rows = pixels * T
    to, at = iota((rows, rows), 0), iota((rows, rows), 1)
    frame = 2 * (to % P2) + (to // P2) % 2
    turn = (at == frame * pixels + to // T).astype(BF)
    values = in_ref[:, pl.ds(first, pixels), :].reshape(rows, C)
    return dot(turn, values).reshape(pixels, 2, P2, C)


def activate(values, norm):
    u = (values - norm[0][None]) * norm[1][None]
    return (u / (1.0 + jnp.exp(-u))).astype(BF).astype(F32)


def time_terms(act):
    pixels = act.shape[0]
    even, odd = act[:, 0], act[:, 1]
    start = iota((pixels * P2, C), 0) % P2 == 0

    def before(v):
        v = pltpu.roll(v.reshape(pixels * P2, C), 1, 0)
        return jnp.where(start, 0.0, v).reshape(pixels, P2, C)

    even1, odd1 = before(even), before(odd)
    return even1 - even, odd1 + even, even - odd1, odd1 - odd


def conv_kernel(place_ref, in_ref, rim_ref, w_ref, mid_ref, stats_ref, terms, ends, sides, latent, sums, norm, held, sems):
    def fetch(j, l):
        slot = 4 * (j % 3) + l
        return pltpu.make_async_copy(w_ref.at[4 * j + l], held.at[slot], sems.at[slot])

    for j in range(3):
        for l in range(4):
            fetch(j, l).start()

    block, z = place_ref[0], place_ref[1]
    half, column = block % 2, block // 2
    above = (half == 0) & (z == 0)
    below = (half == 1) & (z == 3)
    tail = rim_ref[:, 32:RIM, :].reshape(T * 8, C)
    row = iota((T, T * 8), 0)
    row = 2 * (row % P2) + row // P2
    pieces = dot((iota((T, T * 8), 1) == row * 8 + 4).astype(BF), tail).astype(BF)
    for i in range(2):
        norm[i] = sum(
            dot(pieces[:, 128 * k : 128 * k + 128], from_groups(32 * i, BF)) for k in range(3)
        ).reshape(2, P2, C)

    for first, pixels in ((0, 16), (16, 16), (32, 8)):
        act = activate(turned(rim_ref, first, pixels), norm)
        p = iota(act.shape, 0) + first
        out = above & (p < 10) | below & (p >= 10) & (p < 20)
        out = out | (column == 0) & ((p == 0) | (p == 10) | (p >= 20) & (p < 28))
        out = out | (column == 15) & ((p == 9) | (p == 19) | (p >= 28))
        for j, v in enumerate(time_terms(jnp.where(out, 0.0, act))):
            for q in range(pixels):
                p = first + q
                if p < 20:
                    ends[j, p // 10, p % 10] = v[q]
                elif p < 36:
                    sides[j, (p - 20) // S, (p - 20) % S] = v[q]

    def columns(v, j, at):
        v = v.reshape(2, W // 2, 2, P2, C)
        even, odd = v[:, :, 0], v[:, :, 1]
        before, after, odd_before = even[:, :-1], even[:, 1:], odd[:, :-1]
        for l, u in enumerate((before - after, odd_before + after, after - odd_before, odd_before - odd[:, 1:])):
            u = u.astype(BF)
            for i, r in enumerate(at):
                terms[j, l, r] = u[i]

    for j in range(4):
        columns(ends[j], j, (0, W - 1))

    def two_rows(k, _):
        first = pl.multiple_of(16 * k, 16)
        values = turned(in_ref, first, 16)
        latent[pl.ds(first, 16)] = values.astype(BF)
        for j, v in enumerate(time_terms(activate(values, norm))):
            left, right = (sides[j, i, pl.ds(2 * k, 2)][:, None] for i in range(2))
            columns(jnp.concatenate([left, v.reshape(2, S, P2, C), right], axis=1), j, (2 * k + 1, 2 * k + 2))
        return 0

    lax.fori_loop(0, S // 2, two_rows, 0)

    def term(j, _):
        @pl.when(j == 1)
        def _():
            for l in range(4):
                fetch(j + 2, l).start()

        for l in range(4):
            fetch(j, l).wait()
        for q in range(2):
            m = []
            for l in range(4):
                rows = [terms[j, l, 4 * q + b : 4 * q + b + 4].reshape(16 * P2, C) for b in range(3)]
                weight = held[4 * (j % 3) + l].reshape(3 * C, C)
                m.append(dot(jnp.concatenate(rows, axis=1), weight).reshape(4, 4, P2, C))
            sums[j, 0, 4 * q : 4 * q + 4] = m[0] + m[1] + m[2]
            sums[j, 1, 4 * q : 4 * q + 4] = m[1] - m[2] - m[3]
        return 0

    lax.fori_loop(0, 4, term, 0)

    def finish_row(r, total):
        for c in range(S):
            m = [sums[j, c % 2, r, c // 2] for j in range(4)]
            for i, v in enumerate((m[0] + m[1] + m[2], m[1] - m[2] - m[3])):
                v = (latent[S * r + c, i].astype(F32) + v).astype(BF)
                mid_ref[S * r + c, i] = v
                total[i] = total[i] + v.astype(F32)
        return total

    zero = jnp.zeros((P2, C), F32)
    total = lax.fori_loop(0, S, finish_row, [zero, zero])
    mean = [v * (1.0 / (S * S)) for v in total]

    def squares(r, total):
        for c in range(S):
            for i in range(2):
                off = mid_ref[S * r + c, i].astype(F32) - mean[i]
                total[i] = total[i] + off * off
        return total

    total = lax.fori_loop(0, S, squares, [zero, zero])
    stats = sum(group_stats(mean[i], total[i], float(S * S), 64 * i) for i in range(2))
    stats_ref[...] = jnp.broadcast_to(stats[None], stats_ref.shape)


def merge_kernel(parts_ref, out_ref):
    whole = merge(parts_ref[...], float(S * S * 16))
    out_ref[...] = jnp.broadcast_to(whole[None], out_ref.shape)


def attend_kernel(mid_ref, parts_ref, score_ref, update_ref, out_ref, norm):
    @pl.when(pl.program_id(0) == 0)
    def _():
        count = float(S * S * 16 * 8)
        whole = finish(merge(parts_ref[...], count), 16.0 * count)
        for i in range(2):
            for j in range(2):
                norm[i, j] = dot(whole, from_groups(64 * j + 32 * i), HI)

    pixels = mid_ref.shape[0]
    rows = pixels * T
    mid = mid_ref[...].astype(F32)
    flat = ((mid - norm[0][None]) * norm[1][None]).astype(BF).reshape(rows, C)
    query = dot(flat, score_ref[...]).astype(BF)
    n = 256
    row, column = iota((n, n), 0), iota((n, n), 1)
    frame = lambda v: 2 * (v % P2) + (v // P2) % 2
    seen = (row // T == column // T) & (frame(row) >= frame(column))
    parts = []
    for i in range(rows // n):
        at = slice(i * n, i * n + n)
        scores = lax.dot_general(query[at], flat[at], (((1,), (1,)), ((), ())), preferred_element_type=F32)
        scores = jnp.where(seen, scores, -1e30)
        weights = jnp.exp(scores - jnp.max(scores, axis=1, keepdims=True))
        weights = (weights / jnp.sum(weights, axis=1, keepdims=True)).astype(BF)
        parts.append(dot(weights, flat[at]).astype(BF))
    update = dot(jnp.concatenate(parts, axis=0), update_ref[...])
    out = (mid.reshape(rows, C) + update).astype(BF)
    to = iota((n, n), 0)
    frame = to // S
    turn = (iota((n, n), 1) == (to % S) * T + (frame % 2) * P2 + frame // 2).astype(BF)
    for i in range(rows // (2 * n)):
        pair = [dot(turn, out[(2 * i + k) * n : (2 * i + k + 1) * n]).reshape(T, S, C) for k in range(2)]
        out_ref[:, 16 * i : 16 * i + 16, :] = jnp.concatenate(pair, axis=1).astype(BF)


def local(latents, conv_weight, w_query, w_key, w_value, w_out):
    x = latents.reshape(16, 128, C)
    vmem = pl.BlockSpec(memory_space=pltpu.VMEM)
    smem = pl.BlockSpec(memory_space=pltpu.SMEM)
    whole = lambda *shape: pl.BlockSpec(shape, lambda i: (0,) * len(shape))
    exchange = lambda v, axes: lax.all_to_all(v[None], axes, split_axis=1, concat_axis=0, tiled=True)[:, 0]
    place = jnp.stack([lax.axis_index(TM), lax.axis_index("rows")]).astype(jnp.int32)

    inner = pl.pallas_call(
        inner_kernel,
        grid=(4,),
        out_shape=jax.ShapeDtypeStruct((32, S * S, C), BF),
        in_specs=[pl.BlockSpec((16, 32, C), lambda i: (0, i, 0))],
        out_specs=pl.BlockSpec((8, S * S, C), lambda i: (i, 0, 0)),
        compiler_params=params(),
        cost_estimate=cost(2**20, 4 * 2**20),
        name="inner",
    )(x)
    patch = exchange(inner, TM)
    row = jax.ShapeDtypeStruct((144, C), BF)
    up, down, own = pl.pallas_call(
        latent_stats_kernel,
        out_shape=(row, row, jax.ShapeDtypeStruct((16, C), BF)),
        in_specs=[vmem],
        out_specs=(vmem,) * 3,
        compiler_params=params(),
        cost_estimate=cost(2048 * C * 4, 2048 * C * 2),
        name="latent_stats",
    )(x.reshape(2048, C))
    around = lambda v, by: lax.ppermute(v, "rows", [(i, (i + by) % 4) for i in range(4)])
    up, down, far = around(up, 1), around(down, 3), around(own, 2)
    rim = pl.pallas_call(
        rim_kernel,
        grid=(8,),
        out_shape=jax.ShapeDtypeStruct((32, RIM, C), BF),
        in_specs=[whole(16, 128, C), whole(144, C), whole(144, C), whole(16, C), whole(16, C)],
        out_specs=pl.BlockSpec((4, RIM, C), lambda i: (i, 0, 0)),
        compiler_params=params(),
        cost_estimate=cost(32 * RIM * 320 * C * 2, 4 * 2**20),
        name="rim",
    )(x, up, down, own, far)
    rim, patch, conv_weight = lax.optimization_barrier((rim, patch, conv_weight))
    rim = exchange(rim, TM)
    weights = pl.pallas_call(
        weights_kernel,
        grid=(3, 4),
        out_shape=jax.ShapeDtypeStruct((16, 3, C, C), BF),
        in_specs=[pl.BlockSpec((3, 1, 3, 128, C), lambda b, i: (0, b, 0, i, 0))],
        out_specs=pl.BlockSpec((16, 1, 128, C), lambda b, i: (0, b, i, 0)),
        compiler_params=params(),
        cost_estimate=cost(9 * 8 * C * C, 75 * C * C * 2),
        name="weights",
    )(conv_weight)
    score = dot(w_query, w_key.T) * (1.0 / C**0.5)
    score, update = score.astype(BF), dot(w_value, w_out).astype(BF)

    mid, stats = pl.pallas_call(
        conv_kernel,
        out_shape=(jax.ShapeDtypeStruct((S * S, 2, P2, C), BF), jax.ShapeDtypeStruct((8, P2, 128), F32)),
        in_specs=[smem, vmem, vmem, pl.BlockSpec(memory_space=pl.ANY)],
        out_specs=(vmem, vmem),
        scratch_shapes=[
            pltpu.VMEM((4, 4, W, S // 2, P2, C), BF),
            pltpu.VMEM((4, 2, W, P2, C), F32),
            pltpu.VMEM((4, 2, S, P2, C), F32),
            pltpu.VMEM((S * S, 2, P2, C), BF),
            pltpu.VMEM((4, 2, S, S // 2, P2, C), F32),
            pltpu.VMEM((2, 2, P2, C), F32),
            pltpu.VMEM((12, 3, C, C), BF),
            pltpu.SemaphoreType.DMA((12,)),
        ],
        compiler_params=params(),
        cost_estimate=cost(512 * 48 * C * C * 2, 28 * 2**20),
        name="conv",
    )(place, patch, rim, weights)
    parts = pl.pallas_call(
        merge_kernel,
        out_shape=jax.ShapeDtypeStruct((16, P2, 128), F32),
        in_specs=[vmem],
        out_specs=vmem,
        compiler_params=params(),
        name="merge",
    )(exchange(stats, ("core", "rows")))
    parts = exchange(parts, ("x", "y"))
    pixels = 32
    out = pl.pallas_call(
        attend_kernel,
        grid=(S * S // pixels,),
        out_shape=jax.ShapeDtypeStruct((T, S * S, C), BF),
        in_specs=[pl.BlockSpec((pixels, 2, P2, C), lambda i: (i, 0, 0, 0)), whole(16, P2, 128)] + [whole(C, C)] * 2,
        out_specs=pl.BlockSpec((T, pixels, C), lambda i: (0, i, 0)),
        scratch_shapes=[pltpu.VMEM((2, 2, P2, C), F32)],
        compiler_params=params(),
        cost_estimate=cost(2048 * C * C * 2 * 4, 8 * 2**20),
        name="attend",
    )(mid, parts, score, update)
    back = exchange(out, TM)
    back = back.reshape(16, 2, S, S, C).transpose(1, 2, 0, 3, 4)
    return back.reshape(1, 16, 128, C)


def solution(mesh):
    mesh = Mesh(mesh.devices.reshape(4, 4, 2, 4), TM + ("rows",))
    in_specs = (P(TM, "rows", None, None), P(), P(), P(), P(), P())
    out_specs = P(TM, "rows", None, None)
    return jax.shard_map(local, mesh=mesh, in_specs=in_specs, out_specs=out_specs, check_vma=False)
```

```python
import jax
import jax.numpy as jnp
from jax import lax
from jax.experimental import pallas as pl
from jax.experimental.pallas import tpu as pltpu
from jax.sharding import Mesh
from jax.sharding import PartitionSpec as P

GROUPS = 32
T = 32
C = 512
S = 8
W = S + 2
P2 = T // 2
RIM = 24
TM = ("x", "y", "core")
EPS = 1e-6
BF, F32 = jnp.bfloat16, jnp.float32
HI = lax.Precision.HIGHEST


def iota(shape, dim):
    return lax.broadcasted_iota(jnp.int32, shape, dim)


def dot(a, b, precision=None):
    return jnp.dot(a, b, preferred_element_type=F32, precision=precision)


def params():
    return pltpu.CompilerParams(vmem_limit_bytes=56 * 2**20)


def cost(flops, nbytes):
    return pl.CostEstimate(flops=flops, bytes_accessed=nbytes, transcendentals=0)


def to_groups(lane):
    return (iota((C, 128), 0) // 16 + lane == iota((C, 128), 1)).astype(F32)


def from_groups(lane, dtype=F32):
    return (iota((128, C), 1) // 16 + lane == iota((128, C), 0)).astype(dtype)


def group_stats(mean, m2, count, lane):
    group_mean = dot(mean, to_groups(lane), HI) * (1.0 / 16.0)
    off = mean - dot(group_mean, from_groups(lane), HI)
    return group_mean + dot(m2 + count * (off * off), to_groups(lane + 32), HI)


def merge(parts, count):
    n = parts.shape[0]
    total = jnp.sum(parts, axis=0)
    mean = total * (1.0 / n)
    off = parts - mean[None]
    between = pltpu.roll(jnp.sum(off * off, axis=0), 32, 1)
    is_mean = (iota(total.shape, 1) // 32) % 2 == 0
    return jnp.where(is_mean, mean, total + count * between)


def split_terms(v):
    high = v.astype(BF).astype(F32)
    middle = (v - high).astype(BF).astype(F32)
    return jnp.concatenate([high, middle, v - high - middle, jnp.zeros_like(v)], axis=1)


def join_terms(v):
    return sum(v[:, 128 * i : 128 * i + 128].astype(F32) for i in range(3))


def latent_stats_kernel(x_ref, up_ref, down_ref, out_ref):
    n = x_ref.shape[0]
    step = 256

    def add(i, total):
        rows = x_ref[pl.ds(pl.multiple_of(i * step, step), step), :].astype(F32)
        return total + jnp.sum(rows.reshape(step // 8, 8, C), axis=0)

    total = lax.fori_loop(0, n // step, add, jnp.zeros((8, C), F32))
    mean = jnp.sum(total, axis=0, keepdims=True) * (1.0 / n)

    def add_square(i, total):
        rows = x_ref[pl.ds(pl.multiple_of(i * step, step), step), :].astype(F32) - mean
        return total + jnp.sum((rows * rows).reshape(step // 8, 8, C), axis=0)

    total = lax.fori_loop(0, n // step, add_square, jnp.zeros((8, C), F32))
    m2 = jnp.sum(total, axis=0, keepdims=True)
    wide = lambda v: jnp.broadcast_to(v, (8, C))
    row = split_terms(group_stats(wide(mean), wide(m2), float(n), 0))
    row = jnp.concatenate([row, jnp.zeros_like(row)], axis=0).astype(BF)
    out_ref[...] = row
    up_ref[:128, :] = x_ref[n - 128 :, :]
    down_ref[:128, :] = x_ref[:128, :]
    up_ref[128:, :] = row
    down_ref[128:, :] = row


def finish(whole, count):
    is_mean = (iota(whole.shape, 1) // 32) % 2 == 0
    return jnp.where(is_mean, whole, lax.rsqrt(whole * (1.0 / count) + EPS))


def inner_kernel(x_ref, out_ref):
    x = x_ref[...].astype(F32).reshape(2, S, 4, S, C)
    for k in range(4):
        for half in range(2):
            out_ref[2 * k + half] = x[half, :, k].reshape(S * S, C).astype(BF)


def rim_kernel(x_ref, up_ref, down_ref, own_ref, far_ref, out_ref):
    pair = pl.program_id(0)
    n = 2048.0 * 16.0
    parts = [own_ref[...], far_ref[...], up_ref[128:, :], down_ref[128:, :]]
    whole = merge(jnp.stack([join_terms(v)[:8] for v in parts]), n)
    stats = split_terms(jnp.where(iota(whole.shape, 1) < 64, finish(whole, 4.0 * n), 0.0))[:1]
    for odd in range(2):
        start = 16 * pair if odd else 16 * pair - 16
        start = jnp.clip(start, 0, 96)
        first = 16 * pair + 8 * odd - 1 - start
        start = pl.multiple_of(start, 16)
        p, source = iota((RIM, W * 32), 0), iota((RIM, W * 32), 1)
        r = jnp.where(p < 16, p % S + 1, jnp.where(p < 18, 0, 9))
        c = jnp.where(p < 16, jnp.where(p < 8, 0, 9), jnp.where(p % 2 == 0, 0, 9))
        column = first + c
        pick = (source == r * 32 + column) & (column >= 0) & (column < 32) & (p < 20)
        pick = pick.astype(BF)
        for half in range(2):
            cols = pl.ds(start, 32)
            if half == 0:
                block = jnp.concatenate([up_ref[cols, :][None], x_ref[0:9, cols, :]], axis=0)
            else:
                block = jnp.concatenate([x_ref[7:16, cols, :], down_ref[cols, :][None]], axis=0)
            message = dot(pick, block.reshape(W * 32, C))
            out_ref[2 * odd + half] = jnp.where(iota((RIM, C), 0) == 20, stats, message).astype(BF)


def weights_kernel(w_ref, out_ref):
    def products(g):
        ends = (g[0] + g[2]) * 0.5
        middle = g[1] * 0.5
        return g[0], ends + middle, ends - middle, g[2]

    w = [[w_ref[a, 0, e].astype(F32) for e in range(3)] for a in range(3)]
    columns = [products(w[a]) for a in range(3)]
    for l in range(4):
        for j, v in enumerate(products([columns[a][l] for a in range(3)])):
            out_ref[4 * j + l] = v.astype(BF)


def products_kernel(wq_ref, wk_ref, wv_ref, wo_ref, score_ref, update_ref):
    score = lax.dot_general(wq_ref[...], wk_ref[...], (((1,), (1,)), ((), ())), preferred_element_type=F32)
    score_ref[...] = (score * (1.0 / C**0.5)).astype(BF)
    update_ref[...] = dot(wv_ref[...], wo_ref[...]).astype(BF)


def turned(in_ref, first, pixels):
    rows = pixels * T
    to, at = iota((rows, rows), 0), iota((rows, rows), 1)
    frame = 2 * (to % P2) + (to // P2) % 2
    turn = (at == frame * pixels + to // T).astype(BF)
    values = in_ref[:, pl.ds(first, pixels), :].reshape(rows, C)
    return dot(turn, values).reshape(pixels, 2, P2, C)


def activate(values, norm):
    u = (values - norm[0][None]) * norm[1][None]
    return (u / (1.0 + jnp.exp(-u))).astype(BF).astype(F32)


def time_terms(act):
    pixels = act.shape[0]
    even, odd = act[:, 0], act[:, 1]
    start = iota((pixels * P2, C), 0) % P2 == 0

    def before(v):
        v = pltpu.roll(v.reshape(pixels * P2, C), 1, 0)
        return jnp.where(start, 0.0, v).reshape(pixels, P2, C)

    even1, odd1 = before(even), before(odd)
    return even1 - even, odd1 + even, even - odd1, odd1 - odd


def conv_kernel(
    place_ref, in_ref, rim_ref, core_ref, band_ref, w0, w1, w2, mid_ref, stats_ref,
    terms, ends, sides, latent, sums, norm, held, sems,
):
    def fetch(j, l):
        slot = 4 * (j % 3) + l
        return [
            pltpu.make_async_copy(w.at[4 * j + l], held.at[slot, b], sems.at[slot, b])
            for b, w in enumerate((w0, w1, w2))
        ]

    def start(j):
        for l in range(4):
            for copy in fetch(j, l):
                copy.start()

    for j in range(3):
        start(j)

    block, z = place_ref[0], place_ref[1]
    half, column = block % 2, block // 2
    above = (half == 0) & (z == 0)
    below = (half == 1) & (z == 3)
    tail = rim_ref[:, 16:RIM, :].reshape(T * 8, C)
    row = iota((T, T * 8), 0)
    row = 2 * (row % P2) + row // P2
    pieces = dot((iota((T, T * 8), 1) == row * 8 + 4).astype(BF), tail).astype(BF)
    for i in range(2):
        norm[i] = sum(
            dot(pieces[:, 128 * k : 128 * k + 128], from_groups(32 * i, BF)) for k in range(3)
        ).reshape(2, P2, C)

    for first, pixels in ((0, 16), (16, 8)):
        act = activate(turned(rim_ref, first, pixels), norm)
        p = iota(act.shape, 0) + first
        out = (column == 0) & ((p < 8) | (p == 16) | (p == 18))
        out = out | (column == 15) & ((p >= 8) & (p < 16) | (p == 17) | (p == 19))
        out = out | above & ((p == 16) | (p == 17)) | below & (p >= 18)
        for j, v in enumerate(time_terms(jnp.where(out, 0.0, act))):
            for q in range(min(pixels, 20 - first)):
                p = first + q
                if p < 16:
                    sides[j, p // S, p % S] = v[q]
                else:
                    ends[j, (p - 16) // 2, (p % 2) * (W - 1)] = v[q]
    core, band = turned(core_ref, 0, S), turned(band_ref, 0, S)
    for i, values in enumerate((jnp.where(half == 0, band, core), jnp.where(half == 0, core, band))):
        act = jnp.where(below if i else above, 0.0, activate(values, norm))
        for j, v in enumerate(time_terms(act)):
            ends[j, i, 1 : S + 1] = v

    def columns(v, j, at):
        v = v.reshape(2, W // 2, 2, P2, C)
        even, odd = v[:, :, 0], v[:, :, 1]
        before, after, odd_before = even[:, :-1], even[:, 1:], odd[:, :-1]
        for l, u in enumerate((before - after, odd_before + after, after - odd_before, odd_before - odd[:, 1:])):
            u = u.astype(BF)
            for i, r in enumerate(at):
                terms[j, l, r] = u[i]

    for j in range(4):
        columns(ends[j], j, (0, W - 1))

    def two_rows(k, _):
        first = pl.multiple_of(16 * k, 16)
        values = turned(in_ref, first, 16)
        latent[pl.ds(first, 16)] = values.astype(BF)
        for j, v in enumerate(time_terms(activate(values, norm))):
            left, right = (sides[j, i, pl.ds(2 * k, 2)][:, None] for i in range(2))
            columns(jnp.concatenate([left, v.reshape(2, S, P2, C), right], axis=1), j, (2 * k + 1, 2 * k + 2))
        return 0

    lax.fori_loop(0, S // 2, two_rows, 0)

    def term(j, _):
        @pl.when(j == 1)
        def _():
            start(j + 2)

        for l in range(4):
            for copy in fetch(j, l):
                copy.wait()
        for q in range(2):
            m = []
            for l in range(4):
                rows = [terms[j, l, 4 * q + b : 4 * q + b + 4].reshape(16 * P2, C) for b in range(3)]
                weight = held[4 * (j % 3) + l].reshape(3 * C, C)
                m.append(dot(jnp.concatenate(rows, axis=1), weight).reshape(4, 4, P2, C))
            sums[j, 0, 4 * q : 4 * q + 4] = m[0] + m[1] + m[2]
            sums[j, 1, 4 * q : 4 * q + 4] = m[1] - m[2] - m[3]
        return 0

    lax.fori_loop(0, 4, term, 0)

    def finish_row(r, total):
        for c in range(S):
            m = [sums[j, c % 2, r, c // 2] for j in range(4)]
            for i, v in enumerate((m[0] + m[1] + m[2], m[1] - m[2] - m[3])):
                v = (latent[S * r + c, i].astype(F32) + v).astype(BF)
                mid_ref[S * r + c, i] = v
                total[i] = total[i] + v.astype(F32)
        return total

    zero = jnp.zeros((P2, C), F32)
    total = lax.fori_loop(0, S, finish_row, [zero, zero])
    mean = [v * (1.0 / (S * S)) for v in total]

    def squares(r, total):
        for c in range(S):
            for i in range(2):
                off = mid_ref[S * r + c, i].astype(F32) - mean[i]
                total[i] = total[i] + off * off
        return total

    total = lax.fori_loop(0, S, squares, [zero, zero])
    stats = sum(group_stats(mean[i], total[i], float(S * S), 64 * i) for i in range(2))
    stats_ref[...] = jnp.broadcast_to(stats[None], stats_ref.shape)


def merge_kernel(parts_ref, out_ref):
    whole = merge(parts_ref[...], float(S * S * 16))
    out_ref[...] = jnp.broadcast_to(whole[None], out_ref.shape)


def attend_kernel(mid_ref, parts_ref, score_ref, update_ref, out_ref, norm):
    @pl.when(pl.program_id(0) == 0)
    def _():
        count = float(S * S * 16 * 8)
        whole = finish(merge(parts_ref[...], count), 16.0 * count)
        for i in range(2):
            for j in range(2):
                norm[i, j] = dot(whole, from_groups(64 * j + 32 * i), HI)

    pixels = mid_ref.shape[0]
    rows = pixels * T
    mid = mid_ref[...].astype(F32)
    flat = ((mid - norm[0][None]) * norm[1][None]).astype(BF).reshape(rows, C)
    query = dot(flat, score_ref[...]).astype(BF)
    n = 256
    row, column = iota((n, n), 0), iota((n, n), 1)
    frame = lambda v: 2 * (v % P2) + (v // P2) % 2
    seen = (row // T == column // T) & (frame(row) >= frame(column))
    parts = []
    for i in range(rows // n):
        at = slice(i * n, i * n + n)
        scores = lax.dot_general(query[at], flat[at], (((1,), (1,)), ((), ())), preferred_element_type=F32)
        scores = jnp.where(seen, scores, -1e30)
        weights = jnp.exp(scores - jnp.max(scores, axis=1, keepdims=True))
        weights = (weights / jnp.sum(weights, axis=1, keepdims=True)).astype(BF)
        parts.append(dot(weights, flat[at]).astype(BF))
    update = dot(jnp.concatenate(parts, axis=0), update_ref[...])
    out = (mid.reshape(rows, C) + update).astype(BF)
    to = iota((n, n), 0)
    frame = to // S
    turn = (iota((n, n), 1) == (to % S) * T + (frame % 2) * P2 + frame // 2).astype(BF)
    for i in range(rows // (2 * n)):
        pair = [dot(turn, out[(2 * i + k) * n : (2 * i + k + 1) * n]).reshape(T, S, C) for k in range(2)]
        out_ref[:, 16 * i : 16 * i + 16, :] = jnp.concatenate(pair, axis=1).astype(BF)


def local(latents, conv_weight, w_query, w_key, w_value, w_out):
    x = latents.reshape(16, 128, C)
    vmem = pl.BlockSpec(memory_space=pltpu.VMEM)
    smem = pl.BlockSpec(memory_space=pltpu.SMEM)
    whole = lambda *shape: pl.BlockSpec(shape, lambda i: (0,) * len(shape))
    exchange = lambda v, axes: lax.all_to_all(v[None], axes, split_axis=1, concat_axis=0, tiled=True)[:, 0]
    place = jnp.stack([lax.axis_index(TM), lax.axis_index("rows")]).astype(jnp.int32)

    inner = pl.pallas_call(
        inner_kernel,
        grid=(4,),
        out_shape=jax.ShapeDtypeStruct((32, S * S, C), BF),
        in_specs=[pl.BlockSpec((16, 32, C), lambda i: (0, i, 0))],
        out_specs=pl.BlockSpec((8, S * S, C), lambda i: (i, 0, 0)),
        compiler_params=params(),
        cost_estimate=cost(2**20, 4 * 2**20),
        name="inner",
    )(x)
    patch = exchange(inner, TM)
    row = jax.ShapeDtypeStruct((144, C), BF)
    up, down, own = pl.pallas_call(
        latent_stats_kernel,
        out_shape=(row, row, jax.ShapeDtypeStruct((16, C), BF)),
        in_specs=[vmem],
        out_specs=(vmem,) * 3,
        compiler_params=params(),
        cost_estimate=cost(2048 * C * 4, 2048 * C * 2),
        name="latent_stats",
    )(x.reshape(2048, C))
    own, *products = lax.optimization_barrier((own, w_query, w_key, w_value, w_out))
    score, update = pl.pallas_call(
        products_kernel,
        out_shape=(jax.ShapeDtypeStruct((C, C), BF),) * 2,
        in_specs=[vmem] * 4,
        out_specs=(vmem,) * 2,
        compiler_params=params(),
        cost_estimate=cost(2 * 2 * C**3, 6 * C * C * 2),
        name="products",
    )(*products)
    around = lambda v, by: lax.ppermute(v, "rows", [(i, (i + by) % 4) for i in range(4)])
    up, down, far = around(up, 1), around(down, 3), around(own, 2)
    rim = pl.pallas_call(
        rim_kernel,
        grid=(8,),
        out_shape=jax.ShapeDtypeStruct((32, RIM, C), BF),
        in_specs=[whole(16, 128, C), whole(144, C), whole(144, C), whole(16, C), whole(16, C)],
        out_specs=pl.BlockSpec((4, RIM, C), lambda i: (i, 0, 0)),
        compiler_params=params(),
        cost_estimate=cost(32 * RIM * 320 * C * 2, 4 * 2**20),
        name="rim",
    )(x, up, down, own, far)
    def combine(b, conv_weight):
        return pl.pallas_call(
            weights_kernel,
            grid=(4,),
            out_shape=jax.ShapeDtypeStruct((16, C, C), BF),
            in_specs=[pl.BlockSpec((3, 1, 3, 128, C), lambda i: (0, b, 0, i, 0))],
            out_specs=pl.BlockSpec((16, 128, C), lambda i: (0, i, 0)),
            compiler_params=params(),
            cost_estimate=cost(3 * 8 * C * C, 25 * C * C * 2),
            name="weights",
        )(conv_weight)

    rim, early = lax.optimization_barrier((rim, conv_weight))
    weights = [combine(0, early)]
    rim, patch = lax.optimization_barrier((rim, patch))
    rim = exchange(rim, TM)
    first = lax.axis_index("core") == 0
    row = lambda at: lax.dynamic_slice_in_dim(patch, at, S, axis=1)
    core, band = row(jnp.where(first, S * S - S, 0)), row(jnp.where(first, 0, S * S - S))
    core = lax.ppermute(core, "core", [(0, 1), (1, 0)])
    pairs = [(4 + i, i + 1) for i in range(3)] + [(i + 1, 4 + i) for i in range(3)]
    band = lax.ppermute(band, ("core", "rows"), pairs)
    core, band, late = lax.optimization_barrier((core, band, conv_weight))
    weights += [combine(b, late) for b in (1, 2)]

    mid, stats = pl.pallas_call(
        conv_kernel,
        out_shape=(jax.ShapeDtypeStruct((S * S, 2, P2, C), BF), jax.ShapeDtypeStruct((8, P2, 128), F32)),
        in_specs=[smem] + [vmem] * 4 + [pl.BlockSpec(memory_space=pl.ANY)] * 3,
        out_specs=(vmem, vmem),
        scratch_shapes=[
            pltpu.VMEM((4, 4, W, S // 2, P2, C), BF),
            pltpu.VMEM((4, 2, W, P2, C), F32),
            pltpu.VMEM((4, 2, S, P2, C), F32),
            pltpu.VMEM((S * S, 2, P2, C), BF),
            pltpu.VMEM((4, 2, S, S // 2, P2, C), F32),
            pltpu.VMEM((2, 2, P2, C), F32),
            pltpu.VMEM((12, 3, C, C), BF),
            pltpu.SemaphoreType.DMA((12, 3)),
        ],
        compiler_params=params(),
        cost_estimate=cost(512 * 48 * C * C * 2, 28 * 2**20),
        name="conv",
    )(place, patch, rim, core, band, *weights)
    parts = pl.pallas_call(
        merge_kernel,
        out_shape=jax.ShapeDtypeStruct((16, P2, 128), F32),
        in_specs=[vmem],
        out_specs=vmem,
        compiler_params=params(),
        name="merge",
    )(exchange(stats, ("core", "rows")))
    parts = exchange(parts, ("x", "y"))
    pixels = 32
    out = pl.pallas_call(
        attend_kernel,
        grid=(S * S // pixels,),
        out_shape=jax.ShapeDtypeStruct((T, S * S, C), BF),
        in_specs=[pl.BlockSpec((pixels, 2, P2, C), lambda i: (i, 0, 0, 0)), whole(16, P2, 128)] + [whole(C, C)] * 2,
        out_specs=pl.BlockSpec((T, pixels, C), lambda i: (0, i, 0)),
        scratch_shapes=[pltpu.VMEM((2, 2, P2, C), F32)],
        compiler_params=params(),
        cost_estimate=cost(2048 * C * C * 2 * 4, 8 * 2**20),
        name="attend",
    )(mid, parts, score, update)
    back = exchange(out, TM)
    back = back.reshape(16, 2, S, S, C).transpose(1, 2, 0, 3, 4)
    return back.reshape(1, 16, 128, C)


def solution(mesh):
    mesh = Mesh(mesh.devices.reshape(4, 4, 2, 4), TM + ("rows",))
    in_specs = (P(TM, "rows", None, None), P(), P(), P(), P(), P())
    out_specs = P(TM, "rows", None, None)
    return jax.shard_map(local, mesh=mesh, in_specs=in_specs, out_specs=out_specs, check_vma=False)
```

```python
import jax
import jax.numpy as jnp
from jax import lax
from jax.experimental import pallas as pl
from jax.experimental.pallas import tpu as pltpu
from jax.sharding import Mesh
from jax.sharding import PartitionSpec as P

GROUPS = 32
T = 32
C = 512
S = 8
W = S + 2
P2 = T // 2
RIM = 24
TM = ("x", "y", "core")
EPS = 1e-6
COMBINED = {(i // 4, i % 4): n for n, i in enumerate(i for i in range(16) if i not in (0, 3, 12, 15))}
BF, F32 = jnp.bfloat16, jnp.float32
HI = lax.Precision.HIGHEST


def iota(shape, dim):
    return lax.broadcasted_iota(jnp.int32, shape, dim)


def dot(a, b, precision=None):
    return jnp.dot(a, b, preferred_element_type=F32, precision=precision)


def params():
    return pltpu.CompilerParams(vmem_limit_bytes=56 * 2**20)


def cost(flops, nbytes):
    return pl.CostEstimate(flops=flops, bytes_accessed=nbytes, transcendentals=0)


def to_groups(lane):
    return (iota((C, 128), 0) // 16 + lane == iota((C, 128), 1)).astype(F32)


def from_groups(lane, dtype=F32):
    return (iota((128, C), 1) // 16 + lane == iota((128, C), 0)).astype(dtype)


def group_stats(mean, m2, count, lane):
    group_mean = dot(mean, to_groups(lane), HI) * (1.0 / 16.0)
    off = mean - dot(group_mean, from_groups(lane), HI)
    return group_mean + dot(m2 + count * (off * off), to_groups(lane + 32), HI)


def merge(parts, count):
    n = parts.shape[0]
    total = jnp.sum(parts, axis=0)
    mean = total * (1.0 / n)
    off = parts - mean[None]
    between = pltpu.roll(jnp.sum(off * off, axis=0), 32, 1)
    is_mean = (iota(total.shape, 1) // 32) % 2 == 0
    return jnp.where(is_mean, mean, total + count * between)


def split_terms(v):
    high = v.astype(BF).astype(F32)
    middle = (v - high).astype(BF).astype(F32)
    return jnp.concatenate([high, middle, v - high - middle, jnp.zeros_like(v)], axis=1)


def join_terms(v):
    return sum(v[:, 128 * i : 128 * i + 128].astype(F32) for i in range(3))


def latent_stats_kernel(x_ref, up_ref, down_ref, out_ref):
    n = x_ref.shape[0]
    step = 256

    def add(i, total):
        rows = x_ref[pl.ds(pl.multiple_of(i * step, step), step), :].astype(F32)
        return total + jnp.sum(rows.reshape(step // 8, 8, C), axis=0)

    total = lax.fori_loop(0, n // step, add, jnp.zeros((8, C), F32))
    mean = jnp.sum(total, axis=0, keepdims=True) * (1.0 / n)

    def add_square(i, total):
        rows = x_ref[pl.ds(pl.multiple_of(i * step, step), step), :].astype(F32) - mean
        return total + jnp.sum((rows * rows).reshape(step // 8, 8, C), axis=0)

    total = lax.fori_loop(0, n // step, add_square, jnp.zeros((8, C), F32))
    m2 = jnp.sum(total, axis=0, keepdims=True)
    wide = lambda v: jnp.broadcast_to(v, (8, C))
    row = split_terms(group_stats(wide(mean), wide(m2), float(n), 0))
    row = jnp.concatenate([row, jnp.zeros_like(row)], axis=0).astype(BF)
    out_ref[...] = row
    up_ref[:128, :] = x_ref[n - 128 :, :]
    down_ref[:128, :] = x_ref[:128, :]
    up_ref[128:, :] = row
    down_ref[128:, :] = row


def finish(whole, count):
    is_mean = (iota(whole.shape, 1) // 32) % 2 == 0
    return jnp.where(is_mean, whole, lax.rsqrt(whole * (1.0 / count) + EPS))


def inner_kernel(x_ref, out_ref):
    x = x_ref[...].astype(F32).reshape(2, S, 4, S, C)
    for k in range(4):
        for half in range(2):
            out_ref[2 * k + half] = x[half, :, k].reshape(S * S, C).astype(BF)


def rim_kernel(x_ref, up_ref, down_ref, own_ref, far_ref, out_ref, wide, rim):
    n = 2048.0 * 16.0
    parts = [own_ref[...], far_ref[...], up_ref[128:, :], down_ref[128:, :]]
    whole = merge(jnp.stack([join_terms(v)[:8] for v in parts]), n)
    stats = split_terms(jnp.where(iota(whole.shape, 1) < 64, finish(whole, 4.0 * n), 0.0))[:1]
    rim[...] = jnp.zeros_like(rim)

    def lanes(q):
        at = slice(128 * q, 128 * q + 128)
        wide[0] = up_ref[:128, at].astype(F32)
        wide[17] = down_ref[:128, at].astype(F32)
        wide[1:17] = x_ref[:, :, at].astype(F32)
        for half in range(2):
            rim[half, pl.ds(20, 16, stride=RIM), :] = jnp.broadcast_to(stats[:, at], (16, 128))
            for r in range(W):
                left, right = (16, 17) if r == 0 else (18, 19) if r == W - 1 else (r - 1, S + r - 1)
                rim[half, pl.ds(RIM + left, 15, stride=RIM), :] = wide[S * half + r, pl.ds(S - 1, 15, stride=S), :]
                rim[half, pl.ds(right, 15, stride=RIM), :] = wide[S * half + r, pl.ds(S, 15, stride=S), :]
            out_ref[:, half, :, at] = rim[half].reshape(16, RIM, 128).astype(BF)

    for q in range(4):
        lanes(q)


def weights_kernel(w_ref, out_ref):
    def products(g):
        ends = (g[0] + g[2]) * 0.5
        middle = g[1] * 0.5
        return g[0], ends + middle, ends - middle, g[2]

    w = [[w_ref[a, 0, e].astype(F32) for e in range(3)] for a in range(3)]
    columns = [products(w[a]) for a in range(3)]
    for l in range(4):
        for j, v in enumerate(products([columns[a][l] for a in range(3)])):
            if (j, l) in COMBINED:
                out_ref[COMBINED[j, l]] = v.astype(BF)


def products_kernel(wq_ref, wk_ref, wv_ref, wo_ref, score_ref, update_ref):
    score = lax.dot_general(wq_ref[...], wk_ref[...], (((1,), (1,)), ((), ())), preferred_element_type=F32)
    score_ref[...] = (score * (1.0 / C**0.5)).astype(BF)
    update_ref[...] = dot(wv_ref[...], wo_ref[...]).astype(BF)


def turned(in_ref, first, pixels):
    rows = pixels * T
    to, at = iota((rows, rows), 0), iota((rows, rows), 1)
    frame = 2 * (to % P2) + (to // P2) % 2
    turn = (at == frame * pixels + to // T).astype(BF)
    values = in_ref[:, pl.ds(first, pixels), :].reshape(rows, C)
    return dot(turn, values).reshape(pixels, 2, P2, C)


def activate(values, norm):
    u = (values - norm[0][None]) * norm[1][None]
    return (u / (1.0 + jnp.exp(-u))).astype(BF).astype(F32)


def time_terms(act):
    pixels = act.shape[0]
    even, odd = act[:, 0], act[:, 1]
    start = iota((pixels * P2, C), 0) % P2 == 0

    def before(v):
        v = pltpu.roll(v.reshape(pixels * P2, C), 1, 0)
        return jnp.where(start, 0.0, v).reshape(pixels, P2, C)

    even1, odd1 = before(even), before(odd)
    return even1 - even, odd1 + even, even - odd1, odd1 - odd


def conv_kernel(
    place_ref, in_ref, rim_ref, core_ref, band_ref, plain_ref, w0, w1, w2, mid_ref, stats_ref,
    terms, ends, sides, latent, sums, norm, held, sems,
):
    def arrival(j, l, b, source):
        slot = 4 * (j % 3) + l
        return pltpu.make_async_copy(source, held.at[slot, b], sems.at[slot, b])

    def start(j):
        for l in range(4):
            for b, w in enumerate((w0, w1, w2)):
                summed = (j, l) in COMBINED
                arrival(j, l, b, w.at[COMBINED[j, l]] if summed else plain_ref.at[2 * j // 3, b, 2 * l // 3]).start()

    for j in range(3):
        start(j)

    block, z = place_ref[0], place_ref[1]
    half, column = block % 2, block // 2
    above = (half == 0) & (z == 0)
    below = (half == 1) & (z == 3)
    tail = rim_ref[:, 16:RIM, :].reshape(T * 8, C)
    row = iota((T, T * 8), 0)
    row = 2 * (row % P2) + row // P2
    pieces = dot((iota((T, T * 8), 1) == row * 8 + 4).astype(BF), tail).astype(BF)
    for i in range(2):
        norm[i] = sum(
            dot(pieces[:, 128 * k : 128 * k + 128], from_groups(32 * i, BF)) for k in range(3)
        ).reshape(2, P2, C)

    for first, pixels in ((0, 16), (16, 8)):
        act = activate(turned(rim_ref, first, pixels), norm)
        p = iota(act.shape, 0) + first
        out = (column == 0) & ((p < 8) | (p == 16) | (p == 18))
        out = out | (column == 15) & ((p >= 8) & (p < 16) | (p == 17) | (p == 19))
        out = out | above & ((p == 16) | (p == 17)) | below & (p >= 18)
        for j, v in enumerate(time_terms(jnp.where(out, 0.0, act))):
            for q in range(min(pixels, 20 - first)):
                p = first + q
                if p < 16:
                    sides[j, p // S, p % S] = v[q]
                else:
                    ends[j, (p - 16) // 2, (p % 2) * (W - 1)] = v[q]
    core, band = turned(core_ref, 0, S), turned(band_ref, 0, S)
    for i, values in enumerate((jnp.where(half == 0, band, core), jnp.where(half == 0, core, band))):
        act = jnp.where(below if i else above, 0.0, activate(values, norm))
        for j, v in enumerate(time_terms(act)):
            ends[j, i, 1 : S + 1] = v

    def columns(v, j, at):
        v = v.reshape(2, W // 2, 2, P2, C)
        even, odd = v[:, :, 0], v[:, :, 1]
        before, after, odd_before = even[:, :-1], even[:, 1:], odd[:, :-1]
        for l, u in enumerate((before - after, odd_before + after, after - odd_before, odd_before - odd[:, 1:])):
            u = u.astype(BF)
            for i, r in enumerate(at):
                terms[j, l, r] = u[i]

    for j in range(4):
        columns(ends[j], j, (0, W - 1))

    def two_rows(k, _):
        first = pl.multiple_of(16 * k, 16)
        values = turned(in_ref, first, 16)
        latent[pl.ds(first, 16)] = values.astype(BF)
        for j, v in enumerate(time_terms(activate(values, norm))):
            left, right = (sides[j, i, pl.ds(2 * k, 2)][:, None] for i in range(2))
            columns(jnp.concatenate([left, v.reshape(2, S, P2, C), right], axis=1), j, (2 * k + 1, 2 * k + 2))
        return 0

    lax.fori_loop(0, S // 2, two_rows, 0)

    def term(j, _):
        @pl.when(j == 1)
        def _():
            start(3)

        for l in range(4):
            for b in range(3):
                arrival(j, l, b, w0.at[0]).wait()
        for q in range(2):
            m = []
            for l in range(4):
                rows = [terms[j, l, 4 * q + b : 4 * q + b + 4].reshape(16 * P2, C) for b in range(3)]
                weight = held[4 * (j % 3) + l].reshape(3 * C, C)
                m.append(dot(jnp.concatenate(rows, axis=1), weight).reshape(4, 4, P2, C))
            sums[j, 0, 4 * q : 4 * q + 4] = m[0] + m[1] + m[2]
            sums[j, 1, 4 * q : 4 * q + 4] = m[1] - m[2] - m[3]
        return 0

    lax.fori_loop(0, 4, term, 0)

    def finish_row(r, total):
        for c in range(S):
            m = [sums[j, c % 2, r, c // 2] for j in range(4)]
            for i, v in enumerate((m[0] + m[1] + m[2], m[1] - m[2] - m[3])):
                v = (latent[S * r + c, i].astype(F32) + v).astype(BF)
                mid_ref[S * r + c, i] = v
                total[i] = total[i] + v.astype(F32)
        return total

    zero = jnp.zeros((P2, C), F32)
    total = lax.fori_loop(0, S, finish_row, [zero, zero])
    mean = [v * (1.0 / (S * S)) for v in total]

    def squares(r, total):
        for c in range(S):
            for i in range(2):
                off = mid_ref[S * r + c, i].astype(F32) - mean[i]
                total[i] = total[i] + off * off
        return total

    total = lax.fori_loop(0, S, squares, [zero, zero])
    stats = sum(group_stats(mean[i], total[i], float(S * S), 64 * i) for i in range(2))
    stats_ref[...] = jnp.broadcast_to(stats[None], stats_ref.shape)


def merge_kernel(parts_ref, out_ref):
    whole = merge(parts_ref[...], float(S * S * 16))
    out_ref[...] = jnp.broadcast_to(whole[None], out_ref.shape)


def attend_kernel(mid_ref, parts_ref, score_ref, update_ref, out_ref, norm):
    @pl.when(pl.program_id(0) == 0)
    def _():
        count = float(S * S * 16 * 8)
        whole = finish(merge(parts_ref[...], count), 16.0 * count)
        for i in range(2):
            for j in range(2):
                norm[i, j] = dot(whole, from_groups(64 * j + 32 * i), HI)

    pixels = mid_ref.shape[0]
    rows = pixels * T
    mid = mid_ref[...].astype(F32)
    flat = ((mid - norm[0][None]) * norm[1][None]).astype(BF).reshape(rows, C)
    query = dot(flat, score_ref[...]).astype(BF)
    n = 256
    row, column = iota((n, n), 0), iota((n, n), 1)
    frame = lambda v: 2 * (v % P2) + (v // P2) % 2
    seen = (row // T == column // T) & (frame(row) >= frame(column))
    parts = []
    for i in range(rows // n):
        at = slice(i * n, i * n + n)
        scores = lax.dot_general(query[at], flat[at], (((1,), (1,)), ((), ())), preferred_element_type=F32)
        scores = jnp.where(seen, scores, -1e30)
        weights = jnp.exp(scores - jnp.max(scores, axis=1, keepdims=True))
        weights = (weights / jnp.sum(weights, axis=1, keepdims=True)).astype(BF)
        parts.append(dot(weights, flat[at]).astype(BF))
    update = dot(jnp.concatenate(parts, axis=0), update_ref[...])
    out = (mid.reshape(rows, C) + update).astype(BF)
    to = iota((n, n), 0)
    frame = to // S
    turn = (iota((n, n), 1) == (to % S) * T + (frame % 2) * P2 + frame // 2).astype(BF)
    for i in range(rows // (2 * n)):
        pair = [dot(turn, out[(2 * i + k) * n : (2 * i + k + 1) * n]).reshape(T, S, C) for k in range(2)]
        out_ref[:, 16 * i : 16 * i + 16, :] = jnp.concatenate(pair, axis=1).astype(BF)


def local(latents, conv_weight, w_query, w_key, w_value, w_out):
    x = latents.reshape(16, 128, C)
    vmem = pl.BlockSpec(memory_space=pltpu.VMEM)
    smem = pl.BlockSpec(memory_space=pltpu.SMEM)
    whole = lambda *shape: pl.BlockSpec(shape, lambda i: (0,) * len(shape))
    exchange = lambda v, axes: lax.all_to_all(v[None], axes, split_axis=1, concat_axis=0, tiled=True)[:, 0]
    place = jnp.stack([lax.axis_index(TM), lax.axis_index("rows")]).astype(jnp.int32)

    inner = pl.pallas_call(
        inner_kernel,
        grid=(4,),
        out_shape=jax.ShapeDtypeStruct((32, S * S, C), BF),
        in_specs=[pl.BlockSpec((16, 32, C), lambda i: (0, i, 0))],
        out_specs=pl.BlockSpec((8, S * S, C), lambda i: (i, 0, 0)),
        compiler_params=params(),
        cost_estimate=cost(2**20, 4 * 2**20),
        name="inner",
    )(x)
    patch = exchange(inner, TM)
    row = jax.ShapeDtypeStruct((144, C), BF)
    up, down, own = pl.pallas_call(
        latent_stats_kernel,
        out_shape=(row, row, jax.ShapeDtypeStruct((16, C), BF)),
        in_specs=[vmem],
        out_specs=(vmem,) * 3,
        compiler_params=params(),
        cost_estimate=cost(2048 * C * 4, 2048 * C * 2),
        name="latent_stats",
    )(x.reshape(2048, C))
    own, *products = lax.optimization_barrier((own, w_query, w_key, w_value, w_out))
    score, update = pl.pallas_call(
        products_kernel,
        out_shape=(jax.ShapeDtypeStruct((C, C), BF),) * 2,
        in_specs=[vmem] * 4,
        out_specs=(vmem,) * 2,
        compiler_params=params(),
        cost_estimate=cost(2 * 2 * C**3, 6 * C * C * 2),
        name="products",
    )(*products)
    around = lambda v, by: lax.ppermute(v, "rows", [(i, (i + by) % 4) for i in range(4)])
    up, down, far = around(up, 1), around(down, 3), around(own, 2)
    wide_x, score, update = lax.optimization_barrier((x, score, update))
    rim = pl.pallas_call(
        rim_kernel,
        out_shape=jax.ShapeDtypeStruct((16, 2, RIM, C), BF),
        in_specs=[vmem] * 5,
        out_specs=vmem,
        scratch_shapes=[pltpu.VMEM((18, 128, 128), F32), pltpu.VMEM((2, 16 * RIM, 128), F32)],
        compiler_params=params(),
        cost_estimate=cost(2**22, 4 * 2**20),
        name="rim",
    )(wide_x, up, down, own, far).reshape(32, RIM, C)

    def combine(b, conv_weight):
        return pl.pallas_call(
            weights_kernel,
            grid=(4,),
            out_shape=jax.ShapeDtypeStruct((12, C, C), BF),
            in_specs=[pl.BlockSpec((3, 1, 3, 128, C), lambda i: (0, b, 0, i, 0))],
            out_specs=pl.BlockSpec((12, 128, C), lambda i: (0, i, 0)),
            compiler_params=params(),
            cost_estimate=cost(3 * 8 * C * C, 21 * C * C * 2),
            name="weights",
        )(conv_weight)

    rim, early = lax.optimization_barrier((rim, conv_weight))
    rim, patch, *weights = lax.optimization_barrier((rim, patch, combine(0, early)))
    rim = exchange(rim, TM)
    first = lax.axis_index("core") == 0
    row = lambda at: lax.dynamic_slice_in_dim(patch, at, S, axis=1)
    core, band = row(jnp.where(first, S * S - S, 0)), row(jnp.where(first, 0, S * S - S))
    core = lax.ppermute(core, "core", [(0, 1), (1, 0)])
    pairs = [(4 + i, i + 1) for i in range(3)] + [(i + 1, 4 + i) for i in range(3)]
    band = lax.ppermute(band, ("core", "rows"), pairs)
    core, band, late = lax.optimization_barrier((core, band, conv_weight))
    weights += [combine(b, late) for b in (1, 2)]

    mid, stats = pl.pallas_call(
        conv_kernel,
        out_shape=(jax.ShapeDtypeStruct((S * S, 2, P2, C), BF), jax.ShapeDtypeStruct((8, P2, 128), F32)),
        in_specs=[smem] + [vmem] * 4 + [pl.BlockSpec(memory_space=pl.ANY)] * 4,
        out_specs=(vmem, vmem),
        scratch_shapes=[
            pltpu.VMEM((4, 4, W, S // 2, P2, C), BF),
            pltpu.VMEM((4, 2, W, P2, C), F32),
            pltpu.VMEM((4, 2, S, P2, C), F32),
            pltpu.VMEM((S * S, 2, P2, C), BF),
            pltpu.VMEM((4, 2, S, S // 2, P2, C), F32),
            pltpu.VMEM((2, 2, P2, C), F32),
            pltpu.VMEM((12, 3, C, C), BF),
            pltpu.SemaphoreType.DMA((12, 3)),
        ],
        compiler_params=params(),
        cost_estimate=cost(512 * 48 * C * C * 2, 28 * 2**20),
        name="conv",
    )(place, patch, rim, core, band, conv_weight, *weights)
    parts = pl.pallas_call(
        merge_kernel,
        out_shape=jax.ShapeDtypeStruct((16, P2, 128), F32),
        in_specs=[vmem],
        out_specs=vmem,
        compiler_params=params(),
        name="merge",
    )(exchange(stats, ("core", "rows")))
    parts = exchange(parts, ("x", "y"))
    pixels = 32
    out = pl.pallas_call(
        attend_kernel,
        grid=(S * S // pixels,),
        out_shape=jax.ShapeDtypeStruct((T, S * S, C), BF),
        in_specs=[pl.BlockSpec((pixels, 2, P2, C), lambda i: (i, 0, 0, 0)), whole(16, P2, 128)] + [whole(C, C)] * 2,
        out_specs=pl.BlockSpec((T, pixels, C), lambda i: (0, i, 0)),
        scratch_shapes=[pltpu.VMEM((2, 2, P2, C), F32)],
        compiler_params=params(),
        cost_estimate=cost(2048 * C * C * 2 * 4, 8 * 2**20),
        name="attend",
    )(mid, parts, score, update)
    back = exchange(out, TM)
    back = back.reshape(16, 2, S, S, C).transpose(1, 2, 0, 3, 4)
    return back.reshape(1, 16, 128, C)


def solution(mesh):
    mesh = Mesh(mesh.devices.reshape(4, 4, 2, 4), TM + ("rows",))
    in_specs = (P(TM, "rows", None, None), P(), P(), P(), P(), P())
    out_specs = P(TM, "rows", None, None)
    return jax.shard_map(local, mesh=mesh, in_specs=in_specs, out_specs=out_specs, check_vma=False)
```

```python
import jax
import jax.numpy as jnp
from jax import lax
from jax.experimental import pallas as pl
from jax.experimental.pallas import tpu as pltpu
from jax.sharding import Mesh
from jax.sharding import PartitionSpec as P

GROUPS = 32
T = 32
C = 512
S = 8
W = S + 2
P2 = T // 2
RIM = 24
TM = ("x", "y", "core")
EPS = 1e-6
COMBINED = {(i // 4, i % 4): n for n, i in enumerate(i for i in range(16) if i not in (0, 3, 12, 15))}
BF, F32 = jnp.bfloat16, jnp.float32
HI = lax.Precision.HIGHEST


def iota(shape, dim):
    return lax.broadcasted_iota(jnp.int32, shape, dim)


def dot(a, b, precision=None):
    return jnp.dot(a, b, preferred_element_type=F32, precision=precision)


def params():
    return pltpu.CompilerParams(vmem_limit_bytes=56 * 2**20)


def cost(flops, nbytes):
    return pl.CostEstimate(flops=flops, bytes_accessed=nbytes, transcendentals=0)


def to_groups(lane):
    return (iota((C, 128), 0) // 16 + lane == iota((C, 128), 1)).astype(F32)


def from_groups(lane, dtype=F32):
    return (iota((128, C), 1) // 16 + lane == iota((128, C), 0)).astype(dtype)


def group_stats(mean, m2, count, lane):
    group_mean = dot(mean, to_groups(lane), HI) * (1.0 / 16.0)
    off = mean - dot(group_mean, from_groups(lane), HI)
    return group_mean + dot(m2 + count * (off * off), to_groups(lane + 32), HI)


def merge(parts, count):
    n = parts.shape[0]
    total = jnp.sum(parts, axis=0)
    mean = total * (1.0 / n)
    off = parts - mean[None]
    between = pltpu.roll(jnp.sum(off * off, axis=0), 32, 1)
    is_mean = (iota(total.shape, 1) // 32) % 2 == 0
    return jnp.where(is_mean, mean, total + count * between)


def split_terms(v):
    high = v.astype(BF).astype(F32)
    middle = (v - high).astype(BF).astype(F32)
    return jnp.concatenate([high, middle, v - high - middle, jnp.zeros_like(v)], axis=1)


def join_terms(v):
    return sum(v[:, 128 * i : 128 * i + 128].astype(F32) for i in range(3))


def latent_stats_kernel(x_ref, up_ref, down_ref, out_ref):
    n = x_ref.shape[0]
    step = 256

    def add(i, total):
        rows = x_ref[pl.ds(pl.multiple_of(i * step, step), step), :].astype(F32)
        return total + jnp.sum(rows.reshape(step // 8, 8, C), axis=0)

    total = lax.fori_loop(0, n // step, add, jnp.zeros((8, C), F32))
    mean = jnp.sum(total, axis=0, keepdims=True) * (1.0 / n)

    def add_square(i, total):
        rows = x_ref[pl.ds(pl.multiple_of(i * step, step), step), :].astype(F32) - mean
        return total + jnp.sum((rows * rows).reshape(step // 8, 8, C), axis=0)

    total = lax.fori_loop(0, n // step, add_square, jnp.zeros((8, C), F32))
    m2 = jnp.sum(total, axis=0, keepdims=True)
    wide = lambda v: jnp.broadcast_to(v, (8, C))
    row = split_terms(group_stats(wide(mean), wide(m2), float(n), 0))
    row = jnp.concatenate([row, jnp.zeros_like(row)], axis=0).astype(BF)
    out_ref[...] = row
    up_ref[:128, :] = x_ref[n - 128 :, :]
    down_ref[:128, :] = x_ref[:128, :]
    up_ref[128:, :] = row
    down_ref[128:, :] = row


def finish(whole, count):
    is_mean = (iota(whole.shape, 1) // 32) % 2 == 0
    return jnp.where(is_mean, whole, lax.rsqrt(whole * (1.0 / count) + EPS))


def inner_kernel(x_ref, out_ref):
    x = x_ref[...].astype(F32).reshape(2, S, 8, S, C)
    for k in range(8):
        for half in range(2):
            out_ref[2 * k + half] = x[half, :, k].reshape(S * S, C).astype(BF)


def rim_kernel(x_ref, up_ref, down_ref, own_ref, far_ref, out_ref, wide, rim):
    n = 2048.0 * 16.0
    parts = [own_ref[...], far_ref[...], up_ref[128:, :], down_ref[128:, :]]
    whole = merge(jnp.stack([join_terms(v)[:8] for v in parts]), n)
    stats = split_terms(jnp.where(iota(whole.shape, 1) < 64, finish(whole, 4.0 * n), 0.0))[:1]
    rim[...] = jnp.zeros_like(rim)

    def lanes(q):
        at = slice(128 * q, 128 * q + 128)
        wide[0] = up_ref[:128, at].astype(F32)
        wide[17] = down_ref[:128, at].astype(F32)
        wide[1:17] = x_ref[:, :, at].astype(F32)
        for half in range(2):
            rim[half, pl.ds(20, 16, stride=RIM), :] = jnp.broadcast_to(stats[:, at], (16, 128))
            for r in range(W):
                left, right = (16, 17) if r == 0 else (18, 19) if r == W - 1 else (r - 1, S + r - 1)
                rim[half, pl.ds(RIM + left, 15, stride=RIM), :] = wide[S * half + r, pl.ds(S - 1, 15, stride=S), :]
                rim[half, pl.ds(right, 15, stride=RIM), :] = wide[S * half + r, pl.ds(S, 15, stride=S), :]
            out_ref[:, half, :, at] = rim[half].reshape(16, RIM, 128).astype(BF)

    for q in range(4):
        lanes(q)


def weights_kernel(w_ref, *refs):
    out_ref = refs[-1]

    def products(g):
        ends = (g[0] + g[2]) * 0.5
        middle = g[1] * 0.5
        return g[0], ends + middle, ends - middle, g[2]

    def rows(i, _):
        at = pl.ds(pl.multiple_of(16 * i, 16), 16)
        for q in range(4):
            lanes = slice(128 * q, 128 * q + 128)
            columns = [products([w_ref[a, 0, e, at, lanes].astype(F32) for e in range(3)]) for a in range(3)]
            for l in range(4):
                for j, v in enumerate(products([columns[a][l] for a in range(3)])):
                    if (j, l) in COMBINED:
                        out_ref[COMBINED[j, l], 0, at, lanes] = v.astype(BF)
        return 0

    lax.fori_loop(0, 16, rows, 0)


def turned(in_ref, first, pixels):
    rows = pixels * T
    to, at = iota((rows, rows), 0), iota((rows, rows), 1)
    frame = 2 * (to % P2) + (to // P2) % 2
    turn = (at == frame * pixels + to // T).astype(BF)
    values = in_ref[:, pl.ds(first, pixels), :].reshape(rows, C)
    return dot(turn, values).reshape(pixels, 2, P2, C)


def activate(values, norm):
    u = (values - norm[0][None]) * norm[1][None]
    return (u / (1.0 + jnp.exp(-u))).astype(BF).astype(F32)


def time_terms(act):
    pixels = act.shape[0]
    even, odd = act[:, 0], act[:, 1]
    start = iota((pixels * P2, C), 0) % P2 == 0

    def before(v):
        v = pltpu.roll(v.reshape(pixels * P2, C), 1, 0)
        return jnp.where(start, 0.0, v).reshape(pixels, P2, C)

    even1, odd1 = before(even), before(odd)
    return even1 - even, odd1 + even, even - odd1, odd1 - odd


def conv_kernel(
    place_ref, in_ref, rim_ref, core_ref, band_ref, plain_ref, sums_ref, mid_ref, stats_ref,
    terms, ends, sides, latent, sums, norm, held, sems,
):
    def arrival(j, l, b, source):
        slot = 4 * (j % 3) + l
        return pltpu.make_async_copy(source, held.at[slot, b], sems.at[slot, b])

    def start(j):
        for l in range(4):
            for b in range(3):
                summed = (j, l) in COMBINED
                source = sums_ref.at[COMBINED[j, l], b] if summed else plain_ref.at[2 * j // 3, b, 2 * l // 3]
                arrival(j, l, b, source).start()

    for j in range(3):
        start(j)

    block, z = place_ref[0], place_ref[1]
    half, column = block % 2, block // 2
    above = (half == 0) & (z == 0)
    below = (half == 1) & (z == 3)
    tail = rim_ref[:, 16:RIM, :].reshape(T * 8, C)
    row = iota((T, T * 8), 0)
    row = 2 * (row % P2) + row // P2
    pieces = dot((iota((T, T * 8), 1) == row * 8 + 4).astype(BF), tail).astype(BF)
    for i in range(2):
        norm[i] = sum(
            dot(pieces[:, 128 * k : 128 * k + 128], from_groups(32 * i, BF)) for k in range(3)
        ).reshape(2, P2, C)

    for first, pixels in ((0, 16), (16, 8)):
        act = activate(turned(rim_ref, first, pixels), norm)
        p = iota(act.shape, 0) + first
        out = (column == 0) & ((p < 8) | (p == 16) | (p == 18))
        out = out | (column == 15) & ((p >= 8) & (p < 16) | (p == 17) | (p == 19))
        out = out | above & ((p == 16) | (p == 17)) | below & (p >= 18)
        for j, v in enumerate(time_terms(jnp.where(out, 0.0, act))):
            for q in range(min(pixels, 20 - first)):
                p = first + q
                if p < 16:
                    sides[j, p // S, p % S] = v[q]
                else:
                    ends[j, (p - 16) // 2, (p % 2) * (W - 1)] = v[q]
    core, band = turned(core_ref, 0, S), turned(band_ref, 0, S)
    for i, values in enumerate((jnp.where(half == 0, band, core), jnp.where(half == 0, core, band))):
        act = jnp.where(below if i else above, 0.0, activate(values, norm))
        for j, v in enumerate(time_terms(act)):
            ends[j, i, 1 : S + 1] = v

    def columns(v, j, at):
        v = v.reshape(2, W // 2, 2, P2, C)
        even, odd = v[:, :, 0], v[:, :, 1]
        before, after, odd_before = even[:, :-1], even[:, 1:], odd[:, :-1]
        for l, u in enumerate((before - after, odd_before + after, after - odd_before, odd_before - odd[:, 1:])):
            u = u.astype(BF)
            for i, r in enumerate(at):
                terms[j, l, r] = u[i]

    for j in range(4):
        columns(ends[j], j, (0, W - 1))

    def two_rows(k, _):
        first = pl.multiple_of(16 * k, 16)
        values = turned(in_ref, first, 16)
        latent[pl.ds(first, 16)] = values.astype(BF)
        for j, v in enumerate(time_terms(activate(values, norm))):
            left, right = (sides[j, i, pl.ds(2 * k, 2)][:, None] for i in range(2))
            columns(jnp.concatenate([left, v.reshape(2, S, P2, C), right], axis=1), j, (2 * k + 1, 2 * k + 2))
        return 0

    lax.fori_loop(0, S // 2, two_rows, 0)

    def term(j, _):
        @pl.when(j == 1)
        def _():
            start(3)

        for l in range(4):
            for b in range(3):
                arrival(j, l, b, sums_ref.at[0, 0]).wait()
        for q in range(2):
            m = []
            for l in range(4):
                rows = [terms[j, l, 4 * q + b : 4 * q + b + 4].reshape(16 * P2, C) for b in range(3)]
                weight = held[4 * (j % 3) + l].reshape(3 * C, C)
                m.append(dot(jnp.concatenate(rows, axis=1), weight).reshape(4, 4, P2, C))
            sums[j, 0, 4 * q : 4 * q + 4] = m[0] + m[1] + m[2]
            sums[j, 1, 4 * q : 4 * q + 4] = m[1] - m[2] - m[3]
        return 0

    lax.fori_loop(0, 4, term, 0)

    def finish_row(r, total):
        for c in range(S):
            m = [sums[j, c % 2, r, c // 2] for j in range(4)]
            for i, v in enumerate((m[0] + m[1] + m[2], m[1] - m[2] - m[3])):
                v = (latent[S * r + c, i].astype(F32) + v).astype(BF)
                mid_ref[S * r + c, i] = v
                total[i] = total[i] + v.astype(F32)
        return total

    zero = jnp.zeros((P2, C), F32)
    total = lax.fori_loop(0, S, finish_row, [zero, zero])
    mean = [v * (1.0 / (S * S)) for v in total]

    def squares(r, total):
        for c in range(S):
            for i in range(2):
                off = mid_ref[S * r + c, i].astype(F32) - mean[i]
                total[i] = total[i] + off * off
        return total

    total = lax.fori_loop(0, S, squares, [zero, zero])
    stats = sum(group_stats(mean[i], total[i], float(S * S), 64 * i) for i in range(2))
    stats_ref[...] = jnp.broadcast_to(stats[None], stats_ref.shape)


def merge_kernel(parts_ref, out_ref):
    whole = merge(parts_ref[...], float(S * S * 16))
    out_ref[...] = jnp.broadcast_to(whole[None], out_ref.shape)


def attend_kernel(mid_ref, parts_ref, score_ref, update_ref, out_ref, norm):
    @pl.when(pl.program_id(0) == 0)
    def _():
        count = float(S * S * 16 * 8)
        whole = finish(merge(parts_ref[...], count), 16.0 * count)
        for i in range(2):
            for j in range(2):
                norm[i, j] = dot(whole, from_groups(64 * j + 32 * i), HI)

    pixels = mid_ref.shape[0]
    rows = pixels * T
    mid = mid_ref[...].astype(F32)
    flat = ((mid - norm[0][None]) * norm[1][None]).astype(BF).reshape(rows, C)
    query = dot(flat, score_ref[...]).astype(BF)
    n = 256
    row, column = iota((n, n), 0), iota((n, n), 1)
    frame = lambda v: 2 * (v % P2) + (v // P2) % 2
    seen = (row // T == column // T) & (frame(row) >= frame(column))
    parts = []
    for i in range(rows // n):
        at = slice(i * n, i * n + n)
        scores = lax.dot_general(query[at], flat[at], (((1,), (1,)), ((), ())), preferred_element_type=F32)
        scores = jnp.where(seen, scores, -1e30)
        weights = jnp.exp(scores - jnp.max(scores, axis=1, keepdims=True))
        weights = (weights / jnp.sum(weights, axis=1, keepdims=True)).astype(BF)
        parts.append(dot(weights, flat[at]).astype(BF))
    update = dot(jnp.concatenate(parts, axis=0), update_ref[...])
    out = (mid.reshape(rows, C) + update).astype(BF)
    to = iota((n, n), 0)
    frame = to // S
    turn = (iota((n, n), 1) == (to % S) * T + (frame % 2) * P2 + frame // 2).astype(BF)
    for i in range(rows // (2 * n)):
        pair = [dot(turn, out[(2 * i + k) * n : (2 * i + k + 1) * n]).reshape(T, S, C) for k in range(2)]
        out_ref[:, 16 * i : 16 * i + 16, :] = jnp.concatenate(pair, axis=1).astype(BF)


def local(latents, conv_weight, w_query, w_key, w_value, w_out):
    x = latents.reshape(16, 128, C)
    vmem = pl.BlockSpec(memory_space=pltpu.VMEM)
    smem = pl.BlockSpec(memory_space=pltpu.SMEM)
    whole = lambda *shape: pl.BlockSpec(shape, lambda i: (0,) * len(shape))
    exchange = lambda v, axes: lax.all_to_all(v[None], axes, split_axis=1, concat_axis=0, tiled=True)[:, 0]
    place = jnp.stack([lax.axis_index(TM), lax.axis_index("rows")]).astype(jnp.int32)

    inner = pl.pallas_call(
        inner_kernel,
        grid=(2,),
        out_shape=jax.ShapeDtypeStruct((32, S * S, C), BF),
        in_specs=[pl.BlockSpec((16, 64, C), lambda i: (0, i, 0))],
        out_specs=pl.BlockSpec((16, S * S, C), lambda i: (i, 0, 0)),
        compiler_params=params(),
        cost_estimate=cost(2**20, 4 * 2**20),
        name="inner",
    )(x)
    patch = exchange(inner, TM)
    row = jax.ShapeDtypeStruct((144, C), BF)
    up, down, own = pl.pallas_call(
        latent_stats_kernel,
        out_shape=(row, row, jax.ShapeDtypeStruct((16, C), BF)),
        in_specs=[vmem],
        out_specs=(vmem,) * 3,
        compiler_params=params(),
        cost_estimate=cost(2048 * C * 4, 2048 * C * 2),
        name="latent_stats",
    )(x.reshape(2048, C))
    around = lambda v, by: lax.ppermute(v, "rows", [(i, (i + by) % 4) for i in range(4)])
    up, down, far = around(up, 1), around(down, 3), around(own, 2)
    rim = pl.pallas_call(
        rim_kernel,
        out_shape=jax.ShapeDtypeStruct((16, 2, RIM, C), BF),
        in_specs=[vmem] * 5,
        out_specs=vmem,
        scratch_shapes=[pltpu.VMEM((18, 128, 128), F32), pltpu.VMEM((2, 16 * RIM, 128), F32)],
        compiler_params=params(),
        cost_estimate=cost(2**22, 4 * 2**20),
        name="rim",
    )(x, up, down, own, far).reshape(32, RIM, C)

    def combine(first, conv_weight, *before):
        return pl.pallas_call(
            weights_kernel,
            grid=(3,),
            out_shape=jax.ShapeDtypeStruct((12, 3, C, C), BF),
            in_specs=[pl.BlockSpec((3, 1, 3, 256, C), lambda i: (0, (i + first) // 2, 0, (i + first) % 2, 0))]
            + [pl.BlockSpec(memory_space=pl.ANY)] * len(before),
            out_specs=pl.BlockSpec((12, 1, 256, C), lambda i: (0, (i + first) // 2, (i + first) % 2, 0)),
            input_output_aliases={1: 0} if before else {},
            compiler_params=params(),
            cost_estimate=cost(4 * 8 * C * C, 32 * C * C * 2),
            name="weights",
        )(conv_weight, *before)

    rim, early = lax.optimization_barrier((rim, conv_weight))
    rim, patch, weights = lax.optimization_barrier((rim, patch, combine(0, early)))
    rim = exchange(rim, TM)
    first = lax.axis_index("core") == 0
    row = lambda at: lax.dynamic_slice_in_dim(patch, at, S, axis=1)
    core, band = row(jnp.where(first, S * S - S, 0)), row(jnp.where(first, 0, S * S - S))
    core, band, late = lax.optimization_barrier((core, band, conv_weight))
    core = lax.ppermute(core, "core", [(0, 1), (1, 0)])
    pairs = [(4 + i, i + 1) for i in range(3)] + [(i + 1, 4 + i) for i in range(3)]
    band = lax.ppermute(band, ("core", "rows"), pairs)
    weights = combine(3, late, weights)
    score = (dot(w_query, w_key.T) * (1.0 / C**0.5)).astype(BF)
    update = dot(w_value, w_out).astype(BF)

    mid, stats = pl.pallas_call(
        conv_kernel,
        out_shape=(jax.ShapeDtypeStruct((S * S, 2, P2, C), BF), jax.ShapeDtypeStruct((8, P2, 128), F32)),
        in_specs=[smem] + [vmem] * 4 + [pl.BlockSpec(memory_space=pl.ANY)] * 2,
        out_specs=(vmem, vmem),
        scratch_shapes=[
            pltpu.VMEM((4, 4, W, S // 2, P2, C), BF),
            pltpu.VMEM((4, 2, W, P2, C), F32),
            pltpu.VMEM((4, 2, S, P2, C), F32),
            pltpu.VMEM((S * S, 2, P2, C), BF),
            pltpu.VMEM((4, 2, S, S // 2, P2, C), F32),
            pltpu.VMEM((2, 2, P2, C), F32),
            pltpu.VMEM((12, 3, C, C), BF),
            pltpu.SemaphoreType.DMA((12, 3)),
        ],
        compiler_params=params(),
        cost_estimate=cost(512 * 48 * C * C * 2, 28 * 2**20),
        name="conv",
    )(place, patch, rim, core, band, conv_weight, weights)
    parts = pl.pallas_call(
        merge_kernel,
        out_shape=jax.ShapeDtypeStruct((16, P2, 128), F32),
        in_specs=[vmem],
        out_specs=vmem,
        compiler_params=params(),
        name="merge",
    )(exchange(stats, ("core", "rows")))
    parts = exchange(parts, ("x", "y"))
    pixels = 32
    out = pl.pallas_call(
        attend_kernel,
        grid=(S * S // pixels,),
        out_shape=jax.ShapeDtypeStruct((T, S * S, C), BF),
        in_specs=[pl.BlockSpec((pixels, 2, P2, C), lambda i: (i, 0, 0, 0)), whole(16, P2, 128)] + [whole(C, C)] * 2,
        out_specs=pl.BlockSpec((T, pixels, C), lambda i: (0, i, 0)),
        scratch_shapes=[pltpu.VMEM((2, 2, P2, C), F32)],
        compiler_params=params(),
        cost_estimate=cost(2048 * C * C * 2 * 4, 8 * 2**20),
        name="attend",
    )(mid, parts, score, update)
    back = exchange(out, TM)
    back = back.reshape(16, 2, S, S, C).transpose(1, 2, 0, 3, 4)
    return back.reshape(1, 16, 128, C)


def solution(mesh):
    mesh = Mesh(mesh.devices.reshape(4, 4, 2, 4), TM + ("rows",))
    in_specs = (P(TM, "rows", None, None), P(), P(), P(), P(), P())
    out_specs = P(TM, "rows", None, None)
    return jax.shard_map(local, mesh=mesh, in_specs=in_specs, out_specs=out_specs, check_vma=False)
```

```python
import jax
import jax.numpy as jnp
from jax import lax
from jax.experimental import pallas as pl
from jax.experimental.pallas import tpu as pltpu
from jax.sharding import Mesh
from jax.sharding import PartitionSpec as P

GROUPS = 32
T = 32
C = 512
S = 8
W = S + 2
P2 = T // 2
RIM = 24
TM = ("x", "y", "core")
EPS = 1e-6
COMBINED = {(i // 4, i % 4): n for n, i in enumerate(i for i in range(16) if i not in (0, 3, 12, 15))}
BF, F32 = jnp.bfloat16, jnp.float32
HI = lax.Precision.HIGHEST


def iota(shape, dim):
    return lax.broadcasted_iota(jnp.int32, shape, dim)


def dot(a, b, precision=None):
    return jnp.dot(a, b, preferred_element_type=F32, precision=precision)


def params():
    return pltpu.CompilerParams(vmem_limit_bytes=56 * 2**20)


def cost(flops, nbytes):
    return pl.CostEstimate(flops=flops, bytes_accessed=nbytes, transcendentals=0)


def to_groups(lane):
    return (iota((C, 128), 0) // 16 + lane == iota((C, 128), 1)).astype(F32)


def from_groups(lane, dtype=F32):
    return (iota((128, C), 1) // 16 + lane == iota((128, C), 0)).astype(dtype)


def group_stats(mean, m2, count, lane):
    group_mean = dot(mean, to_groups(lane), HI) * (1.0 / 16.0)
    off = mean - dot(group_mean, from_groups(lane), HI)
    return group_mean + dot(m2 + count * (off * off), to_groups(lane + 32), HI)


def merge(parts, count):
    n = parts.shape[0]
    total = jnp.sum(parts, axis=0)
    mean = total * (1.0 / n)
    off = parts - mean[None]
    between = pltpu.roll(jnp.sum(off * off, axis=0), 32, 1)
    is_mean = (iota(total.shape, 1) // 32) % 2 == 0
    return jnp.where(is_mean, mean, total + count * between)


def split_terms(v):
    high = v.astype(BF).astype(F32)
    middle = (v - high).astype(BF).astype(F32)
    return jnp.concatenate([high, middle, v - high - middle, jnp.zeros_like(v)], axis=1)


def join_terms(v):
    return sum(v[:, 128 * i : 128 * i + 128].astype(F32) for i in range(3))


def latent_stats_kernel(x_ref, up_ref, down_ref, out_ref):
    n = x_ref.shape[0]
    step = 64

    pivot = x_ref[:16, :].astype(F32)[:1]

    def add(i, totals):
        rows = x_ref[pl.ds(pl.multiple_of(i * step, step), step), :].astype(F32) - pivot
        rows = rows.reshape(step // 8, 8, C)
        return totals[0] + jnp.sum(rows, axis=0), totals[1] + jnp.sum(rows * rows, axis=0)

    zero = jnp.zeros((8, C), F32)
    totals = lax.fori_loop(0, n // step, add, (zero, zero))
    off = jnp.sum(totals[0], axis=0, keepdims=True) * (1.0 / n)
    mean = pivot + off
    m2 = jnp.sum(totals[1], axis=0, keepdims=True) - n * off * off
    wide = lambda v: jnp.broadcast_to(v, (8, C))
    row = split_terms(group_stats(wide(mean), wide(m2), float(n), 0))
    row = jnp.concatenate([row, jnp.zeros_like(row)], axis=0).astype(BF)
    out_ref[...] = row
    up_ref[:128, :] = x_ref[n - 128 :, :]
    down_ref[:128, :] = x_ref[:128, :]
    up_ref[128:, :] = row
    down_ref[128:, :] = row


def finish(whole, count):
    is_mean = (iota(whole.shape, 1) // 32) % 2 == 0
    return jnp.where(is_mean, whole, lax.rsqrt(whole * (1.0 / count) + EPS))


def inner_kernel(x_ref, out_ref):
    x = x_ref[...].astype(F32).reshape(2, S, 8, S, C)
    for k in range(8):
        for half in range(2):
            out_ref[2 * k + half] = x[half, :, k].reshape(S * S, C).astype(BF)


def rim_kernel(x_ref, up_ref, down_ref, own_ref, far_ref, out_ref, wide, rim):
    n = 2048.0 * 16.0
    parts = [own_ref[...], far_ref[...], up_ref[128:, :], down_ref[128:, :]]
    whole = merge(jnp.stack([join_terms(v)[:8] for v in parts]), n)
    stats = split_terms(jnp.where(iota(whole.shape, 1) < 64, finish(whole, 4.0 * n), 0.0))[:1]
    rim[...] = jnp.zeros_like(rim)

    def lanes(q):
        at = slice(128 * q, 128 * q + 128)
        wide[0] = up_ref[:128, at].astype(F32)
        wide[17] = down_ref[:128, at].astype(F32)
        wide[1:17] = x_ref[:, :, at].astype(F32)
        for half in range(2):
            rim[half, pl.ds(20, 16, stride=RIM), :] = jnp.broadcast_to(stats[:, at], (16, 128))
            for r in range(W):
                left, right = (16, 17) if r == 0 else (18, 19) if r == W - 1 else (r - 1, S + r - 1)
                rim[half, pl.ds(RIM + left, 15, stride=RIM), :] = wide[S * half + r, pl.ds(S - 1, 15, stride=S), :]
                rim[half, pl.ds(right, 15, stride=RIM), :] = wide[S * half + r, pl.ds(S, 15, stride=S), :]
            out_ref[:, half, :, at] = rim[half].reshape(16, RIM, 128).astype(BF)

    for q in range(4):
        lanes(q)


def weights_kernel(w_ref, *refs):
    out_ref = refs[-1]

    def products(g):
        ends = (g[0] + g[2]) * 0.5
        middle = g[1] * 0.5
        return g[0], ends + middle, ends - middle, g[2]

    def rows(i, _):
        at = pl.ds(pl.multiple_of(16 * i, 16), 16)
        for q in range(4):
            lanes = slice(128 * q, 128 * q + 128)
            columns = [products([w_ref[a, 0, e, at, lanes].astype(F32) for e in range(3)]) for a in range(3)]
            for l in range(4):
                for j, v in enumerate(products([columns[a][l] for a in range(3)])):
                    if (j, l) in COMBINED:
                        out_ref[COMBINED[j, l], 0, at, lanes] = v.astype(BF)
        return 0

    lax.fori_loop(0, 16, rows, 0)


def turned(in_ref, first, pixels):
    rows = pixels * T
    to, at = iota((rows, rows), 0), iota((rows, rows), 1)
    frame = 2 * (to % P2) + (to // P2) % 2
    turn = (at == frame * pixels + to // T).astype(BF)
    values = in_ref[:, pl.ds(first, pixels), :].reshape(rows, C)
    return dot(turn, values).reshape(pixels, 2, P2, C)


def activate(values, norm):
    u = (values - norm[0][None]) * norm[1][None]
    return (u / (1.0 + jnp.exp(-u))).astype(BF).astype(F32)


def time_terms(act):
    pixels = act.shape[0]
    even, odd = act[:, 0], act[:, 1]
    start = iota((pixels * P2, C), 0) % P2 == 0

    def before(v):
        v = pltpu.roll(v.reshape(pixels * P2, C), 1, 0)
        return jnp.where(start, 0.0, v).reshape(pixels, P2, C)

    even1, odd1 = before(even), before(odd)
    return even1 - even, odd1 + even, even - odd1, odd1 - odd


def conv_kernel(
    place_ref, in_ref, rim_ref, core_ref, band_ref, plain_ref, sums_ref, mid_ref, stats_ref,
    terms, ends, sides, latent, sums, norm, held, sems,
):
    def arrival(j, l, b, source):
        slot = 4 * (j % 3) + l
        return pltpu.make_async_copy(source, held.at[slot, b], sems.at[slot, b])

    def start(j):
        for l in range(4):
            for b in range(3):
                summed = (j, l) in COMBINED
                source = sums_ref.at[COMBINED[j, l], b] if summed else plain_ref.at[2 * j // 3, b, 2 * l // 3]
                arrival(j, l, b, source).start()

    for j in range(3):
        start(j)

    block, z = place_ref[0], place_ref[1]
    half, column = block % 2, block // 2
    above = (half == 0) & (z == 0)
    below = (half == 1) & (z == 3)
    tail = rim_ref[:, 16:RIM, :].reshape(T * 8, C)
    row = iota((T, T * 8), 0)
    row = 2 * (row % P2) + row // P2
    pieces = dot((iota((T, T * 8), 1) == row * 8 + 4).astype(BF), tail).astype(BF)
    for i in range(2):
        norm[i] = sum(
            dot(pieces[:, 128 * k : 128 * k + 128], from_groups(32 * i, BF)) for k in range(3)
        ).reshape(2, P2, C)

    for first, pixels in ((0, 16), (16, 8)):
        act = activate(turned(rim_ref, first, pixels), norm)
        p = iota(act.shape, 0) + first
        out = (column == 0) & ((p < 8) | (p == 16) | (p == 18))
        out = out | (column == 15) & ((p >= 8) & (p < 16) | (p == 17) | (p == 19))
        out = out | above & ((p == 16) | (p == 17)) | below & (p >= 18)
        for j, v in enumerate(time_terms(jnp.where(out, 0.0, act))):
            for q in range(min(pixels, 20 - first)):
                p = first + q
                if p < 16:
                    sides[j, p // S, p % S] = v[q]
                else:
                    ends[j, (p - 16) // 2, (p % 2) * (W - 1)] = v[q]
    core, band = turned(core_ref, 0, S), turned(band_ref, 0, S)
    for i, values in enumerate((jnp.where(half == 0, band, core), jnp.where(half == 0, core, band))):
        act = jnp.where(below if i else above, 0.0, activate(values, norm))
        for j, v in enumerate(time_terms(act)):
            ends[j, i, 1 : S + 1] = v

    def columns(v, j, at):
        v = v.reshape(2, W // 2, 2, P2, C)
        even, odd = v[:, :, 0], v[:, :, 1]
        before, after, odd_before = even[:, :-1], even[:, 1:], odd[:, :-1]
        for l, u in enumerate((before - after, odd_before + after, after - odd_before, odd_before - odd[:, 1:])):
            u = u.astype(BF)
            for i, r in enumerate(at):
                terms[j, l, r] = u[i]

    for j in range(4):
        columns(ends[j], j, (0, W - 1))

    def two_rows(k, _):
        first = pl.multiple_of(16 * k, 16)
        values = turned(in_ref, first, 16)
        latent[pl.ds(first, 16)] = values.astype(BF)
        for j, v in enumerate(time_terms(activate(values, norm))):
            left, right = (sides[j, i, pl.ds(2 * k, 2)][:, None] for i in range(2))
            columns(jnp.concatenate([left, v.reshape(2, S, P2, C), right], axis=1), j, (2 * k + 1, 2 * k + 2))
        return 0

    lax.fori_loop(0, S // 2, two_rows, 0)

    def term(j, _):
        @pl.when(j == 1)
        def _():
            start(3)

        for l in range(4):
            for b in range(3):
                arrival(j, l, b, sums_ref.at[0, 0]).wait()
        for q in range(2):
            m = []
            for l in range(4):
                rows = [terms[j, l, 4 * q + b : 4 * q + b + 4].reshape(16 * P2, C) for b in range(3)]
                weight = held[4 * (j % 3) + l].reshape(3 * C, C)
                m.append(dot(jnp.concatenate(rows, axis=1), weight).reshape(4, 4, P2, C))
            sums[j, 0, 4 * q : 4 * q + 4] = m[0] + m[1] + m[2]
            sums[j, 1, 4 * q : 4 * q + 4] = m[1] - m[2] - m[3]
        return 0

    lax.fori_loop(0, 4, term, 0)

    def pixel(r, c):
        m = [sums[j, c % 2, r, c // 2] for j in range(4)]
        m = m[0] + m[1] + m[2], m[1] - m[2] - m[3]
        return [(latent[S * r + c, i].astype(F32) + m[i]).astype(BF) for i in range(2)]

    pivot = [v.astype(F32) for v in pixel(0, 0)]

    def finish_row(r, totals):
        for c in range(S):
            for i, v in enumerate(pixel(r, c)):
                mid_ref[S * r + c, i] = v
                off = v.astype(F32) - pivot[i]
                totals[i] = totals[i] + off
                totals[2 + i] = totals[2 + i] + off * off
        return totals

    totals = lax.fori_loop(0, S, finish_row, [jnp.zeros((P2, C), F32)] * 4)
    off = [v * (1.0 / (S * S)) for v in totals[:2]]
    mean = [pivot[i] + off[i] for i in range(2)]
    total = [totals[2 + i] - S * S * off[i] * off[i] for i in range(2)]
    stats = sum(group_stats(mean[i], total[i], float(S * S), 64 * i) for i in range(2))
    stats_ref[...] = jnp.broadcast_to(stats[None], stats_ref.shape)


def merge_kernel(parts_ref, out_ref):
    whole = merge(parts_ref[...], float(S * S * 16))
    out_ref[...] = jnp.broadcast_to(whole[None], out_ref.shape)


def attend_kernel(mid_ref, parts_ref, score_ref, update_ref, out_ref, norm):
    @pl.when(pl.program_id(0) == 0)
    def _():
        count = float(S * S * 16 * 8)
        whole = finish(merge(parts_ref[...], count), 16.0 * count)
        for i in range(2):
            for j in range(2):
                norm[i, j] = dot(whole, from_groups(64 * j + 32 * i), HI)

    pixels = mid_ref.shape[0]
    rows = pixels * T
    mid = mid_ref[...].astype(F32)
    flat = ((mid - norm[0][None]) * norm[1][None]).astype(BF).reshape(rows, C)
    query = dot(flat, score_ref[...]).astype(BF)
    n = 256
    row, column = iota((n, n), 0), iota((n, n), 1)
    frame = lambda v: 2 * (v % P2) + (v // P2) % 2
    seen = (row // T == column // T) & (frame(row) >= frame(column))
    parts = []
    for i in range(rows // n):
        at = slice(i * n, i * n + n)
        scores = lax.dot_general(query[at], flat[at], (((1,), (1,)), ((), ())), preferred_element_type=F32)
        scores = jnp.where(seen, scores, -1e30)
        weights = jnp.exp(scores - jnp.max(scores, axis=1, keepdims=True))
        weights = (weights * (1.0 / jnp.sum(weights, axis=1, keepdims=True))).astype(BF)
        parts.append(dot(weights, flat[at]).astype(BF))
    update = dot(jnp.concatenate(parts, axis=0), update_ref[...])
    out = (mid.reshape(rows, C) + update).astype(BF)
    to = iota((n, n), 0)
    frame = to // S
    turn = (iota((n, n), 1) == (to % S) * T + (frame % 2) * P2 + frame // 2).astype(BF)
    for i in range(rows // (2 * n)):
        pair = [dot(turn, out[(2 * i + k) * n : (2 * i + k + 1) * n]).reshape(T, S, C) for k in range(2)]
        out_ref[:, 16 * i : 16 * i + 16, :] = jnp.concatenate(pair, axis=1).astype(BF)


def local(latents, conv_weight, w_query, w_key, w_value, w_out):
    x = latents.reshape(16, 128, C)
    vmem = pl.BlockSpec(memory_space=pltpu.VMEM)
    smem = pl.BlockSpec(memory_space=pltpu.SMEM)
    whole = lambda *shape: pl.BlockSpec(shape, lambda i: (0,) * len(shape))
    exchange = lambda v, axes: lax.all_to_all(v[None], axes, split_axis=1, concat_axis=0, tiled=True)[:, 0]
    place = jnp.stack([lax.axis_index(TM), lax.axis_index("rows")]).astype(jnp.int32)

    inner = pl.pallas_call(
        inner_kernel,
        grid=(2,),
        out_shape=jax.ShapeDtypeStruct((32, S * S, C), BF),
        in_specs=[pl.BlockSpec((16, 64, C), lambda i: (0, i, 0))],
        out_specs=pl.BlockSpec((16, S * S, C), lambda i: (i, 0, 0)),
        compiler_params=params(),
        cost_estimate=cost(2**20, 4 * 2**20),
        name="inner",
    )(x)
    patch = exchange(inner, TM)
    row = jax.ShapeDtypeStruct((144, C), BF)
    up, down, own = pl.pallas_call(
        latent_stats_kernel,
        out_shape=(row, row, jax.ShapeDtypeStruct((16, C), BF)),
        in_specs=[vmem],
        out_specs=(vmem,) * 3,
        compiler_params=params(),
        cost_estimate=cost(2048 * C * 4, 2048 * C * 2),
        name="latent_stats",
    )(x.reshape(2048, C))
    def combine(first, count, conv_weight, *before):
        return pl.pallas_call(
            weights_kernel,
            grid=(count,),
            out_shape=jax.ShapeDtypeStruct((12, 3, C, C), BF),
            in_specs=[pl.BlockSpec((3, 1, 3, 256, C), lambda i: (0, (i + first) // 2, 0, (i + first) % 2, 0))]
            + [pl.BlockSpec(memory_space=pl.ANY)] * len(before),
            out_specs=pl.BlockSpec((12, 1, 256, C), lambda i: (0, (i + first) // 2, (i + first) % 2, 0)),
            input_output_aliases={1: 0} if before else {},
            compiler_params=params(),
            cost_estimate=cost(count * C * C, count * 11 * C * C * 2),
            name="weights",
        )(conv_weight, *before)

    around = lambda v, by: lax.ppermute(v, "rows", [(i, (i + by) % 4) for i in range(4)])
    up, down, far = around(up, 1), around(down, 3), around(own, 2)
    _, early = lax.optimization_barrier((own, conv_weight))
    rim_x, weights = lax.optimization_barrier((x, combine(0, 1, early)))
    rim = pl.pallas_call(
        rim_kernel,
        out_shape=jax.ShapeDtypeStruct((16, 2, RIM, C), BF),
        in_specs=[vmem] * 5,
        out_specs=vmem,
        scratch_shapes=[pltpu.VMEM((18, 128, 128), F32), pltpu.VMEM((2, 16 * RIM, 128), F32)],
        compiler_params=params(),
        cost_estimate=cost(2**22, 4 * 2**20),
        name="rim",
    )(rim_x, up, down, own, far).reshape(32, RIM, C)

    rim, early = lax.optimization_barrier((rim, conv_weight))
    rim, patch, weights = lax.optimization_barrier((rim, patch, combine(1, 2, early, weights)))
    rim = exchange(rim, TM)
    first = lax.axis_index("core") == 0
    row = lambda at: lax.dynamic_slice_in_dim(patch, at, S, axis=1)
    core, band = row(jnp.where(first, S * S - S, 0)), row(jnp.where(first, 0, S * S - S))
    core, band, late = lax.optimization_barrier((core, band, conv_weight))
    core = lax.ppermute(core, "core", [(0, 1), (1, 0)])
    pairs = [(4 + i, i + 1) for i in range(3)] + [(i + 1, 4 + i) for i in range(3)]
    band = lax.ppermute(band, ("core", "rows"), pairs)
    weights = combine(3, 3, late, weights)
    score = (dot(w_query, w_key.T) * (1.0 / C**0.5)).astype(BF)
    update = dot(w_value, w_out).astype(BF)

    mid, stats = pl.pallas_call(
        conv_kernel,
        out_shape=(jax.ShapeDtypeStruct((S * S, 2, P2, C), BF), jax.ShapeDtypeStruct((8, P2, 128), F32)),
        in_specs=[smem] + [vmem] * 4 + [pl.BlockSpec(memory_space=pl.ANY)] * 2,
        out_specs=(vmem, vmem),
        scratch_shapes=[
            pltpu.VMEM((4, 4, W, S // 2, P2, C), BF),
            pltpu.VMEM((4, 2, W, P2, C), F32),
            pltpu.VMEM((4, 2, S, P2, C), F32),
            pltpu.VMEM((S * S, 2, P2, C), BF),
            pltpu.VMEM((4, 2, S, S // 2, P2, C), F32),
            pltpu.VMEM((2, 2, P2, C), F32),
            pltpu.VMEM((12, 3, C, C), BF),
            pltpu.SemaphoreType.DMA((12, 3)),
        ],
        compiler_params=params(),
        cost_estimate=cost(512 * 48 * C * C * 2, 28 * 2**20),
        name="conv",
    )(place, patch, rim, core, band, conv_weight, weights)
    parts = pl.pallas_call(
        merge_kernel,
        out_shape=jax.ShapeDtypeStruct((16, P2, 128), F32),
        in_specs=[vmem],
        out_specs=vmem,
        compiler_params=params(),
        name="merge",
    )(exchange(stats, ("core", "rows")))
    parts = exchange(parts, ("x", "y"))
    pixels = 32
    out = pl.pallas_call(
        attend_kernel,
        grid=(S * S // pixels,),
        out_shape=jax.ShapeDtypeStruct((T, S * S, C), BF),
        in_specs=[pl.BlockSpec((pixels, 2, P2, C), lambda i: (i, 0, 0, 0)), whole(16, P2, 128)] + [whole(C, C)] * 2,
        out_specs=pl.BlockSpec((T, pixels, C), lambda i: (0, i, 0)),
        scratch_shapes=[pltpu.VMEM((2, 2, P2, C), F32)],
        compiler_params=params(),
        cost_estimate=cost(2048 * C * C * 2 * 4, 8 * 2**20),
        name="attend",
    )(mid, parts, score, update)
    back = exchange(out, TM)
    back = back.reshape(16, 2, S, S, C).transpose(1, 2, 0, 3, 4)
    return back.reshape(1, 16, 128, C)


def solution(mesh):
    mesh = Mesh(mesh.devices.reshape(4, 4, 2, 4), TM + ("rows",))
    in_specs = (P(TM, "rows", None, None), P(), P(), P(), P(), P())
    out_specs = P(TM, "rows", None, None)
    return jax.shard_map(local, mesh=mesh, in_specs=in_specs, out_specs=out_specs, check_vma=False)
```

```python
import jax
import jax.numpy as jnp
from jax import lax
from jax.experimental import pallas as pl
from jax.experimental.pallas import tpu as pltpu
from jax.sharding import Mesh
from jax.sharding import PartitionSpec as P

GROUPS = 32
T = 32
C = 512
S = 8
W = S + 2
P2 = T // 2
RIM = 24
TM = ("x", "y", "core")
EPS = 1e-6
COMBINED = {(i // 4, i % 4): n for n, i in enumerate(i for i in range(16) if i not in (0, 3, 12, 15))}
BF, F32 = jnp.bfloat16, jnp.float32


def iota(shape, dim):
    return lax.broadcasted_iota(jnp.int32, shape, dim)


def dot(a, b):
    return jnp.dot(a, b, preferred_element_type=F32)


def params():
    return pltpu.CompilerParams(vmem_limit_bytes=56 * 2**20)


def cost(flops, nbytes):
    return pl.CostEstimate(flops=flops, bytes_accessed=nbytes, transcendentals=0)


def bf16_terms(v):
    high = v.astype(BF).astype(F32)
    middle = (v - high).astype(BF).astype(F32)
    return [high, middle, v - high - middle]


def pick_dot(v, ones):
    n = v.shape[0]
    parts = dot(jnp.concatenate(bf16_terms(v), axis=0).astype(BF), ones)
    return parts[:n] + parts[n : 2 * n] + parts[2 * n :]


def to_groups(lane):
    return (iota((C, 128), 0) // 16 + lane == iota((C, 128), 1)).astype(BF)


def from_groups(lane):
    return (iota((128, C), 1) // 16 + lane == iota((128, C), 0)).astype(BF)


def group_stats(mean, m2, count):
    group_mean = pick_dot(mean, to_groups(0)) * (1.0 / 16.0)
    off = mean - pick_dot(group_mean, from_groups(0))
    return group_mean + pick_dot(m2 + count * (off * off), to_groups(32))


def merge(parts, count):
    n = parts.shape[0]
    total = jnp.sum(parts, axis=0)
    mean = total * (1.0 / n)
    off = parts - mean[None]
    between = pltpu.roll(jnp.sum(off * off, axis=0), 32, 1)
    is_mean = (iota(total.shape, 1) // 32) % 2 == 0
    return jnp.where(is_mean, mean, total + count * between)


def split_terms(v):
    return jnp.concatenate(bf16_terms(v) + [jnp.zeros_like(v)], axis=1)


def join_terms(v):
    return sum(v[:, 128 * i : 128 * i + 128].astype(F32) for i in range(3))


def latent_stats_kernel(x_ref, up_ref, down_ref, out_ref):
    n = x_ref.shape[0]
    step = 64

    pivot = x_ref[:16, :].astype(F32)[:1]

    def add(i, totals):
        rows = x_ref[pl.ds(pl.multiple_of(i * step, step), step), :].astype(F32) - pivot
        rows = rows.reshape(step // 8, 8, C)
        return totals[0] + jnp.sum(rows, axis=0), totals[1] + jnp.sum(rows * rows, axis=0)

    zero = jnp.zeros((8, C), F32)
    totals = lax.fori_loop(0, n // step, add, (zero, zero))
    off = jnp.sum(totals[0], axis=0, keepdims=True) * (1.0 / n)
    mean = pivot + off
    m2 = jnp.sum(totals[1], axis=0, keepdims=True) - n * off * off
    wide = lambda v: jnp.broadcast_to(v, (8, C))
    row = split_terms(group_stats(wide(mean), wide(m2), float(n)))
    row = jnp.concatenate([row, jnp.zeros_like(row)], axis=0).astype(BF)
    out_ref[...] = row
    up_ref[:128, :] = x_ref[n - 128 :, :]
    down_ref[:128, :] = x_ref[:128, :]
    up_ref[128:, :] = row
    down_ref[128:, :] = row


def finish(whole, count):
    is_mean = (iota(whole.shape, 1) // 32) % 2 == 0
    return jnp.where(is_mean, whole, lax.rsqrt(whole * (1.0 / count) + EPS))


def inner_kernel(x_ref, out_ref):
    x = x_ref[...].astype(F32).reshape(2, S, 8, S, C)
    for k in range(8):
        for half in range(2):
            out_ref[2 * k + half] = x[half, :, k].reshape(S * S, C).astype(BF)


def rim_kernel(x_ref, up_ref, down_ref, own_ref, far_ref, out_ref, wide, rim):
    n = 2048.0 * 16.0
    parts = [own_ref[...], far_ref[...], up_ref[128:, :], down_ref[128:, :]]
    whole = merge(jnp.stack([join_terms(v)[:8] for v in parts]), n)
    stats = split_terms(jnp.where(iota(whole.shape, 1) < 64, finish(whole, 4.0 * n), 0.0))[:1]
    rim[...] = jnp.zeros_like(rim)

    def lanes(q):
        at = slice(128 * q, 128 * q + 128)
        wide[0] = up_ref[:128, at].astype(F32)
        wide[17] = down_ref[:128, at].astype(F32)
        wide[1:17] = x_ref[:, :, at].astype(F32)
        for half in range(2):
            rim[half, pl.ds(20, 16, stride=RIM), :] = jnp.broadcast_to(stats[:, at], (16, 128))
            for r in range(W):
                left, right = (16, 17) if r == 0 else (18, 19) if r == W - 1 else (r - 1, S + r - 1)
                rim[half, pl.ds(RIM + left, 15, stride=RIM), :] = wide[S * half + r, pl.ds(S - 1, 15, stride=S), :]
                rim[half, pl.ds(right, 15, stride=RIM), :] = wide[S * half + r, pl.ds(S, 15, stride=S), :]
            out_ref[:, half, :, at] = rim[half].reshape(16, RIM, 128).astype(BF)

    for q in range(4):
        lanes(q)


def weights_kernel(w_ref, *refs):
    out_ref = refs[-1]

    def products(g):
        ends = (g[0] + g[2]) * 0.5
        middle = g[1] * 0.5
        return g[0], ends + middle, ends - middle, g[2]

    def rows(i, _):
        at = pl.ds(pl.multiple_of(16 * i, 16), 16)
        for q in range(4):
            lanes = slice(128 * q, 128 * q + 128)
            columns = [products([w_ref[a, 0, e, at, lanes].astype(F32) for e in range(3)]) for a in range(3)]
            for l in range(4):
                for j, v in enumerate(products([columns[a][l] for a in range(3)])):
                    if (j, l) in COMBINED:
                        out_ref[COMBINED[j, l], 0, at, lanes] = v.astype(BF)
        return 0

    lax.fori_loop(0, 16, rows, 0)


def turned(in_ref, first, pixels):
    rows = pixels * T
    to, at = iota((rows, rows), 0), iota((rows, rows), 1)
    frame = 2 * (to % P2) + (to // P2) % 2
    turn = (at == frame * pixels + to // T).astype(BF)
    values = in_ref[:, pl.ds(first, pixels), :].reshape(rows, C)
    return dot(turn, values).reshape(pixels, 2, P2, C)


def activate(values, norm):
    u = (values - norm[0][None]) * norm[1][None]
    return (u / (1.0 + jnp.exp(-u))).astype(BF).astype(F32)


def time_terms(act):
    pixels = act.shape[0]
    even, odd = act[:, 0], act[:, 1]
    start = iota((pixels * P2, C), 0) % P2 == 0

    def before(v):
        v = pltpu.roll(v.reshape(pixels * P2, C), 1, 0)
        return jnp.where(start, 0.0, v).reshape(pixels, P2, C)

    even1, odd1 = before(even), before(odd)
    return even1 - even, odd1 + even, even - odd1, odd1 - odd


def conv_kernel(
    place_ref, in_ref, rim_ref, core_ref, band_ref, plain_ref, sums_ref, mid_ref, stats_ref,
    terms, ends, sides, latent, sums, norm, held, sems,
):
    def arrival(j, l, b, source):
        slot = 4 * (j % 3) + l
        return pltpu.make_async_copy(source, held.at[slot, b], sems.at[slot, b])

    def start(j):
        for l in range(4):
            for b in range(3):
                summed = (j, l) in COMBINED
                source = sums_ref.at[COMBINED[j, l], b] if summed else plain_ref.at[2 * j // 3, b, 2 * l // 3]
                arrival(j, l, b, source).start()

    for j in range(3):
        start(j)

    block, z = place_ref[0], place_ref[1]
    half, column = block % 2, block // 2
    above = (half == 0) & (z == 0)
    below = (half == 1) & (z == 3)
    tail = rim_ref[:, 16:RIM, :].reshape(T * 8, C)
    row = iota((T, T * 8), 0)
    row = 2 * (row % P2) + row // P2
    pieces = dot((iota((T, T * 8), 1) == row * 8 + 4).astype(BF), tail).astype(BF)
    for i in range(2):
        norm[i] = sum(
            dot(pieces[:, 128 * k : 128 * k + 128], from_groups(32 * i)) for k in range(3)
        ).reshape(2, P2, C)

    for first, pixels in ((0, 16), (16, 8)):
        act = activate(turned(rim_ref, first, pixels), norm)
        p = iota(act.shape, 0) + first
        out = (column == 0) & ((p < 8) | (p == 16) | (p == 18))
        out = out | (column == 15) & ((p >= 8) & (p < 16) | (p == 17) | (p == 19))
        out = out | above & ((p == 16) | (p == 17)) | below & (p >= 18)
        for j, v in enumerate(time_terms(jnp.where(out, 0.0, act))):
            for q in range(min(pixels, 20 - first)):
                p = first + q
                if p < 16:
                    sides[j, p // S, p % S] = v[q]
                else:
                    ends[j, (p - 16) // 2, (p % 2) * (W - 1)] = v[q]
    core, band = turned(core_ref, 0, S), turned(band_ref, 0, S)
    for i, values in enumerate((jnp.where(half == 0, band, core), jnp.where(half == 0, core, band))):
        act = jnp.where(below if i else above, 0.0, activate(values, norm))
        for j, v in enumerate(time_terms(act)):
            ends[j, i, 1 : S + 1] = v

    def columns(v, j, at):
        v = v.reshape(2, W // 2, 2, P2, C)
        even, odd = v[:, :, 0], v[:, :, 1]
        before, after, odd_before = even[:, :-1], even[:, 1:], odd[:, :-1]
        for l, u in enumerate((before - after, odd_before + after, after - odd_before, odd_before - odd[:, 1:])):
            u = u.astype(BF)
            for i, r in enumerate(at):
                terms[j, l, r] = u[i]

    for j in range(4):
        columns(ends[j], j, (0, W - 1))

    def two_rows(k, _):
        first = pl.multiple_of(16 * k, 16)
        values = turned(in_ref, first, 16)
        latent[pl.ds(first, 16)] = values.astype(BF)
        for j, v in enumerate(time_terms(activate(values, norm))):
            left, right = (sides[j, i, pl.ds(2 * k, 2)][:, None] for i in range(2))
            columns(jnp.concatenate([left, v.reshape(2, S, P2, C), right], axis=1), j, (2 * k + 1, 2 * k + 2))
        return 0

    lax.fori_loop(0, S // 2, two_rows, 0)

    def term(j, _):
        @pl.when(j == 1)
        def _():
            start(3)

        for l in range(4):
            for b in range(3):
                arrival(j, l, b, sums_ref.at[0, 0]).wait()
        for q in range(2):
            m = []
            for l in range(4):
                rows = [terms[j, l, 4 * q + b : 4 * q + b + 4].reshape(16 * P2, C) for b in range(3)]
                weight = held[4 * (j % 3) + l].reshape(3 * C, C)
                m.append(dot(jnp.concatenate(rows, axis=1), weight).reshape(4, 4, P2, C))
            sums[j, 0, 4 * q : 4 * q + 4] = m[0] + m[1] + m[2]
            sums[j, 1, 4 * q : 4 * q + 4] = m[1] - m[2] - m[3]
        return 0

    lax.fori_loop(0, 4, term, 0)

    def pixel(r, c):
        m = [sums[j, c % 2, r, c // 2] for j in range(4)]
        m = m[0] + m[1] + m[2], m[1] - m[2] - m[3]
        return [(latent[S * r + c, i].astype(F32) + m[i]).astype(BF) for i in range(2)]

    pivot = [v.astype(F32) for v in pixel(0, 0)]

    def finish_row(r, totals):
        for c in range(S):
            for i, v in enumerate(pixel(r, c)):
                mid_ref[S * r + c, i] = v
                off = v.astype(F32) - pivot[i]
                totals[i] = totals[i] + off
                totals[2 + i] = totals[2 + i] + off * off
        return totals

    totals = lax.fori_loop(0, S, finish_row, [jnp.zeros((P2, C), F32)] * 4)
    off = [v * (1.0 / (S * S)) for v in totals[:2]]
    mean = [pivot[i] + off[i] for i in range(2)]
    total = [totals[2 + i] - S * S * off[i] * off[i] for i in range(2)]
    stats = group_stats(jnp.concatenate(mean, axis=0), jnp.concatenate(total, axis=0), float(S * S))
    stats = stats[:P2] + pltpu.roll(stats[P2:], 64, 1)
    stats_ref[...] = jnp.broadcast_to(stats[None], stats_ref.shape)


def merge_kernel(parts_ref, out_ref):
    whole = merge(parts_ref[...], float(S * S * 16))
    out_ref[...] = jnp.broadcast_to(whole[None], out_ref.shape)


def attend_kernel(mid_ref, parts_ref, score_ref, update_ref, out_ref, norm):
    @pl.when(pl.program_id(0) == 0)
    def _():
        count = float(S * S * 16 * 8)
        whole = finish(merge(parts_ref[...], count), 16.0 * count)
        both = jnp.concatenate([whole, pltpu.roll(whole, 64, 1)], axis=0)
        for i in range(2):
            norm[i] = pick_dot(both, from_groups(32 * i)).reshape(2, P2, C)

    pixels = mid_ref.shape[0]
    rows = pixels * T
    mid = mid_ref[...].astype(F32)
    flat = ((mid - norm[0][None]) * norm[1][None]).astype(BF).reshape(rows, C)
    query = dot(flat, score_ref[...]).astype(BF)
    n = 256
    row, column = iota((n, n), 0), iota((n, n), 1)
    frame = lambda v: 2 * (v % P2) + (v // P2) % 2
    seen = (row // T == column // T) & (frame(row) >= frame(column))
    parts = []
    for i in range(rows // n):
        at = slice(i * n, i * n + n)
        scores = lax.dot_general(query[at], flat[at], (((1,), (1,)), ((), ())), preferred_element_type=F32)
        scores = jnp.where(seen, scores, -1e30)
        weights = jnp.exp(scores - jnp.max(scores, axis=1, keepdims=True))
        weights = (weights * (1.0 / jnp.sum(weights, axis=1, keepdims=True))).astype(BF)
        parts.append(dot(weights, flat[at]).astype(BF))
    update = dot(jnp.concatenate(parts, axis=0), update_ref[...])
    out = (mid.reshape(rows, C) + update).astype(BF)
    to = iota((n, n), 0)
    frame = to // S
    turn = (iota((n, n), 1) == (to % S) * T + (frame % 2) * P2 + frame // 2).astype(BF)
    for i in range(rows // (2 * n)):
        pair = [dot(turn, out[(2 * i + k) * n : (2 * i + k + 1) * n]).reshape(T, S, C) for k in range(2)]
        out_ref[:, 16 * i : 16 * i + 16, :] = jnp.concatenate(pair, axis=1).astype(BF)


def local(latents, conv_weight, w_query, w_key, w_value, w_out):
    x = latents.reshape(16, 128, C)
    vmem = pl.BlockSpec(memory_space=pltpu.VMEM)
    smem = pl.BlockSpec(memory_space=pltpu.SMEM)
    whole = lambda *shape: pl.BlockSpec(shape, lambda i: (0,) * len(shape))
    exchange = lambda v, axes: lax.all_to_all(v[None], axes, split_axis=1, concat_axis=0, tiled=True)[:, 0]
    place = jnp.stack([lax.axis_index(TM), lax.axis_index("rows")]).astype(jnp.int32)

    inner = pl.pallas_call(
        inner_kernel,
        grid=(2,),
        out_shape=jax.ShapeDtypeStruct((32, S * S, C), BF),
        in_specs=[pl.BlockSpec((16, 64, C), lambda i: (0, i, 0))],
        out_specs=pl.BlockSpec((16, S * S, C), lambda i: (i, 0, 0)),
        compiler_params=params(),
        cost_estimate=cost(2**20, 4 * 2**20),
        name="inner",
    )(x)
    patch = exchange(inner, TM)
    row = jax.ShapeDtypeStruct((144, C), BF)
    up, down, own = pl.pallas_call(
        latent_stats_kernel,
        out_shape=(row, row, jax.ShapeDtypeStruct((16, C), BF)),
        in_specs=[vmem],
        out_specs=(vmem,) * 3,
        compiler_params=params(),
        cost_estimate=cost(2048 * C * 4, 2048 * C * 2),
        name="latent_stats",
    )(x.reshape(2048, C))
    def combine(first, count, conv_weight, *before):
        return pl.pallas_call(
            weights_kernel,
            grid=(count,),
            out_shape=jax.ShapeDtypeStruct((12, 3, C, C), BF),
            in_specs=[pl.BlockSpec((3, 1, 3, 256, C), lambda i: (0, (i + first) // 2, 0, (i + first) % 2, 0))]
            + [pl.BlockSpec(memory_space=pl.ANY)] * len(before),
            out_specs=pl.BlockSpec((12, 1, 256, C), lambda i: (0, (i + first) // 2, (i + first) % 2, 0)),
            input_output_aliases={1: 0} if before else {},
            compiler_params=params(),
            cost_estimate=cost(count * C * C, count * 11 * C * C * 2),
            name="weights",
        )(conv_weight, *before)

    around = lambda v, by: lax.ppermute(v, "rows", [(i, (i + by) % 4) for i in range(4)])
    up, down, far = around(up, 1), around(down, 3), around(own, 2)
    _, early = lax.optimization_barrier((own, conv_weight))
    rim_x, weights = lax.optimization_barrier((x, combine(0, 1, early)))
    rim = pl.pallas_call(
        rim_kernel,
        out_shape=jax.ShapeDtypeStruct((16, 2, RIM, C), BF),
        in_specs=[vmem] * 5,
        out_specs=vmem,
        scratch_shapes=[pltpu.VMEM((18, 128, 128), F32), pltpu.VMEM((2, 16 * RIM, 128), F32)],
        compiler_params=params(),
        cost_estimate=cost(2**22, 4 * 2**20),
        name="rim",
    )(rim_x, up, down, own, far).reshape(32, RIM, C)

    rim, early = lax.optimization_barrier((rim, conv_weight))
    rim, patch, weights = lax.optimization_barrier((rim, patch, combine(1, 3, early, weights)))
    rim = exchange(rim, TM)
    first = lax.axis_index("core") == 0
    row = lambda at: lax.dynamic_slice_in_dim(patch, at, S, axis=1)
    core, band = row(jnp.where(first, S * S - S, 0)), row(jnp.where(first, 0, S * S - S))
    core, band, late = lax.optimization_barrier((core, band, conv_weight))
    core = lax.ppermute(core, "core", [(0, 1), (1, 0)])
    pairs = [(4 + i, i + 1) for i in range(3)] + [(i + 1, 4 + i) for i in range(3)]
    band = lax.ppermute(band, ("core", "rows"), pairs)
    weights = combine(4, 2, late, weights)
    score = (dot(w_query, w_key.T) * (1.0 / C**0.5)).astype(BF)
    update = dot(w_value, w_out).astype(BF)

    mid, stats = pl.pallas_call(
        conv_kernel,
        out_shape=(jax.ShapeDtypeStruct((S * S, 2, P2, C), BF), jax.ShapeDtypeStruct((8, P2, 128), F32)),
        in_specs=[smem] + [vmem] * 4 + [pl.BlockSpec(memory_space=pl.ANY)] * 2,
        out_specs=(vmem, vmem),
        scratch_shapes=[
            pltpu.VMEM((4, 4, W, S // 2, P2, C), BF),
            pltpu.VMEM((4, 2, W, P2, C), F32),
            pltpu.VMEM((4, 2, S, P2, C), F32),
            pltpu.VMEM((S * S, 2, P2, C), BF),
            pltpu.VMEM((4, 2, S, S // 2, P2, C), F32),
            pltpu.VMEM((2, 2, P2, C), F32),
            pltpu.VMEM((12, 3, C, C), BF),
            pltpu.SemaphoreType.DMA((12, 3)),
        ],
        compiler_params=params(),
        cost_estimate=cost(512 * 48 * C * C * 2, 28 * 2**20),
        name="conv",
    )(place, patch, rim, core, band, conv_weight, weights)
    parts = pl.pallas_call(
        merge_kernel,
        out_shape=jax.ShapeDtypeStruct((16, P2, 128), F32),
        in_specs=[vmem],
        out_specs=vmem,
        compiler_params=params(),
        name="merge",
    )(exchange(stats, ("core", "rows")))
    parts = exchange(parts, ("x", "y"))
    pixels = 32
    out = pl.pallas_call(
        attend_kernel,
        grid=(S * S // pixels,),
        out_shape=jax.ShapeDtypeStruct((T, S * S, C), BF),
        in_specs=[pl.BlockSpec((pixels, 2, P2, C), lambda i: (i, 0, 0, 0)), whole(16, P2, 128)] + [whole(C, C)] * 2,
        out_specs=pl.BlockSpec((T, pixels, C), lambda i: (0, i, 0)),
        scratch_shapes=[pltpu.VMEM((2, 2, P2, C), F32)],
        compiler_params=params(),
        cost_estimate=cost(2048 * C * C * 2 * 4, 8 * 2**20),
        name="attend",
    )(mid, parts, score, update)
    back = exchange(out, TM)
    back = back.reshape(16, 2, S, S, C).transpose(1, 2, 0, 3, 4)
    return back.reshape(1, 16, 128, C)


def solution(mesh):
    mesh = Mesh(mesh.devices.reshape(4, 4, 2, 4), TM + ("rows",))
    in_specs = (P(TM, "rows", None, None), P(), P(), P(), P(), P())
    out_specs = P(TM, "rows", None, None)
    return jax.shard_map(local, mesh=mesh, in_specs=in_specs, out_specs=out_specs, check_vma=False)
```

```python
import jax
import jax.numpy as jnp
from jax import lax
from jax.experimental import pallas as pl
from jax.experimental.pallas import tpu as pltpu
from jax.sharding import Mesh
from jax.sharding import PartitionSpec as P

GROUPS = 32
T = 32
C = 512
S = 8
W = S + 2
P2 = T // 2
RIM = 24
TM = ("x", "y", "core")
EPS = 1e-6
COMBINED = {(i // 4, i % 4): n for n, i in enumerate(i for i in range(16) if i not in (0, 3, 12, 15))}
BF, F32 = jnp.bfloat16, jnp.float32


def iota(shape, dim):
    return lax.broadcasted_iota(jnp.int32, shape, dim)


def dot(a, b):
    return jnp.dot(a, b, preferred_element_type=F32)


def params():
    return pltpu.CompilerParams(vmem_limit_bytes=56 * 2**20)


def cost(flops, nbytes):
    return pl.CostEstimate(flops=flops, bytes_accessed=nbytes, transcendentals=0)


def bf16_terms(v):
    high = v.astype(BF).astype(F32)
    middle = (v - high).astype(BF).astype(F32)
    return [high, middle, v - high - middle]


def pick_dot(v, ones):
    n = v.shape[0]
    parts = dot(jnp.concatenate(bf16_terms(v), axis=0).astype(BF), ones)
    return parts[:n] + parts[n : 2 * n] + parts[2 * n :]


def to_groups(lane):
    return ((iota((C, 128), 0) >> 4) + lane == iota((C, 128), 1)).astype(BF)


def from_groups(lane):
    return ((iota((128, C), 1) >> 4) + lane == iota((128, C), 0)).astype(BF)


def group_stats(mean, m2, count):
    group_mean = pick_dot(mean, to_groups(0)) * (1.0 / 16.0)
    off = mean - pick_dot(group_mean, from_groups(0))
    return group_mean + pick_dot(m2 + count * (off * off), to_groups(32))


def merge(parts, count):
    n = parts.shape[0]
    total = jnp.sum(parts, axis=0)
    mean = total * (1.0 / n)
    off = parts - mean[None]
    between = pltpu.roll(jnp.sum(off * off, axis=0), 32, 1)
    is_mean = (iota(total.shape, 1) & 32) == 0
    return jnp.where(is_mean, mean, total + count * between)


def split_terms(v):
    return jnp.concatenate(bf16_terms(v) + [jnp.zeros_like(v)], axis=1)


def join_terms(v):
    return sum(v[:, 128 * i : 128 * i + 128].astype(F32) for i in range(3))


def latent_stats_kernel(x_ref, up_ref, down_ref, out_ref):
    n = x_ref.shape[0]
    step = 64

    pivot = x_ref[:16, :].astype(F32)[:1]

    def add(i, totals):
        rows = x_ref[pl.ds(pl.multiple_of(i * step, step), step), :].astype(F32) - pivot
        rows = rows.reshape(step // 8, 8, C)
        return totals[0] + jnp.sum(rows, axis=0), totals[1] + jnp.sum(rows * rows, axis=0)

    zero = jnp.zeros((8, C), F32)
    totals = lax.fori_loop(0, n // step, add, (zero, zero))
    off = jnp.sum(totals[0], axis=0, keepdims=True) * (1.0 / n)
    mean = pivot + off
    m2 = jnp.sum(totals[1], axis=0, keepdims=True) - n * off * off
    wide = lambda v: jnp.broadcast_to(v, (8, C))
    row = split_terms(group_stats(wide(mean), wide(m2), float(n)))
    row = jnp.concatenate([row, jnp.zeros_like(row)], axis=0).astype(BF)
    out_ref[...] = row
    up_ref[:128, :] = x_ref[n - 128 :, :]
    down_ref[:128, :] = x_ref[:128, :]
    up_ref[128:, :] = row
    down_ref[128:, :] = row


def finish(whole, count):
    is_mean = (iota(whole.shape, 1) & 32) == 0
    return jnp.where(is_mean, whole, lax.rsqrt(whole * (1.0 / count) + EPS))


def inner_kernel(x_ref, out_ref):
    x = x_ref[...].astype(F32).reshape(2, S, 8, S, C)
    for k in range(8):
        for half in range(2):
            out_ref[2 * k + half] = x[half, :, k].reshape(S * S, C).astype(BF)


def rim_kernel(x_ref, up_ref, down_ref, own_ref, far_ref, out_ref, wide, rim):
    n = 2048.0 * 16.0
    parts = [own_ref[...], far_ref[...], up_ref[128:, :], down_ref[128:, :]]
    whole = merge(jnp.stack([join_terms(v)[:8] for v in parts]), n)
    stats = split_terms(jnp.where(iota(whole.shape, 1) < 64, finish(whole, 4.0 * n), 0.0))[:1]
    rim[...] = jnp.zeros_like(rim)

    def lanes(q):
        at = slice(128 * q, 128 * q + 128)
        wide[0] = up_ref[:128, at].astype(F32)
        wide[17] = down_ref[:128, at].astype(F32)
        wide[1:17] = x_ref[:, :, at].astype(F32)
        for half in range(2):
            rim[half, pl.ds(20, 16, stride=RIM), :] = jnp.broadcast_to(stats[:, at], (16, 128))
            for r in range(W):
                left, right = (16, 17) if r == 0 else (18, 19) if r == W - 1 else (r - 1, S + r - 1)
                rim[half, pl.ds(RIM + left, 15, stride=RIM), :] = wide[S * half + r, pl.ds(S - 1, 15, stride=S), :]
                rim[half, pl.ds(right, 15, stride=RIM), :] = wide[S * half + r, pl.ds(S, 15, stride=S), :]
            out_ref[:, half, :, at] = rim[half].reshape(16, RIM, 128).astype(BF)

    for q in range(4):
        lanes(q)


def weights_kernel(w_ref, *refs):
    out_ref = refs[-1]

    def products(g):
        ends = (g[0] + g[2]) * 0.5
        middle = g[1] * 0.5
        return g[0], ends + middle, ends - middle, g[2]

    def rows(i, _):
        at = pl.ds(pl.multiple_of(16 * i, 16), 16)
        for q in range(4):
            lanes = slice(128 * q, 128 * q + 128)
            columns = [products([w_ref[a, 0, e, at, lanes].astype(F32) for e in range(3)]) for a in range(3)]
            for l in range(4):
                for j, v in enumerate(products([columns[a][l] for a in range(3)])):
                    if (j, l) in COMBINED:
                        out_ref[COMBINED[j, l], 0, at, lanes] = v.astype(BF)
        return 0

    lax.fori_loop(0, 16, rows, 0)


def frame_of(v):
    return ((v & (P2 - 1)) << 1) | ((v >> 4) & 1)


def turn_matrix(pixels):
    rows = pixels * T
    to = iota((rows, 1), 0)
    return (iota((rows, rows), 1) == frame_of(to) * pixels + (to >> 5)).astype(BF)


def turned(in_ref, first, pixels, turn):
    values = in_ref[:, pl.ds(first, pixels), :].reshape(pixels * T, C)
    return dot(turn, values).reshape(pixels, 2, P2, C)


def activate(values, norm):
    u = (values - norm[0][None]) * norm[1][None]
    return (u / (1.0 + jnp.exp(-u))).astype(BF).astype(F32)


def time_terms(act):
    pixels = act.shape[0]
    even, odd = act[:, 0], act[:, 1]
    start = (iota((pixels * P2, C), 0) & (P2 - 1)) == 0

    def before(v):
        v = pltpu.roll(v.reshape(pixels * P2, C), 1, 0)
        return jnp.where(start, 0.0, v).reshape(pixels, P2, C)

    even1, odd1 = before(even), before(odd)
    return even1 - even, odd1 + even, even - odd1, odd1 - odd


def conv_kernel(
    place_ref, in_ref, rim_ref, core_ref, band_ref, plain_ref, sums_ref, mid_ref, stats_ref,
    terms, ends, sides, latent, sums, norm, wide_turn, held, sems,
):
    def arrival(j, l, b, source):
        slot = 4 * (j % 3) + l
        return pltpu.make_async_copy(source, held.at[slot, b], sems.at[slot, b])

    def start(j):
        for l in range(4):
            for b in range(3):
                summed = (j, l) in COMBINED
                source = sums_ref.at[COMBINED[j, l], b] if summed else plain_ref.at[2 * j // 3, b, 2 * l // 3]
                arrival(j, l, b, source).start()

    for j in range(3):
        start(j)

    block, z = place_ref[0], place_ref[1]
    half, column = block % 2, block // 2
    above = (half == 0) & (z == 0)
    below = (half == 1) & (z == 3)
    tail = rim_ref[:, 16:RIM, :].reshape(T * 8, C)
    row = iota((T, T * 8), 0)
    row = 2 * (row % P2) + row // P2
    pieces = dot((iota((T, T * 8), 1) == row * 8 + 4).astype(BF), tail).astype(BF)
    for i in range(2):
        norm[i] = sum(
            dot(pieces[:, 128 * k : 128 * k + 128], from_groups(32 * i)) for k in range(3)
        ).reshape(2, P2, C)

    wide_turn[...] = turn_matrix(16)
    turn = turn_matrix(S)
    left, right = column == 0, column == 15
    for first, pixels in ((0, 16), (16, 8)):
        act = activate(turned(rim_ref, first, pixels, wide_turn[...] if pixels == 16 else turn), norm)
        for j, v in enumerate(time_terms(act)):
            for q in range(min(pixels, 20 - first)):
                p = first + q
                out = left if p < 8 or p in (16, 18) else right
                if p >= 16:
                    out = out | (above if p < 18 else below)
                value = v[q] * jnp.where(out, 0.0, 1.0)
                if p < 16:
                    sides[j, p // S, p % S] = value
                else:
                    ends[j, (p - 16) // 2, (p % 2) * (W - 1)] = value
    core, band = turned(core_ref, 0, S, turn), turned(band_ref, 0, S, turn)
    for i, values in enumerate((jnp.where(half == 0, band, core), jnp.where(half == 0, core, band))):
        act = jnp.where(below if i else above, 0.0, activate(values, norm))
        for j, v in enumerate(time_terms(act)):
            ends[j, i, 1 : S + 1] = v

    def columns(v, j, at):
        v = v.reshape(2, W // 2, 2, P2, C)
        even, odd = v[:, :, 0], v[:, :, 1]
        before, after, odd_before = even[:, :-1], even[:, 1:], odd[:, :-1]
        for l, u in enumerate((before - after, odd_before + after, after - odd_before, odd_before - odd[:, 1:])):
            u = u.astype(BF)
            for i, r in enumerate(at):
                terms[j, l, r] = u[i]

    for j in range(4):
        columns(ends[j], j, (0, W - 1))

    def two_rows(k, _):
        first = pl.multiple_of(16 * k, 16)
        values = turned(in_ref, first, 16, wide_turn[...])
        latent[pl.ds(first, 16)] = values.astype(BF)
        for j, v in enumerate(time_terms(activate(values, norm))):
            left, right = (sides[j, i, pl.ds(2 * k, 2)][:, None] for i in range(2))
            columns(jnp.concatenate([left, v.reshape(2, S, P2, C), right], axis=1), j, (2 * k + 1, 2 * k + 2))
        return 0

    lax.fori_loop(0, S // 2, two_rows, 0)

    def term(j, _):
        @pl.when(j == 1)
        def _():
            start(3)

        for l in range(4):
            for b in range(3):
                arrival(j, l, b, sums_ref.at[0, 0]).wait()
        for q in range(2):
            m = []
            for l in range(4):
                rows = [terms[j, l, 4 * q + b : 4 * q + b + 4].reshape(16 * P2, C) for b in range(3)]
                weight = held[4 * (j % 3) + l].reshape(3 * C, C)
                m.append(dot(jnp.concatenate(rows, axis=1), weight).reshape(4, 4, P2, C))
            sums[j, 0, 4 * q : 4 * q + 4] = m[0] + m[1] + m[2]
            sums[j, 1, 4 * q : 4 * q + 4] = m[1] - m[2] - m[3]
        return 0

    lax.fori_loop(0, 4, term, 0)

    def pixel(r, c):
        m = [sums[j, c % 2, r, c // 2] for j in range(4)]
        m = m[0] + m[1] + m[2], m[1] - m[2] - m[3]
        return [(latent[S * r + c, i].astype(F32) + m[i]).astype(BF) for i in range(2)]

    pivot = [v.astype(F32) for v in pixel(0, 0)]

    def finish_row(r, totals):
        for c in range(S):
            for i, v in enumerate(pixel(r, c)):
                mid_ref[S * r + c, i] = v
                off = v.astype(F32) - pivot[i]
                totals[i] = totals[i] + off
                totals[2 + i] = totals[2 + i] + off * off
        return totals

    totals = lax.fori_loop(0, S, finish_row, [jnp.zeros((P2, C), F32)] * 4)
    off = [v * (1.0 / (S * S)) for v in totals[:2]]
    mean = [pivot[i] + off[i] for i in range(2)]
    total = [totals[2 + i] - S * S * off[i] * off[i] for i in range(2)]
    stats = group_stats(jnp.concatenate(mean, axis=0), jnp.concatenate(total, axis=0), float(S * S))
    stats = stats[:P2] + pltpu.roll(stats[P2:], 64, 1)
    stats_ref[...] = jnp.broadcast_to(stats[None], stats_ref.shape)


def merge_kernel(parts_ref, out_ref):
    whole = merge(parts_ref[...], float(S * S * 16))
    out_ref[...] = jnp.broadcast_to(whole[None], out_ref.shape)


def attend_kernel(mid_ref, parts_ref, score_ref, update_ref, out_ref, norm):
    @pl.when(pl.program_id(0) == 0)
    def _():
        count = float(S * S * 16 * 8)
        whole = finish(merge(parts_ref[...], count), 16.0 * count)
        both = jnp.concatenate([whole, pltpu.roll(whole, 64, 1)], axis=0)
        for i in range(2):
            norm[i] = pick_dot(both, from_groups(32 * i)).reshape(2, P2, C)

    pixels = mid_ref.shape[0]
    rows = pixels * T
    mid = mid_ref[...].astype(F32)
    flat = ((mid - norm[0][None]) * norm[1][None]).astype(BF).reshape(rows, C)
    query = dot(flat, score_ref[...]).astype(BF)
    n = 256
    key = lambda v: ((v >> 5) << 6) + frame_of(v)
    apart = key(iota((n, 1), 0)) - key(iota((1, n), 1))
    seen = (apart >= 0) & (apart < T)
    parts = []
    for i in range(rows // n):
        at = slice(i * n, i * n + n)
        scores = lax.dot_general(query[at], flat[at], (((1,), (1,)), ((), ())), preferred_element_type=F32)
        scores = jnp.where(seen, scores, -1e30)
        weights = jnp.exp(scores - jnp.max(scores, axis=1, keepdims=True))
        weights = (weights * (1.0 / jnp.sum(weights, axis=1, keepdims=True))).astype(BF)
        parts.append(dot(weights, flat[at]).astype(BF))
    update = dot(jnp.concatenate(parts, axis=0), update_ref[...])
    out = (mid.reshape(rows, C) + update).astype(BF)
    to = iota((n, 1), 0)
    frame = to >> 3
    turn = (iota((n, n), 1) == (to & (S - 1)) * T + (frame & 1) * P2 + (frame >> 1)).astype(BF)
    for i in range(rows // (2 * n)):
        pair = [dot(turn, out[(2 * i + k) * n : (2 * i + k + 1) * n]).reshape(T, S, C) for k in range(2)]
        out_ref[:, 16 * i : 16 * i + 16, :] = jnp.concatenate(pair, axis=1).astype(BF)


def local(latents, conv_weight, w_query, w_key, w_value, w_out):
    x = latents.reshape(16, 128, C)
    vmem = pl.BlockSpec(memory_space=pltpu.VMEM)
    smem = pl.BlockSpec(memory_space=pltpu.SMEM)
    whole = lambda *shape: pl.BlockSpec(shape, lambda i: (0,) * len(shape))
    exchange = lambda v, axes: lax.all_to_all(v[None], axes, split_axis=1, concat_axis=0, tiled=True)[:, 0]
    place = jnp.stack([lax.axis_index(TM), lax.axis_index("rows")]).astype(jnp.int32)

    inner = pl.pallas_call(
        inner_kernel,
        grid=(2,),
        out_shape=jax.ShapeDtypeStruct((32, S * S, C), BF),
        in_specs=[pl.BlockSpec((16, 64, C), lambda i: (0, i, 0))],
        out_specs=pl.BlockSpec((16, S * S, C), lambda i: (i, 0, 0)),
        compiler_params=params(),
        cost_estimate=cost(2**20, 4 * 2**20),
        name="inner",
    )(x)
    patch = exchange(inner, TM)
    row = jax.ShapeDtypeStruct((144, C), BF)
    up, down, own = pl.pallas_call(
        latent_stats_kernel,
        out_shape=(row, row, jax.ShapeDtypeStruct((16, C), BF)),
        in_specs=[vmem],
        out_specs=(vmem,) * 3,
        compiler_params=params(),
        cost_estimate=cost(2048 * C * 4, 2048 * C * 2),
        name="latent_stats",
    )(x.reshape(2048, C))
    def combine(first, count, conv_weight, *before):
        return pl.pallas_call(
            weights_kernel,
            grid=(count,),
            out_shape=jax.ShapeDtypeStruct((12, 3, C, C), BF),
            in_specs=[pl.BlockSpec((3, 1, 3, 256, C), lambda i: (0, (i + first) // 2, 0, (i + first) % 2, 0))]
            + [pl.BlockSpec(memory_space=pl.ANY)] * len(before),
            out_specs=pl.BlockSpec((12, 1, 256, C), lambda i: (0, (i + first) // 2, (i + first) % 2, 0)),
            input_output_aliases={1: 0} if before else {},
            compiler_params=params(),
            cost_estimate=cost(count * C * C, count * 11 * C * C * 2),
            name="weights",
        )(conv_weight, *before)

    around = lambda v, by: lax.ppermute(v, "rows", [(i, (i + by) % 4) for i in range(4)])
    up, down, far = around(up, 1), around(down, 3), around(own, 2)
    _, early = lax.optimization_barrier((own, conv_weight))
    rim_x, weights = lax.optimization_barrier((x, combine(0, 1, early)))
    rim = pl.pallas_call(
        rim_kernel,
        out_shape=jax.ShapeDtypeStruct((16, 2, RIM, C), BF),
        in_specs=[vmem] * 5,
        out_specs=vmem,
        scratch_shapes=[pltpu.VMEM((18, 128, 128), F32), pltpu.VMEM((2, 16 * RIM, 128), F32)],
        compiler_params=params(),
        cost_estimate=cost(2**22, 4 * 2**20),
        name="rim",
    )(rim_x, up, down, own, far).reshape(32, RIM, C)

    rim, early = lax.optimization_barrier((rim, conv_weight))
    rim, patch, weights = lax.optimization_barrier((rim, patch, combine(1, 3, early, weights)))
    rim = exchange(rim, TM)
    first = lax.axis_index("core") == 0
    row = lambda at: lax.dynamic_slice_in_dim(patch, at, S, axis=1)
    core, band = row(jnp.where(first, S * S - S, 0)), row(jnp.where(first, 0, S * S - S))
    core, band, late = lax.optimization_barrier((core, band, conv_weight))
    core = lax.ppermute(core, "core", [(0, 1), (1, 0)])
    pairs = [(4 + i, i + 1) for i in range(3)] + [(i + 1, 4 + i) for i in range(3)]
    band = lax.ppermute(band, ("core", "rows"), pairs)
    weights = combine(4, 2, late, weights)
    score = (dot(w_query, w_key.T) * (1.0 / C**0.5)).astype(BF)
    update = dot(w_value, w_out).astype(BF)

    mid, stats = pl.pallas_call(
        conv_kernel,
        out_shape=(jax.ShapeDtypeStruct((S * S, 2, P2, C), BF), jax.ShapeDtypeStruct((8, P2, 128), F32)),
        in_specs=[smem] + [vmem] * 4 + [pl.BlockSpec(memory_space=pl.ANY)] * 2,
        out_specs=(vmem, vmem),
        scratch_shapes=[
            pltpu.VMEM((4, 4, W, S // 2, P2, C), BF),
            pltpu.VMEM((4, 2, W, P2, C), F32),
            pltpu.VMEM((4, 2, S, P2, C), F32),
            pltpu.VMEM((S * S, 2, P2, C), BF),
            pltpu.VMEM((4, 2, S, S // 2, P2, C), F32),
            pltpu.VMEM((2, 2, P2, C), F32),
            pltpu.VMEM((16 * T, 16 * T), BF),
            pltpu.VMEM((12, 3, C, C), BF),
            pltpu.SemaphoreType.DMA((12, 3)),
        ],
        compiler_params=params(),
        cost_estimate=cost(512 * 48 * C * C * 2, 28 * 2**20),
        name="conv",
    )(place, patch, rim, core, band, conv_weight, weights)
    parts = pl.pallas_call(
        merge_kernel,
        out_shape=jax.ShapeDtypeStruct((16, P2, 128), F32),
        in_specs=[vmem],
        out_specs=vmem,
        compiler_params=params(),
        name="merge",
    )(exchange(stats, ("core", "rows")))
    parts = exchange(parts, ("x", "y"))
    pixels = 32
    out = pl.pallas_call(
        attend_kernel,
        grid=(S * S // pixels,),
        out_shape=jax.ShapeDtypeStruct((T, S * S, C), BF),
        in_specs=[pl.BlockSpec((pixels, 2, P2, C), lambda i: (i, 0, 0, 0)), whole(16, P2, 128)] + [whole(C, C)] * 2,
        out_specs=pl.BlockSpec((T, pixels, C), lambda i: (0, i, 0)),
        scratch_shapes=[pltpu.VMEM((2, 2, P2, C), F32)],
        compiler_params=params(),
        cost_estimate=cost(2048 * C * C * 2 * 4, 8 * 2**20),
        name="attend",
    )(mid, parts, score, update)
    back = exchange(out, TM)
    back = back.reshape(16, 2, S, S, C).transpose(1, 2, 0, 3, 4)
    return back.reshape(1, 16, 128, C)


def solution(mesh):
    mesh = Mesh(mesh.devices.reshape(4, 4, 2, 4), TM + ("rows",))
    in_specs = (P(TM, "rows", None, None), P(), P(), P(), P(), P())
    out_specs = P(TM, "rows", None, None)
    return jax.shard_map(local, mesh=mesh, in_specs=in_specs, out_specs=out_specs, check_vma=False)
```

```python
import jax
import jax.numpy as jnp
from jax import lax
from jax.experimental import pallas as pl
from jax.experimental.pallas import tpu as pltpu
from jax.sharding import Mesh
from jax.sharding import PartitionSpec as P

GROUPS = 32
T = 32
C = 512
S = 8
W = S + 2
P2 = T // 2
RIM = 24
TM = ("x", "y", "core")
EPS = 1e-6
COMBINED = {(i // 4, i % 4): n for n, i in enumerate(i for i in range(16) if i not in (0, 3, 12, 15))}
BF, F32 = jnp.bfloat16, jnp.float32


def iota(shape, dim):
    return lax.broadcasted_iota(jnp.int32, shape, dim)


def dot(a, b):
    return jnp.dot(a, b, preferred_element_type=F32)


def params(mib):
    return pltpu.CompilerParams(vmem_limit_bytes=mib * 2**20)


def cost(flops, nbytes):
    return pl.CostEstimate(flops=flops, bytes_accessed=nbytes, transcendentals=0)


def bf16_terms(v):
    high = v.astype(BF).astype(F32)
    middle = (v - high).astype(BF).astype(F32)
    return [high, middle, v - high - middle]


def pick_dot(v, ones):
    n = v.shape[0]
    parts = dot(jnp.concatenate(bf16_terms(v), axis=0).astype(BF), ones)
    return parts[:n] + parts[n : 2 * n] + parts[2 * n :]


def to_groups(lane):
    return (iota((C, 128), 0) // 16 + lane == iota((C, 128), 1)).astype(BF)


def from_groups(lane):
    return (iota((128, C), 1) // 16 + lane == iota((128, C), 0)).astype(BF)


def group_stats(mean, m2, count):
    group_mean = pick_dot(mean, to_groups(0)) * (1.0 / 16.0)
    off = mean - pick_dot(group_mean, from_groups(0))
    return group_mean + pick_dot(m2 + count * (off * off), to_groups(32))


def merge(parts, count):
    n = parts.shape[0]
    total = jnp.sum(parts, axis=0)
    mean = total * (1.0 / n)
    off = parts - mean[None]
    between = pltpu.roll(jnp.sum(off * off, axis=0), 32, 1)
    is_mean = (iota(total.shape, 1) // 32) % 2 == 0
    return jnp.where(is_mean, mean, total + count * between)


def split_terms(v):
    return jnp.concatenate(bf16_terms(v) + [jnp.zeros_like(v)], axis=1)


def join_terms(v):
    return sum(v[:, 128 * i : 128 * i + 128].astype(F32) for i in range(3))


def latent_stats_kernel(x_ref, up_ref, down_ref, out_ref):
    n = x_ref.shape[0]
    step = 64

    pivot = x_ref[:16, :].astype(F32)[:1]

    def add(i, totals):
        rows = x_ref[pl.ds(pl.multiple_of(i * step, step), step), :].astype(F32) - pivot
        rows = rows.reshape(step // 8, 8, C)
        return totals[0] + jnp.sum(rows, axis=0), totals[1] + jnp.sum(rows * rows, axis=0)

    zero = jnp.zeros((8, C), F32)
    totals = lax.fori_loop(0, n // step, add, (zero, zero))
    off = jnp.sum(totals[0], axis=0, keepdims=True) * (1.0 / n)
    mean = pivot + off
    m2 = jnp.sum(totals[1], axis=0, keepdims=True) - n * off * off
    wide = lambda v: jnp.broadcast_to(v, (8, C))
    row = split_terms(group_stats(wide(mean), wide(m2), float(n)))
    row = jnp.concatenate([row, jnp.zeros_like(row)], axis=0).astype(BF)
    out_ref[...] = row
    up_ref[:128, :] = x_ref[n - 128 :, :]
    down_ref[:128, :] = x_ref[:128, :]
    up_ref[128:, :] = row
    down_ref[128:, :] = row


def finish(whole, count):
    is_mean = (iota(whole.shape, 1) // 32) % 2 == 0
    return jnp.where(is_mean, whole, lax.rsqrt(whole * (1.0 / count) + EPS))


def inner_kernel(x_ref, out_ref):
    x = x_ref[...].astype(F32).reshape(2, S, 8, S, C)
    for k in range(8):
        for half in range(2):
            out_ref[2 * k + half] = x[half, :, k].reshape(S * S, C).astype(BF)


def rim_kernel(x_ref, up_ref, down_ref, own_ref, far_ref, out_ref, wide, rim):
    n = 2048.0 * 16.0
    parts = [own_ref[...], far_ref[...], up_ref[128:, :], down_ref[128:, :]]
    whole = merge(jnp.stack([join_terms(v)[:8] for v in parts]), n)
    stats = split_terms(jnp.where(iota(whole.shape, 1) < 64, finish(whole, 4.0 * n), 0.0))[:1]
    rim[...] = jnp.zeros_like(rim)

    def lanes(q):
        at = slice(128 * q, 128 * q + 128)
        wide[0] = up_ref[:128, at].astype(F32)
        wide[17] = down_ref[:128, at].astype(F32)
        wide[1:17] = x_ref[:, :, at].astype(F32)
        for half in range(2):
            rim[half, pl.ds(20, 16, stride=RIM), :] = jnp.broadcast_to(stats[:, at], (16, 128))
            for r in range(W):
                left, right = (16, 17) if r == 0 else (18, 19) if r == W - 1 else (r - 1, S + r - 1)
                rim[half, pl.ds(RIM + left, 15, stride=RIM), :] = wide[S * half + r, pl.ds(S - 1, 15, stride=S), :]
                rim[half, pl.ds(right, 15, stride=RIM), :] = wide[S * half + r, pl.ds(S, 15, stride=S), :]
            out_ref[:, half, :, at] = rim[half].reshape(16, RIM, 128).astype(BF)

    for q in range(4):
        lanes(q)


def weights_kernel(w_ref, *refs):
    out_ref = refs[-1]

    def products(g):
        ends = (g[0] + g[2]) * 0.5
        middle = g[1] * 0.5
        return g[0], ends + middle, ends - middle, g[2]

    def rows(i, _):
        at = pl.ds(pl.multiple_of(16 * i, 16), 16)
        for q in range(4):
            lanes = slice(128 * q, 128 * q + 128)
            columns = [products([w_ref[a, 0, e, at, lanes].astype(F32) for e in range(3)]) for a in range(3)]
            for l in range(4):
                for j, v in enumerate(products([columns[a][l] for a in range(3)])):
                    if (j, l) in COMBINED:
                        out_ref[COMBINED[j, l], 0, at, lanes] = v.astype(BF)
        return 0

    lax.fori_loop(0, 16, rows, 0)


def turned(in_ref, first, pixels):
    rows = pixels * T
    to, at = iota((rows, rows), 0), iota((rows, rows), 1)
    frame = 2 * (to % P2) + (to // P2) % 2
    turn = (at == frame * pixels + to // T).astype(BF)
    values = in_ref[:, pl.ds(first, pixels), :].reshape(rows, C)
    return dot(turn, values).reshape(pixels, 2, P2, C)


def activate(values, norm):
    u = (values - norm[0][None]) * norm[1][None]
    return (u / (1.0 + jnp.exp(-u))).astype(BF).astype(F32)


def time_terms(act):
    pixels = act.shape[0]
    even, odd = act[:, 0], act[:, 1]
    start = iota((pixels * P2, C), 0) % P2 == 0

    def before(v):
        v = pltpu.roll(v.reshape(pixels * P2, C), 1, 0)
        return jnp.where(start, 0.0, v).reshape(pixels, P2, C)

    even1, odd1 = before(even), before(odd)
    return even1 - even, odd1 + even, even - odd1, odd1 - odd


def conv_kernel(
    place_ref, in_ref, rim_ref, core_ref, band_ref, plain_ref, sums_ref, mid_ref, stats_ref,
    terms, ends, sides, latent, sums, norm, held, sems,
):
    def arrival(j, l, b, source):
        slot = 4 * (j % 3) + l
        return pltpu.make_async_copy(source, held.at[slot, b], sems.at[slot, b])

    def start(j):
        for l in range(4):
            for b in range(3):
                summed = (j, l) in COMBINED
                source = sums_ref.at[COMBINED[j, l], b] if summed else plain_ref.at[2 * j // 3, b, 2 * l // 3]
                arrival(j, l, b, source).start()

    for j in range(3):
        start(j)

    block, z = place_ref[0], place_ref[1]
    half, column = block % 2, block // 2
    above = (half == 0) & (z == 0)
    below = (half == 1) & (z == 3)
    tail = rim_ref[:, 16:RIM, :].reshape(T * 8, C)
    row = iota((T, T * 8), 0)
    row = 2 * (row % P2) + row // P2
    pieces = dot((iota((T, T * 8), 1) == row * 8 + 4).astype(BF), tail).astype(BF)
    for i in range(2):
        norm[i] = sum(
            dot(pieces[:, 128 * k : 128 * k + 128], from_groups(32 * i)) for k in range(3)
        ).reshape(2, P2, C)

    for first, pixels in ((0, 16), (16, 8)):
        act = activate(turned(rim_ref, first, pixels), norm)
        p = iota(act.shape, 0) + first
        out = (column == 0) & ((p < 8) | (p == 16) | (p == 18))
        out = out | (column == 15) & ((p >= 8) & (p < 16) | (p == 17) | (p == 19))
        out = out | above & ((p == 16) | (p == 17)) | below & (p >= 18)
        for j, v in enumerate(time_terms(jnp.where(out, 0.0, act))):
            for q in range(min(pixels, 20 - first)):
                p = first + q
                if p < 16:
                    sides[j, p // S, p % S] = v[q]
                else:
                    ends[j, (p - 16) // 2, (p % 2) * (W - 1)] = v[q]
    core, band = turned(core_ref, 0, S), turned(band_ref, 0, S)
    for i, values in enumerate((jnp.where(half == 0, band, core), jnp.where(half == 0, core, band))):
        act = jnp.where(below if i else above, 0.0, activate(values, norm))
        for j, v in enumerate(time_terms(act)):
            ends[j, i, 1 : S + 1] = v

    def columns(v, j, at):
        v = v.reshape(2, W // 2, 2, P2, C)
        even, odd = v[:, :, 0], v[:, :, 1]
        before, after, odd_before = even[:, :-1], even[:, 1:], odd[:, :-1]
        for l, u in enumerate((before - after, odd_before + after, after - odd_before, odd_before - odd[:, 1:])):
            u = u.astype(BF)
            for i, r in enumerate(at):
                terms[j, l, r] = u[i]

    for j in range(4):
        columns(ends[j], j, (0, W - 1))

    def two_rows(k, _):
        first = pl.multiple_of(16 * k, 16)
        values = turned(in_ref, first, 16)
        latent[pl.ds(first, 16)] = values.astype(BF)
        for j, v in enumerate(time_terms(activate(values, norm))):
            left, right = (sides[j, i, pl.ds(2 * k, 2)][:, None] for i in range(2))
            columns(jnp.concatenate([left, v.reshape(2, S, P2, C), right], axis=1), j, (2 * k + 1, 2 * k + 2))
        return 0

    lax.fori_loop(0, S // 2, two_rows, 0)

    def term(j, _):
        @pl.when(j == 1)
        def _():
            start(3)

        for l in range(4):
            for b in range(3):
                arrival(j, l, b, sums_ref.at[0, 0]).wait()
        for q in range(2):
            m = []
            for l in range(4):
                rows = [terms[j, l, 4 * q + b : 4 * q + b + 4].reshape(16 * P2, C) for b in range(3)]
                weight = held[4 * (j % 3) + l].reshape(3 * C, C)
                m.append(dot(jnp.concatenate(rows, axis=1), weight).reshape(4, 4, P2, C))
            sums[j, 0, 4 * q : 4 * q + 4] = m[0] + m[1] + m[2]
            sums[j, 1, 4 * q : 4 * q + 4] = m[1] - m[2] - m[3]
        return 0

    lax.fori_loop(0, 4, term, 0)

    def pixel(r, c):
        m = [sums[j, c % 2, r, c // 2] for j in range(4)]
        m = m[0] + m[1] + m[2], m[1] - m[2] - m[3]
        return [(latent[S * r + c, i].astype(F32) + m[i]).astype(BF) for i in range(2)]

    pivot = [v.astype(F32) for v in pixel(0, 0)]

    def finish_row(r, totals):
        for c in range(S):
            for i, v in enumerate(pixel(r, c)):
                mid_ref[S * r + c, i] = v
                off = v.astype(F32) - pivot[i]
                totals[i] = totals[i] + off
                totals[2 + i] = totals[2 + i] + off * off
        return totals

    totals = lax.fori_loop(0, S, finish_row, [jnp.zeros((P2, C), F32)] * 4)
    off = [v * (1.0 / (S * S)) for v in totals[:2]]
    mean = [pivot[i] + off[i] for i in range(2)]
    total = [totals[2 + i] - S * S * off[i] * off[i] for i in range(2)]
    stats = group_stats(jnp.concatenate(mean, axis=0), jnp.concatenate(total, axis=0), float(S * S))
    stats = stats[:P2] + pltpu.roll(stats[P2:], 64, 1)
    stats_ref[...] = jnp.broadcast_to(stats[None], stats_ref.shape)


def merge_kernel(parts_ref, out_ref):
    whole = merge(parts_ref[...], float(S * S * 16))
    out_ref[...] = jnp.broadcast_to(whole[None], out_ref.shape)


def attend_kernel(mid_ref, parts_ref, score_ref, update_ref, out_ref, norm):
    @pl.when(pl.program_id(0) == 0)
    def _():
        count = float(S * S * 16 * 8)
        whole = finish(merge(parts_ref[...], count), 16.0 * count)
        both = jnp.concatenate([whole, pltpu.roll(whole, 64, 1)], axis=0)
        for i in range(2):
            norm[i] = pick_dot(both, from_groups(32 * i)).reshape(2, P2, C)

    pixels = mid_ref.shape[0]
    rows = pixels * T
    mid = mid_ref[...].astype(F32)
    flat = ((mid - norm[0][None]) * norm[1][None]).astype(BF).reshape(rows, C)
    query = dot(flat, score_ref[...]).astype(BF)
    n = 256
    row, column = iota((n, n), 0), iota((n, n), 1)
    frame = lambda v: 2 * (v % P2) + (v // P2) % 2
    seen = (row // T == column // T) & (frame(row) >= frame(column))
    parts = []
    for i in range(rows // n):
        at = slice(i * n, i * n + n)
        scores = lax.dot_general(query[at], flat[at], (((1,), (1,)), ((), ())), preferred_element_type=F32)
        scores = jnp.where(seen, scores, -1e30)
        weights = jnp.exp(scores - jnp.max(scores, axis=1, keepdims=True))
        weights = (weights * (1.0 / jnp.sum(weights, axis=1, keepdims=True))).astype(BF)
        parts.append(dot(weights, flat[at]).astype(BF))
    update = dot(jnp.concatenate(parts, axis=0), update_ref[...])
    out = (mid.reshape(rows, C) + update).astype(BF)
    to = iota((n, n), 0)
    frame = to // S
    turn = (iota((n, n), 1) == (to % S) * T + (frame % 2) * P2 + frame // 2).astype(BF)
    for i in range(rows // (2 * n)):
        pair = [dot(turn, out[(2 * i + k) * n : (2 * i + k + 1) * n]).reshape(T, S, C) for k in range(2)]
        out_ref[:, 16 * i : 16 * i + 16, :] = jnp.concatenate(pair, axis=1).astype(BF)


def local(latents, conv_weight, w_query, w_key, w_value, w_out):
    x = latents.reshape(16, 128, C)
    vmem = pl.BlockSpec(memory_space=pltpu.VMEM)
    smem = pl.BlockSpec(memory_space=pltpu.SMEM)
    whole = lambda *shape: pl.BlockSpec(shape, lambda i: (0,) * len(shape))
    exchange = lambda v, axes: lax.all_to_all(v[None], axes, split_axis=1, concat_axis=0, tiled=True)[:, 0]
    place = jnp.stack([lax.axis_index(TM), lax.axis_index("rows")]).astype(jnp.int32)

    inner = pl.pallas_call(
        inner_kernel,
        grid=(2,),
        out_shape=jax.ShapeDtypeStruct((32, S * S, C), BF),
        in_specs=[pl.BlockSpec((16, 64, C), lambda i: (0, i, 0))],
        out_specs=pl.BlockSpec((16, S * S, C), lambda i: (i, 0, 0)),
        compiler_params=params(16),
        cost_estimate=cost(2**20, 4 * 2**20),
        name="inner",
    )(x)
    patch = exchange(inner, TM)
    row = jax.ShapeDtypeStruct((144, C), BF)
    up, down, own = pl.pallas_call(
        latent_stats_kernel,
        out_shape=(row, row, jax.ShapeDtypeStruct((16, C), BF)),
        in_specs=[vmem],
        out_specs=(vmem,) * 3,
        compiler_params=params(12),
        cost_estimate=cost(2048 * C * 4, 2048 * C * 2),
        name="latent_stats",
    )(x.reshape(2048, C))
    def combine(first, count, conv_weight, *before):
        return pl.pallas_call(
            weights_kernel,
            grid=(count,),
            out_shape=jax.ShapeDtypeStruct((12, 3, C, C), BF),
            in_specs=[pl.BlockSpec((3, 1, 3, 256, C), lambda i: (0, (i + first) // 2, 0, (i + first) % 2, 0))]
            + [pl.BlockSpec(memory_space=pl.ANY)] * len(before),
            out_specs=pl.BlockSpec((12, 1, 256, C), lambda i: (0, (i + first) // 2, (i + first) % 2, 0)),
            input_output_aliases={1: 0} if before else {},
            compiler_params=params(24),
            cost_estimate=cost(count * C * C, count * 11 * C * C * 2),
            name="weights",
        )(conv_weight, *before)

    around = lambda v, by: lax.ppermute(v, "rows", [(i, (i + by) % 4) for i in range(4)])
    up, down, far = around(up, 1), around(down, 3), around(own, 2)
    _, early = lax.optimization_barrier((own, conv_weight))
    rim_x, weights = lax.optimization_barrier((x, combine(0, 1, early)))
    rim = pl.pallas_call(
        rim_kernel,
        out_shape=jax.ShapeDtypeStruct((16, 2, RIM, C), BF),
        in_specs=[vmem] * 5,
        out_specs=vmem,
        scratch_shapes=[pltpu.VMEM((18, 128, 128), F32), pltpu.VMEM((2, 16 * RIM, 128), F32)],
        compiler_params=params(16),
        cost_estimate=cost(2**22, 4 * 2**20),
        name="rim",
    )(rim_x, up, down, own, far).reshape(32, RIM, C)

    rim, early = lax.optimization_barrier((rim, conv_weight))
    rim, patch, weights = lax.optimization_barrier((rim, patch, combine(1, 3, early, weights)))
    rim = exchange(rim, TM)
    first = lax.axis_index("core") == 0
    row = lambda at: lax.dynamic_slice_in_dim(patch, at, S, axis=1)
    core, band = row(jnp.where(first, S * S - S, 0)), row(jnp.where(first, 0, S * S - S))
    core, band, late = lax.optimization_barrier((core, band, conv_weight))
    core = lax.ppermute(core, "core", [(0, 1), (1, 0)])
    pairs = [(4 + i, i + 1) for i in range(3)] + [(i + 1, 4 + i) for i in range(3)]
    band = lax.ppermute(band, ("core", "rows"), pairs)
    weights = combine(4, 2, late, weights)
    score = (dot(w_query, w_key.T) * (1.0 / C**0.5)).astype(BF)
    update = dot(w_value, w_out).astype(BF)

    mid, stats = pl.pallas_call(
        conv_kernel,
        out_shape=(jax.ShapeDtypeStruct((S * S, 2, P2, C), BF), jax.ShapeDtypeStruct((8, P2, 128), F32)),
        in_specs=[smem] + [vmem] * 4 + [pl.BlockSpec(memory_space=pl.ANY)] * 2,
        out_specs=(vmem, vmem),
        scratch_shapes=[
            pltpu.VMEM((4, 4, W, S // 2, P2, C), BF),
            pltpu.VMEM((4, 2, W, P2, C), F32),
            pltpu.VMEM((4, 2, S, P2, C), F32),
            pltpu.VMEM((S * S, 2, P2, C), BF),
            pltpu.VMEM((4, 2, S, S // 2, P2, C), F32),
            pltpu.VMEM((2, 2, P2, C), F32),
            pltpu.VMEM((12, 3, C, C), BF),
            pltpu.SemaphoreType.DMA((12, 3)),
        ],
        compiler_params=params(48),
        cost_estimate=cost(512 * 48 * C * C * 2, 28 * 2**20),
        name="conv",
    )(place, patch, rim, core, band, conv_weight, weights)
    parts = pl.pallas_call(
        merge_kernel,
        out_shape=jax.ShapeDtypeStruct((16, P2, 128), F32),
        in_specs=[vmem],
        out_specs=vmem,
        compiler_params=params(4),
        name="merge",
    )(exchange(stats, ("core", "rows")))
    parts = exchange(parts, ("x", "y"))
    pixels = 32
    out = pl.pallas_call(
        attend_kernel,
        grid=(S * S // pixels,),
        out_shape=jax.ShapeDtypeStruct((T, S * S, C), BF),
        in_specs=[pl.BlockSpec((pixels, 2, P2, C), lambda i: (i, 0, 0, 0)), whole(16, P2, 128)] + [whole(C, C)] * 2,
        out_specs=pl.BlockSpec((T, pixels, C), lambda i: (0, i, 0)),
        scratch_shapes=[pltpu.VMEM((2, 2, P2, C), F32)],
        compiler_params=params(24),
        cost_estimate=cost(2048 * C * C * 2 * 4, 8 * 2**20),
        name="attend",
    )(mid, parts, score, update)
    back = exchange(out, TM)
    back = back.reshape(16, 2, S, S, C).transpose(1, 2, 0, 3, 4)
    return back.reshape(1, 16, 128, C)


def solution(mesh):
    mesh = Mesh(mesh.devices.reshape(4, 4, 2, 4), TM + ("rows",))
    in_specs = (P(TM, "rows", None, None), P(), P(), P(), P(), P())
    out_specs = P(TM, "rows", None, None)
    return jax.shard_map(local, mesh=mesh, in_specs=in_specs, out_specs=out_specs, check_vma=False)
```

```python
import jax
import jax.numpy as jnp
from jax import lax
from jax.experimental import pallas as pl
from jax.experimental.pallas import tpu as pltpu
from jax.sharding import Mesh
from jax.sharding import PartitionSpec as P

GROUPS = 32
T = 32
C = 512
S = 8
W = S + 2
P2 = T // 2
RIM = 24
TM = ("x", "y", "core")
EPS = 1e-6
COMBINED = {(i // 4, i % 4): n for n, i in enumerate(i for i in range(16) if i not in (0, 3, 12, 15))}
BF, F32 = jnp.bfloat16, jnp.float32


def iota(shape, dim):
    return lax.broadcasted_iota(jnp.int32, shape, dim)


def dot(a, b):
    return jnp.dot(a, b, preferred_element_type=F32)


def params(mib):
    return pltpu.CompilerParams(vmem_limit_bytes=mib * 2**20)


def cost(flops, nbytes):
    return pl.CostEstimate(flops=flops, bytes_accessed=nbytes, transcendentals=0)


def bf16_terms(v):
    high = v.astype(BF).astype(F32)
    middle = (v - high).astype(BF).astype(F32)
    return [high, middle, v - high - middle]


def pick_dot(v, ones):
    n = v.shape[0]
    parts = dot(jnp.concatenate(bf16_terms(v), axis=0).astype(BF), ones)
    return parts[:n] + parts[n : 2 * n] + parts[2 * n :]


def to_groups(lane):
    return (iota((C, 128), 0) // 16 + lane == iota((C, 128), 1)).astype(BF)


def from_groups(lane):
    return (iota((128, C), 1) // 16 + lane == iota((128, C), 0)).astype(BF)


def group_stats(mean, m2, count):
    group_mean = pick_dot(mean, to_groups(0)) * (1.0 / 16.0)
    off = mean - pick_dot(group_mean, from_groups(0))
    return group_mean + pick_dot(m2 + count * (off * off), to_groups(32))


def merge(parts, count):
    n = parts.shape[0]
    total = jnp.sum(parts, axis=0)
    mean = total * (1.0 / n)
    off = parts - mean[None]
    between = pltpu.roll(jnp.sum(off * off, axis=0), 32, 1)
    is_mean = (iota(total.shape, 1) // 32) % 2 == 0
    return jnp.where(is_mean, mean, total + count * between)


def split_terms(v):
    return jnp.concatenate(bf16_terms(v) + [jnp.zeros_like(v)], axis=1)


def join_terms(v):
    return sum(v[:, 128 * i : 128 * i + 128].astype(F32) for i in range(3))


def latent_stats_kernel(x_ref, up_ref, down_ref, out_ref):
    n = x_ref.shape[0]
    step = 64

    pivot = x_ref[:16, :].astype(F32)[:1]

    def add(i, totals):
        rows = x_ref[pl.ds(pl.multiple_of(i * step, step), step), :].astype(F32) - pivot
        rows = rows.reshape(step // 8, 8, C)
        return totals[0] + jnp.sum(rows, axis=0), totals[1] + jnp.sum(rows * rows, axis=0)

    zero = jnp.zeros((8, C), F32)
    totals = lax.fori_loop(0, n // step, add, (zero, zero))
    off = jnp.sum(totals[0], axis=0, keepdims=True) * (1.0 / n)
    mean = pivot + off
    m2 = jnp.sum(totals[1], axis=0, keepdims=True) - n * off * off
    wide = lambda v: jnp.broadcast_to(v, (8, C))
    row = split_terms(group_stats(wide(mean), wide(m2), float(n)))
    row = jnp.concatenate([row, jnp.zeros_like(row)], axis=0).astype(BF)
    out_ref[...] = row
    up_ref[:128, :] = x_ref[n - 128 :, :]
    down_ref[:128, :] = x_ref[:128, :]
    up_ref[128:, :] = row
    down_ref[128:, :] = row


def finish(whole, count):
    is_mean = (iota(whole.shape, 1) // 32) % 2 == 0
    return jnp.where(is_mean, whole, lax.rsqrt(whole * (1.0 / count) + EPS))


def inner_kernel(x_ref, out_ref):
    x = x_ref[...].astype(F32).reshape(2, S, 8, S, C)
    for k in range(8):
        for half in range(2):
            out_ref[2 * k + half] = x[half, :, k].reshape(S * S, C).astype(BF)


def rim_kernel(x_ref, up_ref, down_ref, own_ref, far_ref, out_ref, wide, rim):
    n = 2048.0 * 16.0
    parts = [own_ref[...], far_ref[...], up_ref[128:, :], down_ref[128:, :]]
    whole = merge(jnp.stack([join_terms(v)[:8] for v in parts]), n)
    stats = split_terms(jnp.where(iota(whole.shape, 1) < 64, finish(whole, 4.0 * n), 0.0))[:1]
    rim[...] = jnp.zeros_like(rim)

    def lanes(q):
        at = slice(128 * q, 128 * q + 128)
        wide[0] = up_ref[:128, at].astype(F32)
        wide[17] = down_ref[:128, at].astype(F32)
        wide[1:17] = x_ref[:, :, at].astype(F32)
        for half in range(2):
            rim[half, pl.ds(20, 16, stride=RIM), :] = jnp.broadcast_to(stats[:, at], (16, 128))
            for r in range(W):
                left, right = (16, 17) if r == 0 else (18, 19) if r == W - 1 else (r - 1, S + r - 1)
                rim[half, pl.ds(RIM + left, 15, stride=RIM), :] = wide[S * half + r, pl.ds(S - 1, 15, stride=S), :]
                rim[half, pl.ds(right, 15, stride=RIM), :] = wide[S * half + r, pl.ds(S, 15, stride=S), :]
            out_ref[:, half, :, at] = rim[half].reshape(16, RIM, 128).astype(BF)

    for q in range(4):
        lanes(q)


def weights_kernel(w_ref, *refs):
    out_ref = refs[-1]

    def products(g):
        ends = (g[0] + g[2]) * 0.5
        middle = g[1] * 0.5
        return g[0], ends + middle, ends - middle, g[2]

    def rows(i, _):
        at = pl.ds(pl.multiple_of(16 * i, 16), 16)
        for q in range(4):
            lanes = slice(128 * q, 128 * q + 128)
            columns = [products([w_ref[a, 0, e, at, lanes].astype(F32) for e in range(3)]) for a in range(3)]
            for l in range(4):
                for j, v in enumerate(products([columns[a][l] for a in range(3)])):
                    if (j, l) in COMBINED:
                        out_ref[COMBINED[j, l], 0, at, lanes] = v.astype(BF)
        return 0

    lax.fori_loop(0, 16, rows, 0)


def turned(in_ref, first, pixels):
    rows = pixels * T
    to, at = iota((rows, rows), 0), iota((rows, rows), 1)
    frame = 2 * (to % P2) + (to // P2) % 2
    turn = (at == frame * pixels + to // T).astype(BF)
    values = in_ref[:, pl.ds(first, pixels), :].reshape(rows, C)
    return dot(turn, values).reshape(pixels, 2, P2, C)


def activate(values, norm):
    u = (values - norm[0][None]) * norm[1][None]
    return (u / (1.0 + jnp.exp(-u))).astype(BF).astype(F32)


def time_terms(act):
    pixels = act.shape[0]
    even, odd = act[:, 0], act[:, 1]
    start = iota((pixels * P2, C), 0) % P2 == 0

    def before(v):
        v = pltpu.roll(v.reshape(pixels * P2, C), 1, 0)
        return jnp.where(start, 0.0, v).reshape(pixels, P2, C)

    even1, odd1 = before(even), before(odd)
    return even1 - even, odd1 + even, even - odd1, odd1 - odd


def conv_kernel(
    place_ref, in_ref, rim_ref, core_ref, band_ref, plain_ref, sums_ref, mid_ref, stats_ref,
    terms, ends, sides, latent, sums, norm, held, sems,
):
    def arrival(j, l, b, source):
        slot = 4 * (j % 3) + l
        return pltpu.make_async_copy(source, held.at[slot, b], sems.at[slot, b])

    def start(j):
        for l in range(4):
            for b in range(3):
                summed = (j, l) in COMBINED
                source = sums_ref.at[COMBINED[j, l], b] if summed else plain_ref.at[2 * j // 3, b, 2 * l // 3]
                arrival(j, l, b, source).start()

    for j in range(3):
        start(j)

    block, z = place_ref[0], place_ref[1]
    half, column = block % 2, block // 2
    above = (half == 0) & (z == 0)
    below = (half == 1) & (z == 3)
    tail = rim_ref[:, 16:RIM, :].reshape(T * 8, C)
    row = iota((T, T * 8), 0)
    row = 2 * (row % P2) + row // P2
    pieces = dot((iota((T, T * 8), 1) == row * 8 + 4).astype(BF), tail).astype(BF)
    for i in range(2):
        norm[i] = sum(
            dot(pieces[:, 128 * k : 128 * k + 128], from_groups(32 * i)) for k in range(3)
        ).reshape(2, P2, C)

    for first, pixels in ((0, 16), (16, 8)):
        act = activate(turned(rim_ref, first, pixels), norm)
        p = iota(act.shape, 0) + first
        out = (column == 0) & ((p < 8) | (p == 16) | (p == 18))
        out = out | (column == 15) & ((p >= 8) & (p < 16) | (p == 17) | (p == 19))
        out = out | above & ((p == 16) | (p == 17)) | below & (p >= 18)
        for j, v in enumerate(time_terms(jnp.where(out, 0.0, act))):
            for q in range(min(pixels, 20 - first)):
                p = first + q
                if p < 16:
                    sides[j, p // S, p % S] = v[q]
                else:
                    ends[j, (p - 16) // 2, (p % 2) * (W - 1)] = v[q]
    core, band = turned(core_ref, 0, S), turned(band_ref, 0, S)
    for i, values in enumerate((jnp.where(half == 0, band, core), jnp.where(half == 0, core, band))):
        act = jnp.where(below if i else above, 0.0, activate(values, norm))
        for j, v in enumerate(time_terms(act)):
            ends[j, i, 1 : S + 1] = v

    def columns(v, j, at):
        v = v.reshape(2, W // 2, 2, P2, C)
        even, odd = v[:, :, 0], v[:, :, 1]
        before, after, odd_before = even[:, :-1], even[:, 1:], odd[:, :-1]
        for l, u in enumerate((before - after, odd_before + after, after - odd_before, odd_before - odd[:, 1:])):
            u = u.astype(BF)
            for i, r in enumerate(at):
                terms[j, l, r] = u[i]

    for j in range(4):
        columns(ends[j], j, (0, W - 1))

    def two_rows(k, _):
        first = pl.multiple_of(16 * k, 16)
        values = turned(in_ref, first, 16)
        latent[pl.ds(first, 16)] = values.astype(BF)
        for j, v in enumerate(time_terms(activate(values, norm))):
            left, right = (sides[j, i, pl.ds(2 * k, 2)][:, None] for i in range(2))
            columns(jnp.concatenate([left, v.reshape(2, S, P2, C), right], axis=1), j, (2 * k + 1, 2 * k + 2))
        return 0

    lax.fori_loop(0, S // 2, two_rows, 0)

    def term(j, _):
        @pl.when(j == 1)
        def _():
            start(3)

        for l in range(4):
            for b in range(3):
                arrival(j, l, b, sums_ref.at[0, 0]).wait()
        for q in range(2):
            m = []
            for l in range(4):
                rows = [terms[j, l, 4 * q + b : 4 * q + b + 4].reshape(16 * P2, C) for b in range(3)]
                weight = held[4 * (j % 3) + l].reshape(3 * C, C)
                m.append(dot(jnp.concatenate(rows, axis=1), weight).reshape(4, 4, P2, C))
            sums[j, 0, 4 * q : 4 * q + 4] = m[0] + m[1] + m[2]
            sums[j, 1, 4 * q : 4 * q + 4] = m[1] - m[2] - m[3]
        return 0

    lax.fori_loop(0, 4, term, 0)

    def pixel(r, c):
        m = [sums[j, c % 2, r, c // 2] for j in range(4)]
        m = m[0] + m[1] + m[2], m[1] - m[2] - m[3]
        return [(latent[S * r + c, i].astype(F32) + m[i]).astype(BF) for i in range(2)]

    pivot = [v.astype(F32) for v in pixel(0, 0)]

    def finish_row(r, totals):
        for c in range(S):
            for i, v in enumerate(pixel(r, c)):
                mid_ref[S * r + c, i] = v
                off = v.astype(F32) - pivot[i]
                totals[i] = totals[i] + off
                totals[2 + i] = totals[2 + i] + off * off
        return totals

    totals = lax.fori_loop(0, S, finish_row, [jnp.zeros((P2, C), F32)] * 4)
    off = [v * (1.0 / (S * S)) for v in totals[:2]]
    mean = [pivot[i] + off[i] for i in range(2)]
    total = [totals[2 + i] - S * S * off[i] * off[i] for i in range(2)]
    stats = group_stats(jnp.concatenate(mean, axis=0), jnp.concatenate(total, axis=0), float(S * S))
    stats = stats[:P2] + pltpu.roll(stats[P2:], 64, 1)
    stats_ref[...] = jnp.broadcast_to(stats[None], stats_ref.shape)


def merge_kernel(parts_ref, out_ref):
    whole = merge(parts_ref[...], float(S * S * 16))
    out_ref[...] = jnp.broadcast_to(whole[None], out_ref.shape)


def attend_kernel(mid_ref, parts_ref, score_ref, update_ref, out_ref, norm):
    @pl.when(pl.program_id(0) == 0)
    def _():
        count = float(S * S * 16 * 8)
        whole = finish(merge(parts_ref[...], count), 16.0 * count)
        both = jnp.concatenate([whole, pltpu.roll(whole, 64, 1)], axis=0)
        for i in range(2):
            norm[i] = pick_dot(both, from_groups(32 * i)).reshape(2, P2, C)

    pixels = mid_ref.shape[0]
    rows = pixels * T
    mid = mid_ref[...].astype(F32)
    flat = ((mid - norm[0][None]) * norm[1][None]).astype(BF).reshape(rows, C)
    query = dot(flat, score_ref[...]).astype(BF)
    n = 256
    row, column = iota((n, n), 0), iota((n, n), 1)
    frame = lambda v: 2 * (v % P2) + (v // P2) % 2
    seen = (row // T == column // T) & (frame(row) >= frame(column))
    parts = []
    for i in range(rows // n):
        at = slice(i * n, i * n + n)
        scores = lax.dot_general(query[at], flat[at], (((1,), (1,)), ((), ())), preferred_element_type=F32)
        scores = jnp.where(seen, scores, -1e30)
        weights = jnp.exp(scores - jnp.max(scores, axis=1, keepdims=True))
        weights = (weights * (1.0 / jnp.sum(weights, axis=1, keepdims=True))).astype(BF)
        parts.append(dot(weights, flat[at]).astype(BF))
    update = dot(jnp.concatenate(parts, axis=0), update_ref[...])
    out = (mid.reshape(rows, C) + update).astype(BF)
    to = iota((n, n), 0)
    frame = to // S
    turn = (iota((n, n), 1) == (to % S) * T + (frame % 2) * P2 + frame // 2).astype(BF)
    for i in range(rows // (2 * n)):
        pair = [dot(turn, out[(2 * i + k) * n : (2 * i + k + 1) * n]).reshape(T, S, C) for k in range(2)]
        out_ref[:, 16 * i : 16 * i + 16, :] = jnp.concatenate(pair, axis=1).astype(BF)


def local(latents, conv_weight, w_query, w_key, w_value, w_out):
    x = latents.reshape(16, 128, C)
    vmem = pl.BlockSpec(memory_space=pltpu.VMEM)
    smem = pl.BlockSpec(memory_space=pltpu.SMEM)
    whole = lambda *shape: pl.BlockSpec(shape, lambda i: (0,) * len(shape))
    exchange = lambda v, axes: lax.all_to_all(v[None], axes, split_axis=1, concat_axis=0, tiled=True)[:, 0]
    place = jnp.stack([lax.axis_index(TM), lax.axis_index("rows")]).astype(jnp.int32)

    inner = pl.pallas_call(
        inner_kernel,
        grid=(2,),
        out_shape=jax.ShapeDtypeStruct((32, S * S, C), BF),
        in_specs=[pl.BlockSpec((16, 64, C), lambda i: (0, i, 0))],
        out_specs=pl.BlockSpec((16, S * S, C), lambda i: (i, 0, 0)),
        compiler_params=params(56),
        cost_estimate=cost(2**20, 4 * 2**20),
        name="inner",
    )(x)
    patch = exchange(inner, TM)
    row = jax.ShapeDtypeStruct((144, C), BF)
    up, down, own = pl.pallas_call(
        latent_stats_kernel,
        out_shape=(row, row, jax.ShapeDtypeStruct((16, C), BF)),
        in_specs=[vmem],
        out_specs=(vmem,) * 3,
        compiler_params=params(12),
        cost_estimate=cost(2048 * C * 4, 2048 * C * 2),
        name="latent_stats",
    )(x.reshape(2048, C))
    def combine(first, count, conv_weight, *before):
        return pl.pallas_call(
            weights_kernel,
            grid=(count,),
            out_shape=jax.ShapeDtypeStruct((12, 3, C, C), BF),
            in_specs=[pl.BlockSpec((3, 1, 3, 256, C), lambda i: (0, (i + first) // 2, 0, (i + first) % 2, 0))]
            + [pl.BlockSpec(memory_space=pl.ANY)] * len(before),
            out_specs=pl.BlockSpec((12, 1, 256, C), lambda i: (0, (i + first) // 2, (i + first) % 2, 0)),
            input_output_aliases={1: 0} if before else {},
            compiler_params=params(56),
            cost_estimate=cost(count * C * C, count * 11 * C * C * 2),
            name="weights",
        )(conv_weight, *before)

    around = lambda v, by: lax.ppermute(v, "rows", [(i, (i + by) % 4) for i in range(4)])
    up, down, far = around(up, 1), around(down, 3), around(own, 2)
    _, early = lax.optimization_barrier((own, conv_weight))
    rim_x, weights = lax.optimization_barrier((x, combine(0, 1, early)))
    rim = pl.pallas_call(
        rim_kernel,
        out_shape=jax.ShapeDtypeStruct((16, 2, RIM, C), BF),
        in_specs=[vmem] * 5,
        out_specs=vmem,
        scratch_shapes=[pltpu.VMEM((18, 128, 128), F32), pltpu.VMEM((2, 16 * RIM, 128), F32)],
        compiler_params=params(16),
        cost_estimate=cost(2**22, 4 * 2**20),
        name="rim",
    )(rim_x, up, down, own, far).reshape(32, RIM, C)

    rim, early = lax.optimization_barrier((rim, conv_weight))
    rim, patch, weights = lax.optimization_barrier((rim, patch, combine(1, 3, early, weights)))
    rim = exchange(rim, TM)
    first = lax.axis_index("core") == 0
    row = lambda at: lax.dynamic_slice_in_dim(patch, at, S, axis=1)
    core, band = row(jnp.where(first, S * S - S, 0)), row(jnp.where(first, 0, S * S - S))
    core, band, late = lax.optimization_barrier((core, band, conv_weight))
    core = lax.ppermute(core, "core", [(0, 1), (1, 0)])
    pairs = [(4 + i, i + 1) for i in range(3)] + [(i + 1, 4 + i) for i in range(3)]
    band = lax.ppermute(band, ("core", "rows"), pairs)
    weights = combine(4, 2, late, weights)
    score = (dot(w_query, w_key.T) * (1.0 / C**0.5)).astype(BF)
    update = dot(w_value, w_out).astype(BF)

    mid, stats = pl.pallas_call(
        conv_kernel,
        out_shape=(jax.ShapeDtypeStruct((S * S, 2, P2, C), BF), jax.ShapeDtypeStruct((8, P2, 128), F32)),
        in_specs=[smem] + [vmem] * 4 + [pl.BlockSpec(memory_space=pl.ANY)] * 2,
        out_specs=(vmem, vmem),
        scratch_shapes=[
            pltpu.VMEM((4, 4, W, S // 2, P2, C), BF),
            pltpu.VMEM((4, 2, W, P2, C), F32),
            pltpu.VMEM((4, 2, S, P2, C), F32),
            pltpu.VMEM((S * S, 2, P2, C), BF),
            pltpu.VMEM((4, 2, S, S // 2, P2, C), F32),
            pltpu.VMEM((2, 2, P2, C), F32),
            pltpu.VMEM((12, 3, C, C), BF),
            pltpu.SemaphoreType.DMA((12, 3)),
        ],
        compiler_params=params(56),
        cost_estimate=cost(512 * 48 * C * C * 2, 28 * 2**20),
        name="conv",
    )(place, patch, rim, core, band, conv_weight, weights)
    parts = pl.pallas_call(
        merge_kernel,
        out_shape=jax.ShapeDtypeStruct((16, P2, 128), F32),
        in_specs=[vmem],
        out_specs=vmem,
        compiler_params=params(4),
        name="merge",
    )(exchange(stats, ("core", "rows")))
    parts = exchange(parts, ("x", "y"))
    pixels = 32
    out = pl.pallas_call(
        attend_kernel,
        grid=(S * S // pixels,),
        out_shape=jax.ShapeDtypeStruct((T, S * S, C), BF),
        in_specs=[pl.BlockSpec((pixels, 2, P2, C), lambda i: (i, 0, 0, 0)), whole(16, P2, 128)] + [whole(C, C)] * 2,
        out_specs=pl.BlockSpec((T, pixels, C), lambda i: (0, i, 0)),
        scratch_shapes=[pltpu.VMEM((2, 2, P2, C), F32)],
        compiler_params=params(24),
        cost_estimate=cost(2048 * C * C * 2 * 4, 8 * 2**20),
        name="attend",
    )(mid, parts, score, update)
    back = exchange(out, TM)
    back = back.reshape(16, 2, S, S, C).transpose(1, 2, 0, 3, 4)
    return back.reshape(1, 16, 128, C)


def solution(mesh):
    mesh = Mesh(mesh.devices.reshape(4, 4, 2, 4), TM + ("rows",))
    in_specs = (P(TM, "rows", None, None), P(), P(), P(), P(), P())
    out_specs = P(TM, "rows", None, None)
    return jax.shard_map(local, mesh=mesh, in_specs=in_specs, out_specs=out_specs, check_vma=False)
```

```python
import jax
import jax.numpy as jnp
from jax import lax
from jax.experimental import pallas as pl
from jax.experimental.pallas import tpu as pltpu
from jax.sharding import Mesh
from jax.sharding import PartitionSpec as P

GROUPS = 32
T = 32
C = 512
S = 8
W = S + 2
P2 = T // 2
RIM = 24
TM = ("x", "y", "core")
EPS = 1e-6
COMBINED = {(i // 4, i % 4): n for n, i in enumerate(i for i in range(16) if i not in (0, 3, 12, 15))}
BF, F32 = jnp.bfloat16, jnp.float32


def iota(shape, dim):
    return lax.broadcasted_iota(jnp.int32, shape, dim)


def dot(a, b):
    return jnp.dot(a, b, preferred_element_type=F32)


def params(mib):
    return pltpu.CompilerParams(vmem_limit_bytes=mib * 2**20)


def cost(flops, nbytes):
    return pl.CostEstimate(flops=flops, bytes_accessed=nbytes, transcendentals=0)


def bf16_terms(v):
    high = v.astype(BF).astype(F32)
    middle = (v - high).astype(BF).astype(F32)
    return [high, middle, v - high - middle]


def pick_dot(v, ones):
    n = v.shape[0]
    parts = dot(jnp.concatenate(bf16_terms(v), axis=0).astype(BF), ones)
    return parts[:n] + parts[n : 2 * n] + parts[2 * n :]


def to_groups(lane):
    return (iota((C, 128), 0) // 16 + lane == iota((C, 128), 1)).astype(BF)


def from_groups(lane):
    return (iota((128, C), 1) // 16 + lane == iota((128, C), 0)).astype(BF)


def group_stats(mean, m2, count):
    group_mean = pick_dot(mean, to_groups(0)) * (1.0 / 16.0)
    off = mean - pick_dot(group_mean, from_groups(0))
    return group_mean + pick_dot(m2 + count * (off * off), to_groups(32))


def merge(parts, count):
    n = parts.shape[0]
    total = jnp.sum(parts, axis=0)
    mean = total * (1.0 / n)
    off = parts - mean[None]
    between = pltpu.roll(jnp.sum(off * off, axis=0), 32, 1)
    is_mean = (iota(total.shape, 1) // 32) % 2 == 0
    return jnp.where(is_mean, mean, total + count * between)


def split_terms(v):
    return jnp.concatenate(bf16_terms(v) + [jnp.zeros_like(v)], axis=1)


def join_terms(v):
    return sum(v[:, 128 * i : 128 * i + 128].astype(F32) for i in range(3))


def latent_stats_kernel(x_ref, up_ref, down_ref, out_ref):
    n = x_ref.shape[0]
    step = 64

    pivot = x_ref[:16, :].astype(F32)[:1]

    def add(i, totals):
        rows = x_ref[pl.ds(pl.multiple_of(i * step, step), step), :].astype(F32) - pivot
        rows = rows.reshape(step // 8, 8, C)
        return totals[0] + jnp.sum(rows, axis=0), totals[1] + jnp.sum(rows * rows, axis=0)

    zero = jnp.zeros((8, C), F32)
    totals = lax.fori_loop(0, n // step, add, (zero, zero))
    off = jnp.sum(totals[0], axis=0, keepdims=True) * (1.0 / n)
    mean = pivot + off
    m2 = jnp.sum(totals[1], axis=0, keepdims=True) - n * off * off
    wide = lambda v: jnp.broadcast_to(v, (8, C))
    row = split_terms(group_stats(wide(mean), wide(m2), float(n)))
    row = jnp.concatenate([row, jnp.zeros_like(row)], axis=0).astype(BF)
    out_ref[...] = row
    up_ref[:128, :] = x_ref[n - 128 :, :]
    down_ref[:128, :] = x_ref[:128, :]
    up_ref[128:, :] = row
    down_ref[128:, :] = row


def finish(whole, count):
    is_mean = (iota(whole.shape, 1) // 32) % 2 == 0
    return jnp.where(is_mean, whole, lax.rsqrt(whole * (1.0 / count) + EPS))


def inner_kernel(x_ref, out_ref):
    x = x_ref[...].astype(F32).reshape(2, S, 8, S, C)
    for k in range(8):
        for half in range(2):
            out_ref[2 * k + half] = x[half, :, k].reshape(S * S, C).astype(BF)


def rim_kernel(x_ref, up_ref, down_ref, own_ref, far_ref, out_ref, wide, rim):
    n = 2048.0 * 16.0
    parts = [own_ref[...], far_ref[...], up_ref[128:, :], down_ref[128:, :]]
    whole = merge(jnp.stack([join_terms(v)[:8] for v in parts]), n)
    stats = split_terms(jnp.where(iota(whole.shape, 1) < 64, finish(whole, 4.0 * n), 0.0))[:1]
    rim[...] = jnp.zeros_like(rim)

    def lanes(q):
        at = slice(128 * q, 128 * q + 128)
        wide[0] = up_ref[:128, at].astype(F32)
        wide[17] = down_ref[:128, at].astype(F32)
        wide[1:17] = x_ref[:, :, at].astype(F32)
        for half in range(2):
            rim[half, pl.ds(20, 16, stride=RIM), :] = jnp.broadcast_to(stats[:, at], (16, 128))
            for r in range(W):
                left, right = (16, 17) if r == 0 else (18, 19) if r == W - 1 else (r - 1, S + r - 1)
                rim[half, pl.ds(RIM + left, 15, stride=RIM), :] = wide[S * half + r, pl.ds(S - 1, 15, stride=S), :]
                rim[half, pl.ds(right, 15, stride=RIM), :] = wide[S * half + r, pl.ds(S, 15, stride=S), :]
            out_ref[:, half, :, at] = rim[half].reshape(16, RIM, 128).astype(BF)

    for q in range(4):
        lanes(q)


def weights_kernel(w_ref, *refs):
    out_ref = refs[-1]

    def products(g):
        ends = (g[0] + g[2]) * 0.5
        middle = g[1] * 0.5
        return g[0], ends + middle, ends - middle, g[2]

    def rows(i, _):
        at = pl.ds(pl.multiple_of(16 * i, 16), 16)
        for q in range(4):
            lanes = slice(128 * q, 128 * q + 128)
            columns = [products([w_ref[a, 0, e, at, lanes].astype(F32) for e in range(3)]) for a in range(3)]
            for l in range(4):
                for j, v in enumerate(products([columns[a][l] for a in range(3)])):
                    if (j, l) in COMBINED:
                        out_ref[COMBINED[j, l], 0, at, lanes] = v.astype(BF)
        return 0

    lax.fori_loop(0, 16, rows, 0)


def turned(in_ref, first, pixels):
    rows = pixels * T
    to, at = iota((rows, rows), 0), iota((rows, rows), 1)
    frame = 2 * (to % P2) + (to // P2) % 2
    turn = (at == frame * pixels + to // T).astype(BF)
    values = in_ref[:, pl.ds(first, pixels), :].reshape(rows, C)
    return dot(turn, values).reshape(pixels, 2, P2, C)


def activate(values, norm):
    u = (values - norm[0][None]) * norm[1][None]
    return (u / (1.0 + jnp.exp(-u))).astype(BF).astype(F32)


def time_terms(act):
    pixels = act.shape[0]
    even, odd = act[:, 0], act[:, 1]
    start = iota((pixels * P2, C), 0) % P2 == 0

    def before(v):
        v = pltpu.roll(v.reshape(pixels * P2, C), 1, 0)
        return jnp.where(start, 0.0, v).reshape(pixels, P2, C)

    even1, odd1 = before(even), before(odd)
    return even1 - even, odd1 + even, even - odd1, odd1 - odd


def conv_kernel(
    place_ref, in_ref, rim_ref, core_ref, band_ref, plain_ref, sums_ref, mid_ref, stats_ref,
    terms, ends, sides, latent, sums, norm, held, sems,
):
    def arrival(j, l, b, source):
        slot = 4 * (j % 3) + l
        return pltpu.make_async_copy(source, held.at[slot, b], sems.at[slot, b])

    def start(j):
        for l in range(4):
            for b in range(3):
                summed = (j, l) in COMBINED
                source = sums_ref.at[COMBINED[j, l], b] if summed else plain_ref.at[2 * j // 3, b, 2 * l // 3]
                arrival(j, l, b, source).start()

    for j in range(3):
        start(j)

    block, z = place_ref[0], place_ref[1]
    half, column = block % 2, block // 2
    above = (half == 0) & (z == 0)
    below = (half == 1) & (z == 3)
    tail = rim_ref[:, 16:RIM, :].reshape(T * 8, C)
    row = iota((T, T * 8), 0)
    row = 2 * (row % P2) + row // P2
    pieces = dot((iota((T, T * 8), 1) == row * 8 + 4).astype(BF), tail).astype(BF)
    for i in range(2):
        norm[i] = sum(
            dot(pieces[:, 128 * k : 128 * k + 128], from_groups(32 * i)) for k in range(3)
        ).reshape(2, P2, C)

    for first, pixels in ((0, 16), (16, 8)):
        act = activate(turned(rim_ref, first, pixels), norm)
        p = iota(act.shape, 0) + first
        out = (column == 0) & ((p < 8) | (p == 16) | (p == 18))
        out = out | (column == 15) & ((p >= 8) & (p < 16) | (p == 17) | (p == 19))
        out = out | above & ((p == 16) | (p == 17)) | below & (p >= 18)
        for j, v in enumerate(time_terms(jnp.where(out, 0.0, act))):
            for q in range(min(pixels, 20 - first)):
                p = first + q
                if p < 16:
                    sides[j, p // S, p % S] = v[q]
                else:
                    ends[j, (p - 16) // 2, (p % 2) * (W - 1)] = v[q]
    core, band = turned(core_ref, 0, S), turned(band_ref, 0, S)
    for i, values in enumerate((jnp.where(half == 0, band, core), jnp.where(half == 0, core, band))):
        act = jnp.where(below if i else above, 0.0, activate(values, norm))
        for j, v in enumerate(time_terms(act)):
            ends[j, i, 1 : S + 1] = v

    def columns(v, j, at):
        v = v.reshape(2, W // 2, 2, P2, C)
        even, odd = v[:, :, 0], v[:, :, 1]
        before, after, odd_before = even[:, :-1], even[:, 1:], odd[:, :-1]
        for l, u in enumerate((before - after, odd_before + after, after - odd_before, odd_before - odd[:, 1:])):
            u = u.astype(BF)
            for i, r in enumerate(at):
                terms[j, l, r] = u[i]

    for j in range(4):
        columns(ends[j], j, (0, W - 1))

    def two_rows(k, _):
        first = pl.multiple_of(16 * k, 16)
        values = turned(in_ref, first, 16)
        latent[pl.ds(first, 16)] = values.astype(BF)
        for j, v in enumerate(time_terms(activate(values, norm))):
            left, right = (sides[j, i, pl.ds(2 * k, 2)][:, None] for i in range(2))
            columns(jnp.concatenate([left, v.reshape(2, S, P2, C), right], axis=1), j, (2 * k + 1, 2 * k + 2))
        return 0

    lax.fori_loop(0, S // 2, two_rows, 0)

    def term(j, _):
        @pl.when(j == 1)
        def _():
            start(3)

        for l in range(4):
            for b in range(3):
                arrival(j, l, b, sums_ref.at[0, 0]).wait()
        for q in range(2):
            m = []
            for l in range(4):
                rows = [terms[j, l, 4 * q + b : 4 * q + b + 4].reshape(16 * P2, C) for b in range(3)]
                weight = held[4 * (j % 3) + l].reshape(3 * C, C)
                m.append(dot(jnp.concatenate(rows, axis=1), weight).reshape(4, 4, P2, C))
            sums[j, 0, 4 * q : 4 * q + 4] = m[0] + m[1] + m[2]
            sums[j, 1, 4 * q : 4 * q + 4] = m[1] - m[2] - m[3]
        return 0

    lax.fori_loop(0, 4, term, 0)

    def pixel(r, c):
        m = [sums[j, c % 2, r, c // 2] for j in range(4)]
        m = m[0] + m[1] + m[2], m[1] - m[2] - m[3]
        return [(latent[S * r + c, i].astype(F32) + m[i]).astype(BF) for i in range(2)]

    pivot = [v.astype(F32) for v in pixel(0, 0)]

    def finish_row(r, totals):
        for c in range(S):
            for i, v in enumerate(pixel(r, c)):
                mid_ref[S * r + c, i] = v
                off = v.astype(F32) - pivot[i]
                totals[i] = totals[i] + off
                totals[2 + i] = totals[2 + i] + off * off
        return totals

    totals = lax.fori_loop(0, S, finish_row, [jnp.zeros((P2, C), F32)] * 4)
    off = [v * (1.0 / (S * S)) for v in totals[:2]]
    mean = [pivot[i] + off[i] for i in range(2)]
    total = [totals[2 + i] - S * S * off[i] * off[i] for i in range(2)]
    stats = group_stats(jnp.concatenate(mean, axis=0), jnp.concatenate(total, axis=0), float(S * S))
    stats = stats[:P2] + pltpu.roll(stats[P2:], 64, 1)
    stats_ref[...] = jnp.broadcast_to(stats[None], stats_ref.shape)


def merge_kernel(parts_ref, out_ref):
    whole = merge(parts_ref[...], float(S * S * 16))
    out_ref[...] = jnp.broadcast_to(whole[None], out_ref.shape)


def attend_kernel(mid_ref, parts_ref, score_ref, update_ref, out_ref, norm):
    @pl.when(pl.program_id(0) == 0)
    def _():
        count = float(S * S * 16 * 8)
        whole = finish(merge(parts_ref[...], count), 16.0 * count)
        both = jnp.concatenate([whole, pltpu.roll(whole, 64, 1)], axis=0)
        for i in range(2):
            norm[i] = pick_dot(both, from_groups(32 * i)).reshape(2, P2, C)

    pixels = mid_ref.shape[0]
    rows = pixels * T
    mid = mid_ref[...].astype(F32)
    flat = ((mid - norm[0][None]) * norm[1][None]).astype(BF).reshape(rows, C)
    query = dot(flat, score_ref[...]).astype(BF)
    n = 256
    row, column = iota((n, n), 0), iota((n, n), 1)
    frame = lambda v: 2 * (v % P2) + (v // P2) % 2
    seen = (row // T == column // T) & (frame(row) >= frame(column))
    parts = []
    for i in range(rows // n):
        at = slice(i * n, i * n + n)
        scores = lax.dot_general(query[at], flat[at], (((1,), (1,)), ((), ())), preferred_element_type=F32)
        scores = jnp.where(seen, scores, -1e30)
        weights = jnp.exp(scores - jnp.max(scores, axis=1, keepdims=True))
        weights = (weights * (1.0 / jnp.sum(weights, axis=1, keepdims=True))).astype(BF)
        parts.append(dot(weights, flat[at]).astype(BF))
    update = dot(jnp.concatenate(parts, axis=0), update_ref[...])
    out = (mid.reshape(rows, C) + update).astype(BF)
    to = iota((n, n), 0)
    frame = to // S
    turn = (iota((n, n), 1) == (to % S) * T + (frame % 2) * P2 + frame // 2).astype(BF)
    for i in range(rows // (2 * n)):
        pair = [dot(turn, out[(2 * i + k) * n : (2 * i + k + 1) * n]).reshape(T, S, C) for k in range(2)]
        out_ref[:, 16 * i : 16 * i + 16, :] = jnp.concatenate(pair, axis=1).astype(BF)


def local(latents, conv_weight, w_query, w_key, w_value, w_out):
    x = latents.reshape(16, 128, C)
    vmem = pl.BlockSpec(memory_space=pltpu.VMEM)
    smem = pl.BlockSpec(memory_space=pltpu.SMEM)
    whole = lambda *shape: pl.BlockSpec(shape, lambda i: (0,) * len(shape))
    exchange = lambda v, axes: lax.all_to_all(v[None], axes, split_axis=1, concat_axis=0, tiled=True)[:, 0]
    place = jnp.stack([lax.axis_index(TM), lax.axis_index("rows")]).astype(jnp.int32)

    inner = pl.pallas_call(
        inner_kernel,
        grid=(2,),
        out_shape=jax.ShapeDtypeStruct((32, S * S, C), BF),
        in_specs=[pl.BlockSpec((16, 64, C), lambda i: (0, i, 0))],
        out_specs=pl.BlockSpec((16, S * S, C), lambda i: (i, 0, 0)),
        compiler_params=params(56),
        cost_estimate=cost(2**20, 4 * 2**20),
        name="inner",
    )(x)
    patch = exchange(inner, TM)
    row = jax.ShapeDtypeStruct((144, C), BF)
    up, down, own = pl.pallas_call(
        latent_stats_kernel,
        out_shape=(row, row, jax.ShapeDtypeStruct((16, C), BF)),
        in_specs=[vmem],
        out_specs=(vmem,) * 3,
        compiler_params=params(12),
        cost_estimate=cost(2048 * C * 4, 2048 * C * 2),
        name="latent_stats",
    )(x.reshape(2048, C))
    def combine(first, count, conv_weight, *before):
        return pl.pallas_call(
            weights_kernel,
            grid=(count,),
            out_shape=jax.ShapeDtypeStruct((12, 3, C, C), BF),
            in_specs=[pl.BlockSpec((3, 1, 3, 256, C), lambda i: (0, (i + first) // 2, 0, (i + first) % 2, 0))]
            + [pl.BlockSpec(memory_space=pl.ANY)] * len(before),
            out_specs=pl.BlockSpec((12, 1, 256, C), lambda i: (0, (i + first) // 2, (i + first) % 2, 0)),
            input_output_aliases={1: 0} if before else {},
            compiler_params=params(56),
            cost_estimate=cost(count * C * C, count * 11 * C * C * 2),
            name="weights",
        )(conv_weight, *before)

    around = lambda v, by: lax.ppermute(v, "rows", [(i, (i + by) % 4) for i in range(4)])
    up, down, far = around(up, 1), around(down, 3), around(own, 2)
    _, early = lax.optimization_barrier((own, conv_weight))
    rim_x, weights = lax.optimization_barrier((x, combine(0, 1, early)))
    rim = pl.pallas_call(
        rim_kernel,
        out_shape=jax.ShapeDtypeStruct((16, 2, RIM, C), BF),
        in_specs=[vmem] * 5,
        out_specs=vmem,
        scratch_shapes=[pltpu.VMEM((18, 128, 128), F32), pltpu.VMEM((2, 16 * RIM, 128), F32)],
        compiler_params=params(16),
        cost_estimate=cost(2**22, 4 * 2**20),
        name="rim",
    )(rim_x, up, down, own, far).reshape(32, RIM, C)

    rim, early = lax.optimization_barrier((rim, conv_weight))
    rim, patch, weights = lax.optimization_barrier((rim, patch, combine(1, 4, early, weights)))
    rim = exchange(rim, TM)
    first = lax.axis_index("core") == 0
    row = lambda at: lax.dynamic_slice_in_dim(patch, at, S, axis=1)
    core, band = row(jnp.where(first, S * S - S, 0)), row(jnp.where(first, 0, S * S - S))
    core, band, late = lax.optimization_barrier((core, band, conv_weight))
    core = lax.ppermute(core, "core", [(0, 1), (1, 0)])
    pairs = [(4 + i, i + 1) for i in range(3)] + [(i + 1, 4 + i) for i in range(3)]
    band = lax.ppermute(band, ("core", "rows"), pairs)
    weights = combine(5, 1, late, weights)
    score = (dot(w_query, w_key.T) * (1.0 / C**0.5)).astype(BF)
    update = dot(w_value, w_out).astype(BF)

    mid, stats = pl.pallas_call(
        conv_kernel,
        out_shape=(jax.ShapeDtypeStruct((S * S, 2, P2, C), BF), jax.ShapeDtypeStruct((8, P2, 128), F32)),
        in_specs=[smem] + [vmem] * 4 + [pl.BlockSpec(memory_space=pl.ANY)] * 2,
        out_specs=(vmem, vmem),
        scratch_shapes=[
            pltpu.VMEM((4, 4, W, S // 2, P2, C), BF),
            pltpu.VMEM((4, 2, W, P2, C), F32),
            pltpu.VMEM((4, 2, S, P2, C), F32),
            pltpu.VMEM((S * S, 2, P2, C), BF),
            pltpu.VMEM((4, 2, S, S // 2, P2, C), F32),
            pltpu.VMEM((2, 2, P2, C), F32),
            pltpu.VMEM((12, 3, C, C), BF),
            pltpu.SemaphoreType.DMA((12, 3)),
        ],
        compiler_params=params(56),
        cost_estimate=cost(512 * 48 * C * C * 2, 28 * 2**20),
        name="conv",
    )(place, patch, rim, core, band, conv_weight, weights)
    parts = pl.pallas_call(
        merge_kernel,
        out_shape=jax.ShapeDtypeStruct((16, P2, 128), F32),
        in_specs=[vmem],
        out_specs=vmem,
        compiler_params=params(4),
        name="merge",
    )(exchange(stats, ("core", "rows")))
    parts = exchange(parts, ("x", "y"))
    pixels = 32
    out = pl.pallas_call(
        attend_kernel,
        grid=(S * S // pixels,),
        out_shape=jax.ShapeDtypeStruct((T, S * S, C), BF),
        in_specs=[pl.BlockSpec((pixels, 2, P2, C), lambda i: (i, 0, 0, 0)), whole(16, P2, 128)] + [whole(C, C)] * 2,
        out_specs=pl.BlockSpec((T, pixels, C), lambda i: (0, i, 0)),
        scratch_shapes=[pltpu.VMEM((2, 2, P2, C), F32)],
        compiler_params=params(24),
        cost_estimate=cost(2048 * C * C * 2 * 4, 8 * 2**20),
        name="attend",
    )(mid, parts, score, update)
    back = exchange(out, TM)
    back = back.reshape(16, 2, S, S, C).transpose(1, 2, 0, 3, 4)
    return back.reshape(1, 16, 128, C)


def solution(mesh):
    mesh = Mesh(mesh.devices.reshape(4, 4, 2, 4), TM + ("rows",))
    in_specs = (P(TM, "rows", None, None), P(), P(), P(), P(), P())
    out_specs = P(TM, "rows", None, None)
    return jax.shard_map(local, mesh=mesh, in_specs=in_specs, out_specs=out_specs, check_vma=False)
```
